32 devices in a mesh: dp: 8 (over z, x), fsdp: 4 (over y, core).
Axes of the slice: x: 2, y: 2, z: 4, core: 2. Of those that a mesh axis runs over, the one named last changes fastest.
Arguments:
- chars: int32 [64, 256], P(('dp', 'fsdp')), may hold values from 0 to 26
- steps: int32 [64], P(('dp', 'fsdp')), may hold values from 0 to 999
- embed: bfloat16 [13824], P(('dp', 'fsdp')), may hold values from -4 to 4
- layer_params: bfloat16 [2, 3216384], P(None, ('dp', 'fsdp')), may hold values from -2 to 2, as said below
- cotangent: bfloat16 [64, 256, 512], P(('dp', 'fsdp')), may hold values from -6 to 6
Outputs:
- out_act: bfloat16 [64, 256, 512], P(('dp', 'fsdp'))
- grad_embed: float32 [13824], P(('dp', 'fsdp'))
- grad_params: float32 [2, 3216384], P(None, ('dp', 'fsdp'))
The draws below stay inside these ranges and needn't reach their ends.
Inputs may be any that keep to these rules, and one draw needn't show every extreme that they name: `layer_params`: parameters of 2 layers in the layout of the steps.
All inputs are finite; a program needn't handle non-finite values.
Results may differ from the reference program's by a relative error of at most 0.01.
Values may be sent and summed in bfloat16 or wider, within the bound.
No kernel may reach another device: no remote copies, remote signals or barrier semaphores. Data moves between devices by JAX's collectives and lax.ppermute only.
A program may use at most 256 MiB of HBM per device.

```python
import math
import jax
import jax.numpy as jnp
from jax import lax

D = 512
HEADS = 8
FF = 2048
VOCAB = 27
TD = 128
TSTEPS = 1000
LAYERS = 2
LEN = 256
HD = 64
SEQS = 64
P_SIZE = 3216384


def draw_layer_params(key, part):
    key = jax.random.fold_in(key, 7)
    segment_table = ((D, 0.1, 1.0), (D, 0.3, 0.0), (TD * D, 1.0 / math.sqrt(TD), 0.0), (D, 0.5, 0.0), (3 * D * D, 1.0 / math.sqrt(D), 0.0), (D * D, math.sqrt(8.0 / D), 0.0), (D, 0.1, 1.0), (D, 0.3, 0.0), (D * FF, 1.0 / math.sqrt(D), 0.0), (FF, 0.3, 0.0), (FF * D, 1.0 / math.sqrt(FF), 0.0), (D, 0.3, 0.0))
    scale_vec = jnp.concatenate([jnp.full((seg_entry[0],), seg_entry[1], jnp.float32) for seg_entry in segment_table])
    shift_vec = jnp.concatenate([jnp.full((seg_entry[0],), seg_entry[2], jnp.float32) for seg_entry in segment_table])
    noise_draw = jnp.clip(jax.random.normal(key, (LAYERS, P_SIZE), jnp.float32), -4.0, 4.0)
    return (noise_draw * scale_vec[None, :] + shift_vec[None, :]).astype(jnp.bfloat16)


def set_ends(entries, own_key, smallest, top_value):
    extent = entries.shape
    place = [jax.random.randint(jax.random.fold_in(own_key, axis), (), 0, extent[axis]) for axis in range(len(extent))]
    entries = entries.at[tuple(place)].set(smallest)
    longest = extent.index(max(extent))
    place[longest] = (place[longest] + 1) % extent[longest]
    return entries.at[tuple(place)].set(top_value)


def steps_of(stream_key, dims, cuts, low, largest):
    gain, own = 1.0, jax.random.fold_in(stream_key, 6)
    for dim, parts in cuts:
        heights = jnp.exp(jax.random.uniform(jax.random.fold_in(own, dim), (parts,), jnp.float32, low / len(cuts), largest / len(cuts)))
        gain = gain * jnp.repeat(heights, dims[dim] // parts).reshape([-1 if axis == dim else 1 for axis in range(len(dims))])
    return gain


def gaussian(stream_key, extent, width, limit, shards=(), kind=jnp.bfloat16):
    level = steps_of(stream_key, extent, shards, -0.22, 0.18) if shards else 1.0
    entries = jax.random.normal(stream_key, extent, jnp.float32) * width * level
    return jnp.minimum(jnp.maximum(entries, -limit), limit).astype(kind)


def setup_inputs(seed: int = 0) -> dict:
    arg_keys = jax.random.split(jax.random.key(seed), 6)
    return {
        "chars": set_ends(jax.random.randint(arg_keys[0], (SEQS, LEN), 0, VOCAB), jax.random.fold_in(arg_keys[0], 1), 0, VOCAB - 1).astype(jnp.int32),
        "steps": set_ends(jax.random.randint(arg_keys[1], (SEQS,), 0, TSTEPS), jax.random.fold_in(arg_keys[1], 1), 0, TSTEPS - 1).astype(jnp.int32),
        "embed": gaussian(arg_keys[2], (VOCAB * D,), 1.0, 4.0, ((0, 32),)),
        "layer_params": draw_layer_params(jax.random.fold_in(arg_keys[5], 71), 0),
        "cotangent": gaussian(arg_keys[4], (SEQS, LEN, D), 1.0, 6.0, ((0, 32),)),
    }


HIGHEST = lax.Precision.HIGHEST
EPSILON = 1e-05

@jax.custom_vjp
def low(v):
    return lax.optimization_barrier(v.astype(jnp.bfloat16)).astype(jnp.float32)

@jax.custom_vjp
def low_back(v):
    return v

def low_keep(v):
    return (low(v), None)

def low_pass(kept, grad):
    return (grad,)

def back_keep(v):
    return (v, None)

def back_low(kept, grad):
    return (low(grad),)
low.defvjp(low_keep, low_pass)
low_back.defvjp(back_keep, back_low)

def timestep_embed(step_ids):
    half_dim = TD // 2
    freq_base = jnp.exp(jnp.arange(half_dim, dtype=jnp.float32) * (-math.log(10000.0) / half_dim))
    angle_grid = step_ids.astype(jnp.float32)[:, None] * freq_base[None, :]
    return jnp.concatenate([jnp.sin(angle_grid), jnp.cos(angle_grid)], axis=1)

def split_params(flat_vec):
    piece_shapes = ((D,), (D,), (TD, D), (D,), (D, 3 * D), (D, D), (D,), (D,), (D, FF), (FF,), (FF, D), (D,))
    pieces_out = []
    offset_now = 0
    for piece_shape in piece_shapes:
        piece_size = math.prod(piece_shape)
        pieces_out.append(flat_vec[offset_now:offset_now + piece_size].reshape(piece_shape))
        offset_now = offset_now + piece_size
    return pieces_out

def normalize(values, gain_vec, bias_vec):
    mean_val = lax.optimization_barrier(jnp.mean(values, -1, keepdims=True))
    centered = values - mean_val
    variance = lax.optimization_barrier(jnp.mean(centered * centered, -1, keepdims=True))
    return centered * lax.rsqrt(variance + EPSILON) * gain_vec + bias_vec

def matmul_spec(spec_text, left, right):
    return jnp.einsum(spec_text, left, right, precision=HIGHEST)

def layer_step(stream, emb_low, weights):
    gain_one, bias_one, w_time, b_time, w_qkv, w_out, gain_two, bias_two, w_up, b_up, w_down, b_down = weights
    group_count = stream.shape[0]
    time_vec = low_back(jnp.dot(emb_low, w_time, precision=HIGHEST) + b_time)
    mixed_in = stream + time_vec[:, None, :]
    normed_low = low(normalize(mixed_in, gain_one, bias_one))
    qkv_low = low_back(low(matmul_spec('gld,de->gle', normed_low, w_qkv)))
    queries = qkv_low[..., :D].reshape(group_count, LEN, HEADS, HD)
    key_rows = qkv_low[..., D:2 * D].reshape(group_count, LEN, HEADS, HD)
    values = qkv_low[..., 2 * D:].reshape(group_count, LEN, HEADS, HD)
    scores = low_back(matmul_spec('gqhe,gkhe->ghqk', queries, key_rows) * (1.0 / math.sqrt(HD)))
    top_score = lax.optimization_barrier(jnp.max(scores, -1, keepdims=True))
    expd = jnp.exp(scores - top_score)
    prob_full = expd / lax.optimization_barrier(jnp.sum(expd, -1, keepdims=True))
    heads_out = matmul_spec('ghqk,gkhe->gqhe', low(prob_full), values).reshape(group_count, LEN, D)
    attn_low = low_back(low(heads_out))
    after_attn = mixed_in + low_back(matmul_spec('gld,de->gle', attn_low, w_out))
    normed_two = low(normalize(after_attn, gain_two, bias_two))
    up_proj = low_back(matmul_spec('gld,df->glf', normed_two, w_up) + b_up)
    hidden_low = low(jax.nn.gelu(up_proj, approximate=True))
    return after_attn + low_back(matmul_spec('glf,fd->gld', hidden_low, w_down) + b_down)

def forward(layer_weights, embed_vec, chars, steps):
    char_table = embed_vec.reshape(VOCAB, D)
    group_seqs = math.gcd(SEQS, max(1, 4096 // LEN))
    group_total = SEQS // group_seqs

    def group_step(scan_carry, group_item):
        chars_group, steps_group = group_item
        one_hot = (chars_group[..., None] == jnp.arange(VOCAB, dtype=jnp.int32)).astype(jnp.float32)
        stream = low_back(matmul_spec('glv,vd->gld', one_hot, char_table))
        emb_low = low(timestep_embed(steps_group))
        for layer_index in range(LAYERS):
            stream = layer_step(stream, emb_low, split_params(layer_weights[layer_index]))
        return (scan_carry, stream)
    unused_carry, outputs = lax.scan(jax.checkpoint(group_step), jnp.zeros((), jnp.float32), (chars.reshape(group_total, group_seqs, LEN), steps.reshape(group_total, group_seqs)))
    return outputs.reshape(SEQS, LEN, D)

def reference(chars, steps, embed, layer_params, cotangent):

    def run_forward(weights_in, table_in):
        return forward(weights_in, table_in, chars, steps)
    result, pullback = jax.vjp(run_forward, layer_params.astype(jnp.float32), embed.astype(jnp.float32))
    grad_params, grad_embed = pullback(cotangent.astype(jnp.float32))
    return (result.astype(jnp.bfloat16), grad_embed, grad_params)
```

```python
import functools
import math

import jax
import jax.numpy as jnp
from jax import lax
from jax.experimental import pallas as pl
from jax.experimental.pallas import tpu as pltpu
from jax.sharding import PartitionSpec as P

D = 512
HEADS = 8
FF = 2048
VOCAB = 27
TD = 128
HD = 64
LANES = 128
EPSILON = 1e-05
AXES = ("dp", "fsdp")
F32 = jnp.float32
BF16 = jnp.bfloat16
VMEM_BYTES = 52 * 2**20

ROW_GAIN_ONE, ROW_BIAS_ONE, ROW_W_TIME, ROW_B_TIME = 0, 4, 8, 520
ROW_QKV, ROW_OUT, ROW_GAIN_TWO, ROW_BIAS_TWO = 524, 6668, 8716, 8720
ROW_UP, ROW_B_UP, ROW_DOWN, ROW_B_DOWN, ROW_END = 8724, 16916, 16932, 25124, 25128
CHUNK_PAD = 832


def ceil_to(value, step):
    return -(-value // step) * step


class Geometry:
    def __init__(self, devices, shard, embed_shard):
        self.devices, self.shard, self.embed_shard = devices, shard, embed_shard
        self.param_rows = max(self.count(d, shard) for d in range(devices))
        self.embed_rows = max(self.count(d, embed_shard) for d in range(devices))
        self.embed_at = ceil_to(self.param_rows, 8)
        self.rows = ceil_to(self.embed_at + 8, 16)

    @staticmethod
    def first(d, size):
        return d * size // LANES

    @staticmethod
    def count(d, size):
        return -(-(d + 1) * size // LANES) - d * size // LANES


def params(flops, nbytes):
    return dict(
        compiler_params=pltpu.CompilerParams(vmem_limit_bytes=VMEM_BYTES),
        cost_estimate=pl.CostEstimate(flops=flops, bytes_accessed=nbytes, transcendentals=0),
    )


VM = pl.BlockSpec(memory_space=pltpu.VMEM)
SM = pl.BlockSpec(memory_space=pltpu.SMEM)
ANY = pl.BlockSpec(memory_space=pl.ANY)


def nn(left, right):
    return lax.dot_general(left, right, (((1,), (0,)), ((), ())), preferred_element_type=F32)


def nt(left, right):
    return lax.dot_general(left, right, (((1,), (1,)), ((), ())), preferred_element_type=F32)


def tn(left, right):
    return nn(left.T, right)


def shift_in(flat, offset):
    rolled = pltpu.roll(flat, offset, 1)
    above = jnp.concatenate([jnp.zeros((1, LANES), F32), rolled[:-1]], 0)
    lane = lax.broadcasted_iota(jnp.int32, flat.shape, 1)
    return jnp.where(lane >= offset, rolled, above)


def shift_out(flat, offset):
    rolled = pltpu.roll(flat, lax.rem(LANES - offset, LANES), 1)
    below = jnp.concatenate([rolled[1:], jnp.zeros((1, LANES), F32)], 0)
    lane = lax.broadcasted_iota(jnp.int32, flat.shape, 1)
    return jnp.where(lane < LANES - offset, rolled, below)


def pack_kernel(geo, place_ref, layers_ref, embed_ref, first_ref, second_ref):
    main = geo.embed_at
    for layer, out_ref in ((0, first_ref), (1, second_ref)):
        moved = shift_in(layers_ref[layer].astype(F32), place_ref[1])
        if layer == 0:
            tail = shift_in(embed_ref[...].astype(F32), place_ref[2])
            parts = [moved[:main], tail] + ([moved[main + 8 :]] if geo.rows > main + 8 else [])
            moved = jnp.concatenate(parts, 0)
        out_ref[...] = moved.astype(BF16)


def pack_shards(geo, place, layer_params, embed):
    layers = jnp.pad(layer_params, ((0, 0), (0, geo.rows * LANES - geo.shard)))
    table = jnp.pad(embed, (0, 8 * LANES - geo.embed_shard))
    out = jax.ShapeDtypeStruct((geo.rows, LANES), BF16)
    return pl.pallas_call(
        functools.partial(pack_kernel, geo),
        out_shape=(out, out),
        in_specs=[SM, VM, VM],
        out_specs=(VM, VM),
        **params(10**6, geo.rows * 1024),
    )(place, layers.reshape(2, geo.rows, LANES), table.reshape(8, LANES))


def finish_kernel(geo, place_ref, *refs):
    n_param, n_embed = 4, 4
    firsts, seconds, tables = refs[:n_param], refs[n_param : 2 * n_param], refs[2 * n_param : 2 * n_param + n_embed]
    grads_ref, embed_ref = refs[-2:]
    for layer, parts in ((0, firsts), (1, seconds)):
        total = parts[0][...].astype(F32)
        for part in parts[1:]:
            total = total + part[...].astype(F32)
        grads_ref[layer] = shift_out(total, place_ref[1])
    total = tables[0][...].astype(F32)
    for part in tables[1:]:
        total = total + part[...].astype(F32)
    embed_ref[...] = shift_out(total, place_ref[2])


def finish(geo, place, firsts, seconds, tables):
    operands = list(firsts) + list(seconds) + list(tables)
    grads, table = pl.pallas_call(
        functools.partial(finish_kernel, geo),
        out_shape=(
            jax.ShapeDtypeStruct((2, geo.rows, LANES), F32),
            jax.ShapeDtypeStruct((8, LANES), F32),
        ),
        in_specs=[SM] + [VM] * len(operands),
        out_specs=(VM, VM),
        **params(10**6, geo.rows * 4096),
    )(place, *operands)
    grads = grads.reshape(2, geo.rows * LANES)[:, : geo.shard]
    return grads, table.reshape(-1)[: geo.embed_shard]


def unpack_kernel(geo, layer, plan, place_ref, *refs):
    n_in = len(plan)
    chunk_refs = refs[:n_in]
    w_time, w_qkv, w_out, w_up, w_down, vectors = refs[n_in : n_in + 6]
    table = refs[n_in + 6] if layer == 0 else None
    held, flat, flat_table, sems = refs[-4:]
    me = place_ref[0]
    copies = []
    for source, pieces in zip(chunk_refs, plan):
        for src_at, relative, absolute, dst_at, count in pieces:
            if absolute is None:
                target = held.at[lax.bitwise_xor(me, relative), pl.ds(dst_at, count)]
                origin = source.at[pl.ds(src_at, count)]
            else:
                target, origin = held, source
            copies.append(pltpu.make_async_copy(origin, target, sems.at[len(copies)]))
    for copy in copies:
        copy.start()
    for copy in copies:
        copy.wait()
    for d in range(geo.devices):
        block = held[d].astype(F32)
        start, rows = geo.first(d, geo.shard), geo.count(d, geo.shard)
        split = (d * geo.shard) % LANES != 0
        if split:
            shared = flat[pl.ds(start, 1), :] + block[:1]
        flat[pl.ds(start, rows), :] = block[:rows]
        if split:
            flat[pl.ds(start, 1), :] = shared
        if layer == 0:
            tail = block[geo.embed_at : geo.embed_at + 8]
            start, rows = geo.first(d, geo.embed_shard), geo.count(d, geo.embed_shard)
            split = (d * geo.embed_shard) % LANES != 0
            if split:
                shared = flat_table[pl.ds(start, 1), :] + tail[:1]
            flat_table[pl.ds(start, rows), :] = tail[:rows]
            if split:
                flat_table[pl.ds(start, 1), :] = shared
    for out, start, rows, width in (
        (w_time, ROW_W_TIME, TD, 4),
        (w_qkv, ROW_QKV, D, 12),
        (w_out, ROW_OUT, D, 4),
        (w_up, ROW_UP, D, 16),
        (w_down, ROW_DOWN, FF, 4),
    ):
        for c in range(width):
            out[:, c * LANES : (c + 1) * LANES] = flat[pl.ds(start + c, rows, stride=width), :].astype(BF16)
    for row, start, width in (
        (0, ROW_GAIN_ONE, 4),
        (1, ROW_BIAS_ONE, 4),
        (2, ROW_B_TIME, 4),
        (3, ROW_GAIN_TWO, 4),
        (4, ROW_BIAS_TWO, 4),
        (5, ROW_B_DOWN, 4),
        (6, ROW_B_UP, 16),
    ):
        for c in range(width):
            vectors[row : row + 1, c * LANES : (c + 1) * LANES] = flat[pl.ds(start + c, 1), :]
    if layer == 0:
        table[...] = jnp.zeros(table.shape, BF16)
        for c in range(4):
            table[0:VOCAB, c * LANES : (c + 1) * LANES] = flat_table[pl.ds(c, VOCAB, stride=4), :].astype(BF16)


def unpack(geo, layer, place, gathered):
    arrays = [array for array, pieces in gathered]
    plan = tuple(tuple(pieces) for array, pieces in gathered)
    shapes = [
        jax.ShapeDtypeStruct((TD, D), BF16),
        jax.ShapeDtypeStruct((D, 3 * D), BF16),
        jax.ShapeDtypeStruct((D, D), BF16),
        jax.ShapeDtypeStruct((D, FF), BF16),
        jax.ShapeDtypeStruct((FF, D), BF16),
        jax.ShapeDtypeStruct((8, FF), F32),
    ]
    if layer == 0:
        shapes.append(jax.ShapeDtypeStruct((32, D), BF16))
    return pl.pallas_call(
        functools.partial(unpack_kernel, geo, layer, plan),
        out_shape=tuple(shapes),
        in_specs=[SM] + [ANY] * len(arrays),
        out_specs=(VM,) * len(shapes),
        scratch_shapes=[
            pltpu.VMEM((geo.devices, geo.rows, LANES), BF16),
            pltpu.VMEM((ROW_END + 8, LANES), F32),
            pltpu.VMEM((4 * 32, LANES), F32),
            pltpu.SemaphoreType.DMA((sum(len(pieces) for pieces in plan),)),
        ],
        **params(10**7, 4 * 6432768),
    )(place, *arrays)


def norm_stats(values):
    mean = jnp.mean(values, -1, keepdims=True)
    centered = values - mean
    variance = jnp.mean(centered * centered, -1, keepdims=True)
    scale = lax.rsqrt(variance + EPSILON)
    return centered * scale, scale


def norm_back(grad, values, gain):
    unit, scale = norm_stats(values)
    grad_gain = jnp.sum(grad * unit, 0, keepdims=True)
    grad_bias = jnp.sum(grad, 0, keepdims=True)
    inner = grad * gain
    shifted = inner - jnp.mean(inner, -1, keepdims=True)
    return scale * (shifted - unit * jnp.mean(inner * unit, -1, keepdims=True)), grad_gain, grad_bias


def gelu_both(u):
    root = math.sqrt(2.0 / math.pi)
    square = u * u
    t = jnp.tanh(root * (u + 0.044715 * (square * u)))
    half = 0.5 * (1.0 + t)
    slope = half + 0.5 * u * (1.0 - t * t) * (root * (1.0 + 3.0 * 0.044715 * square))
    return u * half, slope


def head_masks(shape, scale):
    lane = lax.broadcasted_iota(jnp.int32, shape, 1)
    one = jnp.where(lane < HD, scale, 0.0).astype(BF16)
    two = jnp.where(lane < HD, 0.0, scale).astype(BF16)
    return one, two


def forward_kernel(layer, seqs, *refs):
    if layer == 0:
        chars, table = refs[:2]
        refs = refs[2:]
    else:
        stream_in = refs[0]
        refs = refs[1:]
    emb, w_time, w_qkv, w_out, w_up, w_down, vectors = refs[:7]
    stream_out, x_out, a_out, qkv_out, prob_out, o_out, x2_out, a2_out, gl_out, slope_out = refs[7:]
    tokens = x_out.shape[0]
    length = tokens // seqs
    time_vec = nn(emb[...], w_time[...]) + vectors[2:3, :D]
    if layer == 0:
        lane = lax.broadcasted_iota(jnp.int32, (tokens, 32), 1)
        stream = nn((chars[...] == lane).astype(BF16), table[...])
    else:
        stream = stream_in[...]
    for s in range(seqs):
        x_out[s * length : (s + 1) * length, :] = stream[s * length : (s + 1) * length] + time_vec[s : s + 1]
    unit, _ = norm_stats(x_out[...])
    a_out[...] = (unit * vectors[0:1, :D] + vectors[1:2, :D]).astype(BF16)
    for c in range(3):
        part = slice(c * D, (c + 1) * D)
        qkv_out[:, part] = nn(a_out[...], w_qkv[:, part]).astype(BF16)
    masks = head_masks((length, LANES), 1.0 / math.sqrt(HD))
    for s in range(seqs):
        rows = slice(s * length, (s + 1) * length)
        for pair in range(HEADS // 2):
            cols = slice(pair * LANES, (pair + 1) * LANES)
            q = qkv_out[rows, pair * LANES : (pair + 1) * LANES]
            k = qkv_out[rows, D + pair * LANES : D + (pair + 1) * LANES]
            v_t = qkv_out[rows, 2 * D + pair * LANES : 2 * D + (pair + 1) * LANES].T
            mixed = []
            for h in range(2):
                scores = nt(k * masks[h], q)
                top = jnp.max(scores, 0, keepdims=True)
                expd = jnp.exp(scores - top)
                prob = (expd / jnp.sum(expd, 0, keepdims=True)).astype(BF16)
                prob_out[s * HEADS + 2 * pair + h] = prob
                mixed.append(nn(v_t[h * HD : (h + 1) * HD], prob))
            o_out[rows, cols] = jnp.concatenate(mixed, 0).T.astype(BF16)
    x2_out[...] = x_out[...] + nn(o_out[...], w_out[...])
    unit, _ = norm_stats(x2_out[...])
    a2_out[...] = (unit * vectors[3:4, :D] + vectors[4:5, :D]).astype(BF16)
    total = x2_out[...] + vectors[5:6, :D]
    for c in range(4):
        part = slice(c * D, (c + 1) * D)
        u = nn(a2_out[...], w_up[:, part]) + vectors[6:7, part]
        gl, slope = gelu_both(u)
        gl_out[:, part] = gl.astype(BF16)
        slope_out[:, part] = slope.astype(BF16)
        total = total + nn(gl_out[:, part], w_down[part, :])
    stream_out[...] = total.astype(stream_out.dtype)


def forward(layer, seqs, tokens, first_inputs, emb, weights, out_dtype):
    length = tokens // seqs
    shapes = (
        jax.ShapeDtypeStruct((tokens, D), out_dtype),
        jax.ShapeDtypeStruct((tokens, D), F32),
        jax.ShapeDtypeStruct((tokens, D), BF16),
        jax.ShapeDtypeStruct((tokens, 3 * D), BF16),
        jax.ShapeDtypeStruct((seqs * HEADS, length, length), BF16),
        jax.ShapeDtypeStruct((tokens, D), BF16),
        jax.ShapeDtypeStruct((tokens, D), F32),
        jax.ShapeDtypeStruct((tokens, D), BF16),
        jax.ShapeDtypeStruct((tokens, FF), BF16),
        jax.ShapeDtypeStruct((tokens, FF), BF16),
    )
    operands = list(first_inputs) + [emb] + list(weights)
    return pl.pallas_call(
        functools.partial(forward_kernel, layer, seqs),
        out_shape=shapes,
        in_specs=[VM] * len(operands),
        out_specs=(VM,) * len(shapes),
        **params(2 * tokens * 3216384 * 2, 3 * 10**7),
    )(*operands)


def place_chunks(geo, owners, flat, base, me, outs, fast):
    for d in owners:
        block = flat[pl.ds(geo.first(d, geo.shard) - base, geo.rows), :].astype(BF16)
        if fast:
            keep, send = outs
            relative = lax.bitwise_xor(me, d)
            row = lax.bitwise_and(relative, 4) + lax.bitwise_and(relative, 2)
            row = row + lax.bitwise_and(lax.shift_right_logical(relative, 3), 1)
            core = lax.bitwise_and(relative, 1)

            @pl.when(core == 0)
            def _():
                keep[row] = block

            @pl.when(core == 1)
            def _():
                send[row] = block
        else:
            outs[0][d - owners[0]] = block


def back_mlp_kernel(geo, layer, fast, place_ref, grad, x2, a2, gl, slope, w_up, w_down, vectors, *refs):
    grad_out, rest_out = refs[:2]
    outs = refs[2:-1]
    flat = refs[-1]
    base = ROW_GAIN_TWO
    tokens = x2.shape[0]
    grad_in = grad[...].astype(F32)
    grad_low = grad_in.astype(BF16)
    flat[pl.ds(ROW_END - base, CHUNK_PAD), :] = jnp.zeros((CHUNK_PAD, LANES), F32)
    grad_bias = jnp.sum(grad_low.astype(F32), 0, keepdims=True)
    for c in range(4):
        flat[pl.ds(ROW_B_DOWN - base + c, 1), :] = grad_bias[:, c * LANES : (c + 1) * LANES]
    normed_grad = jnp.zeros((tokens, D), F32)
    for j in range(4):
        part = slice(j * D, (j + 1) * D)
        hidden = nt(grad_low, w_down[part, :])
        up_grad = (hidden * slope[:, part].astype(F32)).astype(BF16)
        bias_grad = jnp.sum(up_grad.astype(F32), 0, keepdims=True)
        down = tn(gl[:, part], grad_low)
        up = tn(a2[...], up_grad)
        for c in range(4):
            cols = slice(c * LANES, (c + 1) * LANES)
            flat[pl.ds(ROW_B_UP - base + 4 * j + c, 1), :] = bias_grad[:, cols]
            flat[pl.ds(ROW_DOWN - base + 4 * D * j + c, D, stride=4), :] = down[:, cols]
            flat[pl.ds(ROW_UP - base + 4 * j + c, D, stride=16), :] = up[:, cols]
        normed_grad = normed_grad + nt(up_grad, w_up[:, part])
    back, grad_gain, grad_bias = norm_back(normed_grad, x2[...], vectors[3:4, :D])
    grad_out[...] = grad_in + back
    for c in range(4):
        cols = slice(c * LANES, (c + 1) * LANES)
        flat[pl.ds(ROW_GAIN_TWO - base + c, 1), :] = grad_gain[:, cols]
        flat[pl.ds(ROW_BIAS_TWO - base + c, 1), :] = grad_bias[:, cols]
    rest_out[...] = flat[pl.ds(0, rest_out.shape[0]), :]
    owners = list(range(geo.devices // 2, geo.devices))
    place_chunks(geo, owners, flat, base, place_ref[0], outs, fast)


def chunk_shapes(geo, fast):
    if fast:
        shape = jax.ShapeDtypeStruct((geo.devices // 4, geo.rows, LANES), BF16)
        return (shape, shape)
    return (jax.ShapeDtypeStruct((geo.devices // 2, geo.rows, LANES), BF16),)


def rest_rows(geo):
    middle = geo.first(geo.devices // 2, geo.shard)
    return ceil_to(middle + geo.rows - ROW_GAIN_TWO, 8)


def back_mlp(geo, layer, fast, place, grad, kept, weights):
    x2, a2, gl, slope = kept
    w_up, w_down, vectors = weights
    tokens = x2.shape[0]
    chunks = chunk_shapes(geo, fast)
    return pl.pallas_call(
        functools.partial(back_mlp_kernel, geo, layer, fast),
        out_shape=(
            jax.ShapeDtypeStruct((tokens, D), F32),
            jax.ShapeDtypeStruct((rest_rows(geo), LANES), F32),
        )
        + chunks,
        in_specs=[SM] + [VM] * 8,
        out_specs=(VM,) * (2 + len(chunks)),
        scratch_shapes=[pltpu.VMEM((ROW_END - ROW_GAIN_TWO + CHUNK_PAD, LANES), F32)],
        **params(4 * tokens * 2100000 * 2, 2 * 10**7),
    )(place, grad, x2, a2, gl, slope, w_up, w_down, vectors)


def back_attn_kernel(geo, layer, fast, seqs, place_ref, grad, x, a, qkv, prob, o, w_qkv, w_out, vectors, emb_t, rest, *refs):
    if layer == 0:
        chars = refs[0]
        refs = refs[1:]
    n_chunks = 2 if fast else 1
    if layer == 0:
        outs, embed_outs = refs[:n_chunks], refs[n_chunks : 2 * n_chunks]
        flat, qkv_grad, heads_grad, flat_table = refs[2 * n_chunks :]
    else:
        grad_out = refs[0]
        outs = refs[1 : 1 + n_chunks]
        flat, qkv_grad, heads_grad = refs[1 + n_chunks :]
    tokens = x.shape[0]
    length = tokens // seqs
    me = place_ref[0]
    flat[pl.ds(ROW_GAIN_TWO, rest.shape[0]), :] = rest[...]
    grad_in = grad[...]
    grad_low = grad_in.astype(BF16)
    out_grad = tn(o[...], grad_low)
    for c in range(4):
        flat[pl.ds(ROW_OUT + c, D, stride=4), :] = out_grad[:, c * LANES : (c + 1) * LANES]
    heads_grad[...] = nt(grad_low, w_out[...]).astype(BF16)
    masks = head_masks((length, LANES), 1.0)
    scale = 1.0 / math.sqrt(HD)
    lane = lax.broadcasted_iota(jnp.int32, (length, LANES), 1)
    for s in range(seqs):
        rows = slice(s * length, (s + 1) * length)
        for pair in range(HEADS // 2):
            cols = [slice(c * D + pair * LANES, c * D + (pair + 1) * LANES) for c in range(3)]
            q, k, v = qkv[rows, cols[0]], qkv[rows, cols[1]], qkv[rows, cols[2]]
            go = heads_grad[rows, cols[0]]
            k_t = k.T
            to_q, to_k, to_v = [], [], []
            for h in range(2):
                prob_low = prob[s * HEADS + 2 * pair + h]
                prob_full = prob_low.astype(F32)
                prob_grad = nt(v * masks[h], go)
                weighted = prob_full * prob_grad
                row_dot = jnp.sum(weighted, 0, keepdims=True)
                score_grad = (weighted - prob_full * row_dot).astype(BF16)
                to_q.append(nn(k_t[h * HD : (h + 1) * HD], score_grad))
                to_k.append(nn(score_grad, q))
                to_v.append(nn(prob_low, go))
            qkv_grad[rows, cols[0]] = (jnp.concatenate(to_q, 0).T * scale).astype(BF16)
            qkv_grad[rows, cols[1]] = (jnp.where(lane < HD, to_k[0], to_k[1]) * scale).astype(BF16)
            qkv_grad[rows, cols[2]] = jnp.where(lane < HD, to_v[0], to_v[1]).astype(BF16)
    normed_grad = jnp.zeros((tokens, D), F32)
    a_t = a[...].T
    for part in range(3):
        cols = slice(part * D, (part + 1) * D)
        piece = nn(a_t, qkv_grad[:, cols])
        for c in range(4):
            flat[pl.ds(ROW_QKV + 4 * part + c, D, stride=12), :] = piece[:, c * LANES : (c + 1) * LANES]
        normed_grad = normed_grad + nt(qkv_grad[:, cols], w_qkv[:, cols])
    back, grad_gain, grad_bias = norm_back(normed_grad, x[...], vectors[0:1, :D])
    total = grad_in + back
    if layer != 0:
        grad_out[...] = total
    time_grad = [
        jnp.sum(total[s * length : (s + 1) * length], 0, keepdims=True).astype(BF16).astype(F32) for s in range(seqs)
    ]
    bias_grad = sum(time_grad[1:], time_grad[0])
    weight_grad = sum(emb_t[:, s : s + 1] * time_grad[s] for s in range(seqs))
    for c in range(4):
        cols = slice(c * LANES, (c + 1) * LANES)
        flat[pl.ds(ROW_GAIN_ONE + c, 1), :] = grad_gain[:, cols]
        flat[pl.ds(ROW_BIAS_ONE + c, 1), :] = grad_bias[:, cols]
        flat[pl.ds(ROW_B_TIME + c, 1), :] = bias_grad[:, cols]
        flat[pl.ds(ROW_W_TIME + c, TD, stride=4), :] = weight_grad[:, cols]
    place_chunks(geo, list(range(geo.devices // 2)), flat, 0, me, outs, fast)
    if layer == 0:
        kind = lax.broadcasted_iota(jnp.int32, (32, tokens), 0)
        table_grad = nn((chars[...] == kind).astype(BF16), total.astype(BF16))
        for c in range(4):
            flat_table[pl.ds(c, 32, stride=4), :] = table_grad[:, c * LANES : (c + 1) * LANES]
        for d in range(geo.devices):
            block = flat_table[pl.ds(geo.first(d, geo.embed_shard), 8), :]
            if fast:
                relative = lax.bitwise_xor(me, d)
                row = lax.shift_right_logical(relative, 1)
                core = lax.bitwise_and(relative, 1)

                @pl.when(core == 0)
                def _():
                    embed_outs[0][row] = block

                @pl.when(core == 1)
                def _():
                    embed_outs[1][row] = block
            else:
                embed_outs[0][d] = block


def back_attn(geo, layer, fast, seqs, place, grad, kept, weights, emb_t, rest, chars_row):
    x, a, qkv, prob, o = kept
    w_qkv, w_out, vectors = weights
    tokens = x.shape[0]
    chunks = chunk_shapes(geo, fast)
    shapes = () if layer == 0 else (jax.ShapeDtypeStruct((tokens, D), F32),)
    shapes = shapes + chunks
    operands = [grad, x, a, qkv, prob, o, w_qkv, w_out, vectors, emb_t, rest]
    scratch = [
        pltpu.VMEM((ROW_GAIN_TWO + rest.shape[0], LANES), F32),
        pltpu.VMEM((tokens, 3 * D), BF16),
        pltpu.VMEM((tokens, D), BF16),
    ]
    if layer == 0:
        operands.append(chars_row)
        if fast:
            tables = (jax.ShapeDtypeStruct((geo.devices // 2, 8, LANES), F32),) * 2
        else:
            tables = (jax.ShapeDtypeStruct((geo.devices, 8, LANES), F32),)
        shapes = shapes + tables
        scratch.append(pltpu.VMEM((4 * 32, LANES), F32))
    return pl.pallas_call(
        functools.partial(back_attn_kernel, geo, layer, fast, seqs),
        out_shape=shapes,
        in_specs=[SM] + [VM] * len(operands),
        out_specs=(VM,) * len(shapes),
        scratch_shapes=scratch,
        **params(4 * tokens * 1100000 * 2, 2 * 10**7),
    )(place, *operands)


def permute(value, distance, devices):
    return lax.ppermute(value, AXES, [(d, d ^ distance) for d in range(devices)])


Z1, Z2, Z3, X, Y, CORE = 8, 16, 24, 4, 2, 1


def gather_fast(geo, chunk):
    n, rows = geo.devices, geo.rows
    half = ceil_to(rows // 2, 16)
    column = jnp.concatenate([chunk] + [permute(chunk, k, n) for k in (Z1, Z2, Z3)], 0)
    over_x, over_y = permute(column, X, n), permute(column, Y, n)
    cut_x = over_x.reshape(4, rows, LANES)[:, :half].reshape(-1, LANES)
    cut_y = over_y.reshape(4, rows, LANES)[:, half:].reshape(-1, LANES)
    corner_one, corner_two = permute(cut_x, Y, n), permute(cut_y, X, n)
    found = []
    for array, relative, at, count in (
        (column, 0, 0, rows),
        (over_x, X, 0, rows),
        (over_y, Y, 0, rows),
        (corner_one, X + Y, 0, half),
        (corner_two, X + Y, half, rows - half),
    ):
        for core in (0, CORE):
            held = permute(array, core, n) if core else array
            pieces = [(z * count, relative + core + 8 * z, None, at, count) for z in range(4)]
            found.append((held, pieces))
    return found


def gather_any(geo, chunk):
    gathered = lax.all_gather(chunk, AXES, axis=0)
    return [(gathered, [(0, 0, 0, 0, 0)])]


def add(*values):
    total = values[0].astype(F32)
    for value in values[1:]:
        total = total + value.astype(F32)
    return total


def plane_sum(geo, keep, send):
    n, rows = geo.devices, geo.rows
    half = ceil_to(rows // 2, 16)
    keep = keep.reshape(2, 2, 2, rows, LANES)
    came = permute(send, CORE, n).reshape(2, 2, 2, rows, LANES)
    one = add(keep[:, :, :, :half], came[:, :, :, :half])
    two = add(keep[:, :, :, half:], came[:, :, :, half:])
    from_x = permute(one[1].astype(BF16), X, n)
    from_y = permute(two[:, 1].astype(BF16), Y, n)
    one = add(one[0], from_x)
    two = add(two[:, 0], from_y)
    from_y = permute(one[1].astype(BF16), Y, n)
    from_x = permute(two[1].astype(BF16), X, n)
    return jnp.concatenate([add(one[0], from_y), add(two[0], from_x)], 1)


def column_sum(geo, place, upper, lower):
    n = geo.devices
    is_upper = place[3] >= 2
    near = jnp.where(is_upper, upper, lower)
    far = jnp.where(is_upper, lower, upper).astype(BF16)
    return [near[0], permute(near[1].astype(BF16), Z1, n), permute(far[0], Z2, n), permute(far[1], Z3, n)]


def table_sum(geo, keep, send):
    n = geo.devices
    total = add(keep, permute(send.astype(BF16), CORE, n)).reshape(4, 2, 2, 8, LANES)
    total = add(total[:, 0], permute(total[:, 1].astype(BF16), X, n))
    total = add(total[:, 0], permute(total[:, 1].astype(BF16), Y, n))
    low = total.astype(BF16)
    return [total[0]] + [permute(low[k], 8 * k, n) for k in (1, 2, 3)]


def sum_any(chunks):
    total = lax.psum_scatter(chunks.astype(F32), AXES, scatter_dimension=0, tiled=True)[0]
    zero = jnp.zeros_like(total)
    return [total, zero, zero, zero]


def timestep_embed(step_ids):
    half_dim = TD // 2
    freq_base = jnp.exp(jnp.arange(half_dim, dtype=F32) * (-math.log(10000.0) / half_dim))
    angle_grid = step_ids.astype(F32)[:, None] * freq_base[None, :]
    return jnp.concatenate([jnp.sin(angle_grid), jnp.cos(angle_grid)], axis=1)


def body(fast, chars, steps, embed, layer_params, cotangent):
    seqs, length = chars.shape
    tokens = seqs * length
    geo = Geometry(lax.axis_size(AXES), layer_params.shape[1], embed.shape[0])
    index = lax.axis_index(AXES).astype(jnp.int32)
    place = jnp.stack(
        [index, index * geo.shard % LANES, index * geo.embed_shard % LANES, index // 8]
    ).astype(jnp.int32)
    gather = gather_fast if fast else gather_any
    chunks = pack_shards(geo, place, layer_params, embed)
    emb = timestep_embed(steps).astype(BF16)
    emb_rows = jnp.concatenate([emb, jnp.zeros((8 - seqs, TD), BF16)], 0) if seqs < 8 else emb
    emb_t = emb.astype(F32).T
    gathered = [gather(geo, chunk) for chunk in chunks]

    stream = None
    kept, weights = [], []
    for layer in range(2):
        got = unpack(geo, layer, place, gathered[layer])
        if layer == 0:
            first_inputs = [chars.reshape(tokens, 1), got[6]]
        else:
            first_inputs = [stream]
        stream, *saved = forward(
            layer, seqs, tokens, first_inputs, emb_rows, got[:6], F32 if layer == 0 else BF16
        )
        kept.append(saved)
        weights.append(got[:6])
    output = stream.reshape(seqs, length, D)

    grad = cotangent.reshape(tokens, D)
    sums = [None, None]
    for layer in (1, 0):
        x, a, qkv, prob, o, x2, a2, gl, slope = kept[layer]
        w_time, w_qkv, w_out, w_up, w_down, vectors = weights[layer]
        grad, rest, *upper = back_mlp(
            geo, layer, fast, place, grad, (x2, a2, gl, slope), (w_up, w_down, vectors)
        )
        if fast:
            upper = plane_sum(geo, *upper)
        got = back_attn(
            geo,
            layer,
            fast,
            seqs,
            place,
            grad,
            (x, a, qkv, prob, o),
            (w_qkv, w_out, vectors),
            emb_t,
            rest,
            chars.reshape(1, tokens),
        )
        if layer == 0:
            lower, tables = (got[:2], got[2:]) if fast else (got[:1], got[1:])
        else:
            grad, *lower = got
        if fast:
            sums[layer] = column_sum(geo, place, upper, plane_sum(geo, *lower))
        else:
            sums[layer] = sum_any(jnp.concatenate([lower[0], upper[0]], 0))
    tables = table_sum(geo, *tables) if fast else sum_any(tables[0])
    grad_params, grad_embed = finish(geo, place, sums[0], sums[1], tables)
    return (output, grad_embed, grad_params)


def solution(mesh):
    both = P(AXES)
    fast = dict(mesh.shape) == {"dp": 8, "fsdp": 4}
    return jax.shard_map(
        functools.partial(body, fast),
        mesh=mesh,
        in_specs=(P(AXES, None), both, both, P(None, AXES), P(AXES, None, None)),
        out_specs=(P(AXES, None, None), both, P(None, AXES)),
        check_vma=False,
    )
```

```python
import functools
import math

import jax
import jax.numpy as jnp
from jax import lax
from jax.experimental import pallas as pl
from jax.experimental.pallas import tpu as pltpu
from jax.sharding import PartitionSpec as P

D = 512
HEADS = 8
FF = 2048
VOCAB = 27
TD = 128
HD = 64
LANES = 128
EPSILON = 1e-05
AXES = ("dp", "fsdp")
F32 = jnp.float32
BF16 = jnp.bfloat16
VMEM_BYTES = 52 * 2**20

ROW_GAIN_ONE, ROW_BIAS_ONE, ROW_W_TIME, ROW_B_TIME = 0, 4, 8, 520
ROW_QKV, ROW_OUT, ROW_GAIN_TWO, ROW_BIAS_TWO = 524, 6668, 8716, 8720
ROW_UP, ROW_B_UP, ROW_DOWN, ROW_B_DOWN, ROW_END = 8724, 16916, 16932, 25124, 25128
CHUNK_PAD = 832


def ceil_to(value, step):
    return -(-value // step) * step


class Geometry:
    def __init__(self, devices, shard, embed_shard):
        self.devices, self.shard, self.embed_shard = devices, shard, embed_shard
        self.param_rows = max(self.count(d, shard) for d in range(devices))
        self.embed_rows = max(self.count(d, embed_shard) for d in range(devices))
        self.embed_at = ceil_to(self.param_rows, 8)
        self.rows = ceil_to(max(self.embed_at + 8, self.param_rows + 2 * self.embed_rows), 16)

    @staticmethod
    def first(d, size):
        return d * size // LANES

    @staticmethod
    def count(d, size):
        return -(-(d + 1) * size // LANES) - d * size // LANES


def params(flops, nbytes, weight=0):
    flops, nbytes = max(flops * weight, 1000), max(nbytes * weight, 1000)
    return dict(
        compiler_params=pltpu.CompilerParams(vmem_limit_bytes=VMEM_BYTES),
        cost_estimate=pl.CostEstimate(flops=flops, bytes_accessed=nbytes, transcendentals=0),
    )


VM = pl.BlockSpec(memory_space=pltpu.VMEM)
SM = pl.BlockSpec(memory_space=pltpu.SMEM)
ANY = pl.BlockSpec(memory_space=pl.ANY)


def nn(left, right):
    return lax.dot_general(left, right, (((1,), (0,)), ((), ())), preferred_element_type=F32)


def nt(left, right):
    return lax.dot_general(left, right, (((1,), (1,)), ((), ())), preferred_element_type=F32)


def tn(left, right):
    return nn(left.T, right)


def shift_in(flat, offset):
    rolled = pltpu.roll(flat, offset, 1)
    above = jnp.concatenate([jnp.zeros((1, LANES), F32), rolled[:-1]], 0)
    lane = lax.broadcasted_iota(jnp.int32, flat.shape, 1)
    return jnp.where(lane >= offset, rolled, above)


def shift_out(flat, offset):
    rolled = pltpu.roll(flat, lax.rem(LANES - offset, LANES), 1)
    below = jnp.concatenate([rolled[1:], jnp.zeros((1, LANES), F32)], 0)
    lane = lax.broadcasted_iota(jnp.int32, flat.shape, 1)
    return jnp.where(lane < LANES - offset, rolled, below)


def pack_kernel(geo, place_ref, layers_ref, embed_ref, first_ref, second_ref):
    main = geo.embed_at
    for layer, out_ref in ((0, first_ref), (1, second_ref)):
        moved = shift_in(layers_ref[layer].astype(F32), place_ref[1])
        if layer == 0:
            tail = shift_in(embed_ref[...].astype(F32), place_ref[2])
            parts = [moved[:main], tail] + ([moved[main + 8 :]] if geo.rows > main + 8 else [])
            moved = jnp.concatenate(parts, 0)
        out_ref[...] = moved.astype(BF16)


def pack_shards(geo, place, layer_params, embed):
    layers = jnp.pad(layer_params, ((0, 0), (0, geo.rows * LANES - geo.shard)))
    table = jnp.pad(embed, (0, 8 * LANES - geo.embed_shard))
    out = jax.ShapeDtypeStruct((geo.rows, LANES), BF16)
    return pl.pallas_call(
        functools.partial(pack_kernel, geo),
        out_shape=(out, out),
        in_specs=[SM, VM, VM],
        out_specs=(VM, VM),
        **params(10**6, geo.rows * 1024),
    )(place, layers.reshape(2, geo.rows, LANES), table.reshape(8, LANES))


def finish_kernel(geo, fast, place_ref, *refs):
    grads_ref, embed_ref = refs[-2:]
    parts = refs[:-2]
    count = 4 if fast else 1
    for layer in range(2):
        total = parts[layer * count][...].astype(F32)
        for part in parts[layer * count + 1 : (layer + 1) * count]:
            total = total + part[...].astype(F32)
        grads_ref[layer] = shift_out(total, place_ref[1])
        if fast and layer == 0:
            first, size = geo.param_rows, geo.embed_rows
            lower, upper = total[first : first + size], total[first + size : first + 2 * size]
            tail = jnp.where(place_ref[3] >= 2, upper, lower)
            tail = jnp.concatenate([tail, jnp.zeros((8 - size, LANES), F32)], 0)
    if not fast:
        tail = parts[2][...]
    embed_ref[...] = shift_out(tail, place_ref[2])


def finish(geo, fast, place, operands):
    grads, table = pl.pallas_call(
        functools.partial(finish_kernel, geo, fast),
        out_shape=(
            jax.ShapeDtypeStruct((2, geo.rows, LANES), F32),
            jax.ShapeDtypeStruct((8, LANES), F32),
        ),
        in_specs=[SM] + [VM] * len(operands),
        out_specs=(VM, VM),
        **params(10**6, geo.rows * 4096),
    )(place, *operands)
    grads = grads.reshape(2, geo.rows * LANES)[:, : geo.shard]
    return grads, table.reshape(-1)[: geo.embed_shard]


def unpack_kernel(geo, layer, plan, place_ref, *refs):
    n_in = len(plan)
    chunk_refs = refs[:n_in]
    w_time, w_qkv, w_out, w_up, w_down, vectors = refs[n_in : n_in + 6]
    table = refs[n_in + 6] if layer == 0 else None
    held, flat, flat_table, sems = refs[-4:]
    me = place_ref[0]
    copies = []
    for source, pieces in zip(chunk_refs, plan):
        for src_at, relative, absolute, dst_at, count in pieces:
            if absolute is None:
                target = held.at[lax.bitwise_xor(me, relative), pl.ds(dst_at, count)]
                origin = source.at[pl.ds(src_at, count)]
            else:
                target, origin = held, source
            copies.append(pltpu.make_async_copy(origin, target, sems.at[len(copies)]))
    for copy in copies:
        copy.start()
    for copy in copies:
        copy.wait()
    for d in range(geo.devices):
        block = held[d].astype(F32)
        start, rows = geo.first(d, geo.shard), geo.count(d, geo.shard)
        split = (d * geo.shard) % LANES != 0
        if split:
            shared = flat[pl.ds(start, 1), :] + block[:1]
        flat[pl.ds(start, rows), :] = block[:rows]
        if split:
            flat[pl.ds(start, 1), :] = shared
        if layer == 0:
            tail = block[geo.embed_at : geo.embed_at + 8]
            start, rows = geo.first(d, geo.embed_shard), geo.count(d, geo.embed_shard)
            split = (d * geo.embed_shard) % LANES != 0
            if split:
                shared = flat_table[pl.ds(start, 1), :] + tail[:1]
            flat_table[pl.ds(start, rows), :] = tail[:rows]
            if split:
                flat_table[pl.ds(start, 1), :] = shared
    for out, start, rows, width in (
        (w_time, ROW_W_TIME, TD, 4),
        (w_qkv, ROW_QKV, D, 12),
        (w_out, ROW_OUT, D, 4),
        (w_up, ROW_UP, D, 16),
        (w_down, ROW_DOWN, FF, 4),
    ):
        for c in range(width):
            out[:, c * LANES : (c + 1) * LANES] = flat[pl.ds(start + c, rows, stride=width), :].astype(BF16)
    for row, start, width in (
        (0, ROW_GAIN_ONE, 4),
        (1, ROW_BIAS_ONE, 4),
        (2, ROW_B_TIME, 4),
        (3, ROW_GAIN_TWO, 4),
        (4, ROW_BIAS_TWO, 4),
        (5, ROW_B_DOWN, 4),
        (6, ROW_B_UP, 16),
    ):
        for c in range(width):
            vectors[row : row + 1, c * LANES : (c + 1) * LANES] = flat[pl.ds(start + c, 1), :]
    if layer == 0:
        table[...] = jnp.zeros(table.shape, BF16)
        for c in range(4):
            table[0:VOCAB, c * LANES : (c + 1) * LANES] = flat_table[pl.ds(c, VOCAB, stride=4), :].astype(BF16)


def unpack(geo, layer, place, gathered):
    arrays = [array for array, pieces in gathered]
    plan = tuple(tuple(pieces) for array, pieces in gathered)
    shapes = [
        jax.ShapeDtypeStruct((TD, D), BF16),
        jax.ShapeDtypeStruct((D, 3 * D), BF16),
        jax.ShapeDtypeStruct((D, D), BF16),
        jax.ShapeDtypeStruct((D, FF), BF16),
        jax.ShapeDtypeStruct((FF, D), BF16),
        jax.ShapeDtypeStruct((8, FF), F32),
    ]
    if layer == 0:
        shapes.append(jax.ShapeDtypeStruct((32, D), BF16))
    return pl.pallas_call(
        functools.partial(unpack_kernel, geo, layer, plan),
        out_shape=tuple(shapes),
        in_specs=[SM] + [ANY] * len(arrays),
        out_specs=(VM,) * len(shapes),
        scratch_shapes=[
            pltpu.VMEM((geo.devices, geo.rows, LANES), BF16),
            pltpu.VMEM((ROW_END + 8, LANES), F32),
            pltpu.VMEM((4 * 32, LANES), F32),
            pltpu.SemaphoreType.DMA((sum(len(pieces) for pieces in plan),)),
        ],
        **params(10**7, 4 * 6432768, 1),
    )(place, *arrays)


def norm_stats(values):
    mean = jnp.mean(values, -1, keepdims=True)
    centered = values - mean
    variance = jnp.mean(centered * centered, -1, keepdims=True)
    scale = lax.rsqrt(variance + EPSILON)
    return centered * scale, scale


def norm_back(grad, values, gain):
    unit, scale = norm_stats(values)
    grad_gain = jnp.sum(grad * unit, 0, keepdims=True)
    grad_bias = jnp.sum(grad, 0, keepdims=True)
    inner = grad * gain
    shifted = inner - jnp.mean(inner, -1, keepdims=True)
    return scale * (shifted - unit * jnp.mean(inner * unit, -1, keepdims=True)), grad_gain, grad_bias


def gelu_both(u):
    root = math.sqrt(2.0 / math.pi)
    square = u * u
    t = jnp.tanh(root * (u + 0.044715 * (square * u)))
    half = 0.5 * (1.0 + t)
    slope = half + 0.5 * u * (1.0 - t * t) * (root * (1.0 + 3.0 * 0.044715 * square))
    return u * half, slope


def head_masks(shape, scale):
    lane = lax.broadcasted_iota(jnp.int32, shape, 1)
    one = jnp.where(lane < HD, scale, 0.0).astype(BF16)
    two = jnp.where(lane < HD, 0.0, scale).astype(BF16)
    return one, two


def ahead_attn_kernel(layer, seqs, *refs):
    if layer == 0:
        chars, table = refs[:2]
        refs = refs[2:]
    else:
        stream_in = refs[0]
        refs = refs[1:]
    emb, w_time, w_qkv, w_out, vectors = refs[:5]
    x_out, a_out, qkv_out, prob_out, o_out, x2_out, a2_out = refs[5:]
    tokens = x_out.shape[0]
    length = tokens // seqs
    time_vec = nn(emb[...], w_time[...]) + vectors[2:3, :D]
    if layer == 0:
        lane = lax.broadcasted_iota(jnp.int32, (tokens, 32), 1)
        stream = nn((chars[...] == lane).astype(BF16), table[...])
    else:
        stream = stream_in[...]
    for s in range(seqs):
        x_out[s * length : (s + 1) * length, :] = stream[s * length : (s + 1) * length] + time_vec[s : s + 1]
    unit, _ = norm_stats(x_out[...])
    a_out[...] = (unit * vectors[0:1, :D] + vectors[1:2, :D]).astype(BF16)
    for c in range(3):
        part = slice(c * D, (c + 1) * D)
        qkv_out[:, part] = nn(a_out[...], w_qkv[:, part]).astype(BF16)
    masks = head_masks((length, LANES), 1.0 / math.sqrt(HD))
    for s in range(seqs):
        rows = slice(s * length, (s + 1) * length)
        for pair in range(HEADS // 2):
            cols = slice(pair * LANES, (pair + 1) * LANES)
            q = qkv_out[rows, pair * LANES : (pair + 1) * LANES]
            k = qkv_out[rows, D + pair * LANES : D + (pair + 1) * LANES]
            v_t = qkv_out[rows, 2 * D + pair * LANES : 2 * D + (pair + 1) * LANES].T
            mixed = []
            for h in range(2):
                scores = nt(k * masks[h], q)
                top = jnp.max(scores, 0, keepdims=True)
                expd = jnp.exp(scores - top)
                prob = (expd / jnp.sum(expd, 0, keepdims=True)).astype(BF16)
                prob_out[s * HEADS + 2 * pair + h] = prob
                mixed.append(nn(v_t[h * HD : (h + 1) * HD], prob))
            o_out[rows, cols] = jnp.concatenate(mixed, 0).T.astype(BF16)
    x2_out[...] = x_out[...] + nn(o_out[...], w_out[...])
    unit, _ = norm_stats(x2_out[...])
    a2_out[...] = (unit * vectors[3:4, :D] + vectors[4:5, :D]).astype(BF16)


def ahead_attn(layer, seqs, tokens, first_inputs, emb, weights):
    length = tokens // seqs
    shapes = (
        jax.ShapeDtypeStruct((tokens, D), F32),
        jax.ShapeDtypeStruct((tokens, D), BF16),
        jax.ShapeDtypeStruct((tokens, 3 * D), BF16),
        jax.ShapeDtypeStruct((seqs * HEADS, length, length), BF16),
        jax.ShapeDtypeStruct((tokens, D), BF16),
        jax.ShapeDtypeStruct((tokens, D), F32),
        jax.ShapeDtypeStruct((tokens, D), BF16),
    )
    operands = list(first_inputs) + [emb] + list(weights)
    return pl.pallas_call(
        functools.partial(ahead_attn_kernel, layer, seqs),
        out_shape=shapes,
        in_specs=[VM] * len(operands),
        out_specs=(VM,) * len(shapes),
        **params(2 * tokens * 1100000 * 2, 10**7, 1),
    )(*operands)


def ahead_mlp_kernel(x2, a2, w_up, w_down, vectors, stream_out, gl_out, slope_out):
    total = x2[...] + vectors[5:6, :D]
    for c in range(4):
        part = slice(c * D, (c + 1) * D)
        u = nn(a2[...], w_up[:, part]) + vectors[6:7, part]
        gl, slope = gelu_both(u)
        gl_out[:, part] = gl.astype(BF16)
        slope_out[:, part] = slope.astype(BF16)
        total = total + nn(gl_out[:, part], w_down[part, :])
    stream_out[...] = total.astype(stream_out.dtype)


def ahead_mlp(x2, a2, w_up, w_down, vectors, out_dtype):
    tokens = x2.shape[0]
    shapes = (
        jax.ShapeDtypeStruct((tokens, D), out_dtype),
        jax.ShapeDtypeStruct((tokens, FF), BF16),
        jax.ShapeDtypeStruct((tokens, FF), BF16),
    )
    return pl.pallas_call(
        ahead_mlp_kernel,
        out_shape=shapes,
        in_specs=[VM] * 5,
        out_specs=(VM,) * 3,
        **params(2 * tokens * 2100000 * 2, 10**7, 1),
    )(x2, a2, w_up, w_down, vectors)


def place_chunks(geo, owners, flat, base, me, outs, fast, table=None):
    for d in owners:
        block = flat[pl.ds(geo.first(d, geo.shard) - base, geo.rows), :]
        if table is not None:
            first, size = geo.param_rows, geo.embed_rows
            tails = [
                table[pl.ds(geo.first(e, geo.embed_shard), size), :] for e in (d, d + geo.devices // 2)
            ]
            block = jnp.concatenate([block[:first], *tails, block[first + 2 * size :]], 0)
        block = block.astype(BF16)
        if fast:
            keep, send = outs
            relative = lax.bitwise_xor(me, d)
            row = lax.bitwise_and(relative, 4) + lax.bitwise_and(relative, 2)
            row = row + lax.bitwise_and(lax.shift_right_logical(relative, 3), 1)
            core = lax.bitwise_and(relative, 1)

            @pl.when(core == 0)
            def _():
                keep[row] = block

            @pl.when(core == 1)
            def _():
                send[row] = block
        else:
            outs[0][d - owners[0]] = block


def back_mlp_kernel(geo, layer, fast, place_ref, grad, x2, a2, gl, slope, w_up, w_down, vectors, *refs):
    grad_out, rest_out = refs[:2]
    outs = refs[2:-1]
    flat = refs[-1]
    base = ROW_GAIN_TWO
    tokens = x2.shape[0]
    grad_in = grad[...].astype(F32)
    grad_low = grad_in.astype(BF16)
    flat[pl.ds(ROW_END - base, CHUNK_PAD), :] = jnp.zeros((CHUNK_PAD, LANES), F32)
    grad_bias = jnp.sum(grad_low.astype(F32), 0, keepdims=True)
    for c in range(4):
        flat[pl.ds(ROW_B_DOWN - base + c, 1), :] = grad_bias[:, c * LANES : (c + 1) * LANES]
    normed_grad = jnp.zeros((tokens, D), F32)
    for j in range(4):
        part = slice(j * D, (j + 1) * D)
        hidden = nt(grad_low, w_down[part, :])
        up_grad = (hidden * slope[:, part].astype(F32)).astype(BF16)
        bias_grad = jnp.sum(up_grad.astype(F32), 0, keepdims=True)
        down = tn(gl[:, part], grad_low)
        up = tn(a2[...], up_grad)
        for c in range(4):
            cols = slice(c * LANES, (c + 1) * LANES)
            flat[pl.ds(ROW_B_UP - base + 4 * j + c, 1), :] = bias_grad[:, cols]
            flat[pl.ds(ROW_DOWN - base + 4 * D * j + c, D, stride=4), :] = down[:, cols]
            flat[pl.ds(ROW_UP - base + 4 * j + c, D, stride=16), :] = up[:, cols]
        normed_grad = normed_grad + nt(up_grad, w_up[:, part])
    back, grad_gain, grad_bias = norm_back(normed_grad, x2[...], vectors[3:4, :D])
    grad_out[...] = grad_in + back
    for c in range(4):
        cols = slice(c * LANES, (c + 1) * LANES)
        flat[pl.ds(ROW_GAIN_TWO - base + c, 1), :] = grad_gain[:, cols]
        flat[pl.ds(ROW_BIAS_TWO - base + c, 1), :] = grad_bias[:, cols]
    rest_out[...] = flat[pl.ds(0, rest_out.shape[0]), :]
    owners = list(range(geo.devices // 2, geo.devices))
    place_chunks(geo, owners, flat, base, place_ref[0], outs, fast)


def chunk_shapes(geo, fast):
    if fast:
        shape = jax.ShapeDtypeStruct((geo.devices // 4, geo.rows, LANES), BF16)
        return (shape, shape)
    return (jax.ShapeDtypeStruct((geo.devices // 2, geo.rows, LANES), BF16),)


def rest_rows(geo):
    middle = geo.first(geo.devices // 2, geo.shard)
    return ceil_to(middle + geo.rows - ROW_GAIN_TWO, 8)


def back_mlp(geo, layer, fast, place, grad, kept, weights):
    x2, a2, gl, slope = kept
    w_up, w_down, vectors = weights
    tokens = x2.shape[0]
    chunks = chunk_shapes(geo, fast)
    return pl.pallas_call(
        functools.partial(back_mlp_kernel, geo, layer, fast),
        out_shape=(
            jax.ShapeDtypeStruct((tokens, D), F32),
            jax.ShapeDtypeStruct((rest_rows(geo), LANES), F32),
        )
        + chunks,
        in_specs=[SM] + [VM] * 8,
        out_specs=(VM,) * (2 + len(chunks)),
        scratch_shapes=[pltpu.VMEM((ROW_END - ROW_GAIN_TWO + CHUNK_PAD, LANES), F32)],
        **params(4 * tokens * 2100000 * 2, 2 * 10**7, 1),
    )(place, grad, x2, a2, gl, slope, w_up, w_down, vectors)


def back_attn_kernel(geo, layer, fast, seqs, place_ref, grad, x, a, qkv, prob, o, w_qkv, w_out, vectors, emb_t, rest, *refs):
    if layer == 0:
        chars = refs[0]
        refs = refs[1:]
    n_chunks = 2 if fast else 1
    if layer == 0:
        outs, embed_outs = refs[:n_chunks], refs[n_chunks:-4]
        flat, qkv_grad, heads_grad, flat_table = refs[-4:]
    else:
        grad_out = refs[0]
        outs = refs[1 : 1 + n_chunks]
        flat, qkv_grad, heads_grad = refs[1 + n_chunks :]
    tokens = x.shape[0]
    length = tokens // seqs
    me = place_ref[0]
    flat[pl.ds(ROW_GAIN_TWO, rest.shape[0]), :] = rest[...]
    grad_in = grad[...]
    grad_low = grad_in.astype(BF16)
    out_grad = tn(o[...], grad_low)
    for c in range(4):
        flat[pl.ds(ROW_OUT + c, D, stride=4), :] = out_grad[:, c * LANES : (c + 1) * LANES]
    heads_grad[...] = nt(grad_low, w_out[...]).astype(BF16)
    masks = head_masks((length, LANES), 1.0)
    scale = 1.0 / math.sqrt(HD)
    lane = lax.broadcasted_iota(jnp.int32, (length, LANES), 1)
    for s in range(seqs):
        rows = slice(s * length, (s + 1) * length)
        for pair in range(HEADS // 2):
            cols = [slice(c * D + pair * LANES, c * D + (pair + 1) * LANES) for c in range(3)]
            q, k, v = qkv[rows, cols[0]], qkv[rows, cols[1]], qkv[rows, cols[2]]
            go = heads_grad[rows, cols[0]]
            k_t = k.T
            to_q, to_k, to_v = [], [], []
            for h in range(2):
                prob_low = prob[s * HEADS + 2 * pair + h]
                prob_full = prob_low.astype(F32)
                prob_grad = nt(v * masks[h], go)
                weighted = prob_full * prob_grad
                row_dot = jnp.sum(weighted, 0, keepdims=True)
                score_grad = (weighted - prob_full * row_dot).astype(BF16)
                to_q.append(nn(k_t[h * HD : (h + 1) * HD], score_grad))
                to_k.append(nn(score_grad, q))
                to_v.append(nn(prob_low, go))
            qkv_grad[rows, cols[0]] = (jnp.concatenate(to_q, 0).T * scale).astype(BF16)
            qkv_grad[rows, cols[1]] = (jnp.where(lane < HD, to_k[0], to_k[1]) * scale).astype(BF16)
            qkv_grad[rows, cols[2]] = jnp.where(lane < HD, to_v[0], to_v[1]).astype(BF16)
    normed_grad = jnp.zeros((tokens, D), F32)
    a_t = a[...].T
    for part in range(3):
        cols = slice(part * D, (part + 1) * D)
        piece = nn(a_t, qkv_grad[:, cols])
        for c in range(4):
            flat[pl.ds(ROW_QKV + 4 * part + c, D, stride=12), :] = piece[:, c * LANES : (c + 1) * LANES]
        normed_grad = normed_grad + nt(qkv_grad[:, cols], w_qkv[:, cols])
    back, grad_gain, grad_bias = norm_back(normed_grad, x[...], vectors[0:1, :D])
    total = grad_in + back
    if layer != 0:
        grad_out[...] = total
    time_grad = [
        jnp.sum(total[s * length : (s + 1) * length], 0, keepdims=True).astype(BF16).astype(F32) for s in range(seqs)
    ]
    bias_grad = sum(time_grad[1:], time_grad[0])
    weight_grad = sum(emb_t[:, s : s + 1] * time_grad[s] for s in range(seqs))
    for c in range(4):
        cols = slice(c * LANES, (c + 1) * LANES)
        flat[pl.ds(ROW_GAIN_ONE + c, 1), :] = grad_gain[:, cols]
        flat[pl.ds(ROW_BIAS_ONE + c, 1), :] = grad_bias[:, cols]
        flat[pl.ds(ROW_B_TIME + c, 1), :] = bias_grad[:, cols]
        flat[pl.ds(ROW_W_TIME + c, TD, stride=4), :] = weight_grad[:, cols]
    if layer == 0:
        kind = lax.broadcasted_iota(jnp.int32, (32, tokens), 0)
        table_grad = nn((chars[...] == kind).astype(BF16), total.astype(BF16))
        for c in range(4):
            flat_table[pl.ds(c, 32, stride=4), :] = table_grad[:, c * LANES : (c + 1) * LANES]
    owners = list(range(geo.devices // 2))
    place_chunks(geo, owners, flat, 0, me, outs, fast, flat_table if layer == 0 and fast else None)
    if layer == 0 and not fast:
        for d in range(geo.devices):
            embed_outs[0][d] = flat_table[pl.ds(geo.first(d, geo.embed_shard), 8), :]


def back_attn(geo, layer, fast, seqs, place, grad, kept, weights, emb_t, rest, chars_row):
    x, a, qkv, prob, o = kept
    w_qkv, w_out, vectors = weights
    tokens = x.shape[0]
    chunks = chunk_shapes(geo, fast)
    shapes = () if layer == 0 else (jax.ShapeDtypeStruct((tokens, D), F32),)
    shapes = shapes + chunks
    operands = [grad, x, a, qkv, prob, o, w_qkv, w_out, vectors, emb_t, rest]
    scratch = [
        pltpu.VMEM((ROW_GAIN_TWO + rest.shape[0], LANES), F32),
        pltpu.VMEM((tokens, 3 * D), BF16),
        pltpu.VMEM((tokens, D), BF16),
    ]
    if layer == 0:
        operands.append(chars_row)
        if not fast:
            shapes = shapes + (jax.ShapeDtypeStruct((geo.devices, 8, LANES), F32),)
        scratch.append(pltpu.VMEM((4 * 32, LANES), F32))
    return pl.pallas_call(
        functools.partial(back_attn_kernel, geo, layer, fast, seqs),
        out_shape=shapes,
        in_specs=[SM] + [VM] * len(operands),
        out_specs=(VM,) * len(shapes),
        scratch_shapes=scratch,
        **params(4 * tokens * 1100000 * 2, 2 * 10**7, 1),
    )(place, *operands)


def permute(value, distance, devices):
    return lax.ppermute(value, AXES, [(d, d ^ distance) for d in range(devices)])


Z1, Z2, Z3, X, Y, CORE = 8, 16, 24, 4, 2, 1


def after(value, *others):
    return lax.optimization_barrier((value, *others))[0]


def sync(*values):
    return lax.optimization_barrier(values)


def gather_both(geo, first, second):
    n, rows = geo.devices, geo.rows
    half = ceil_to(rows // 2, 16)

    def sides(held):
        return permute(held, X, n), permute(held, Y, n)

    def corners(over_x, over_y):
        return permute(over_x[:half], Y, n), permute(over_y[half:], X, n)

    def other(*arrays):
        return permute(jnp.concatenate(arrays, 0), CORE, n)

    near, over = permute(first, Z1, n), permute(first, Z2, n)
    sides_0 = sides(first)
    sides_0 = sync(*sides_0)
    corners_0 = corners(*sides_0)
    near, _ = sync(near, sides_0[0])
    sides_1 = sides(near)
    over, _ = sync(over, near)
    far = permute(over, Z1, n)
    sides_2 = sides(over)
    *sides_1, _ = sync(*sides_1, over)
    corners_1 = corners(*sides_1)
    far, *corners_0 = sync(far, *corners_0, sides_1[0])[:3]
    sides_3 = sides(far)
    other_0 = other(first, *sides_0, *corners_0)
    second, _ = sync(second, far)
    near_b, over_b = permute(second, Z1, n), permute(second, Z2, n)
    *sides_2, _ = sync(*sides_2, far)
    corners_2 = corners(*sides_2)
    *corners_1, _ = sync(*corners_1, sides_2[0])
    other_1 = other(near, *sides_1, *corners_1)
    *sides_3, _ = sync(*sides_3, sides_2[0])
    corners_3 = corners(*sides_3)
    over_b, near_b, _ = sync(over_b, near_b, sides_3[0])
    far_b = permute(over_b, Z1, n)
    *corners_2, _ = sync(*corners_2, sides_3[0])
    other_2 = other(over, *sides_2, *corners_2)
    *corners_3, far_b, _ = sync(*corners_3, far_b, corners_2[0])
    other_3 = other(far, *sides_3, *corners_3)
    column = jnp.concatenate([second, near_b, over_b, far_b], 0)
    found = []
    for z, arrays, packed in (
        (0, (first, *sides_0, *corners_0), other_0),
        (Z1, (near, *sides_1, *corners_1), other_1),
        (Z2, (over, *sides_2, *corners_2), other_2),
        (Z3, (far, *sides_3, *corners_3), other_3),
    ):
        pieces = [
            (0, z, None, 0, rows),
            (rows, z + X, None, 0, rows),
            (2 * rows, z + Y, None, 0, rows),
            (3 * rows, z + X + Y, None, 0, half),
            (3 * rows + half, z + X + Y, None, half, rows - half),
        ]
        for array, (_, relative, _, at, count) in zip(arrays, pieces):
            found.append((array, [(0, relative, None, at, count)]))
        found.append((packed, [(src, rel + CORE, None, at, count) for src, rel, _, at, count in pieces]))
    return found, column


def gather_sides(geo, column):
    return permute(column, X, geo.devices), permute(column, Y, geo.devices)


def gather_corners(geo, over_x, over_y):
    n, rows = geo.devices, geo.rows
    half = ceil_to(rows // 2, 16)
    cut_x = over_x.reshape(4, rows, LANES)[:, :half].reshape(-1, LANES)
    cut_y = over_y.reshape(4, rows, LANES)[:, half:].reshape(-1, LANES)
    return permute(cut_x, Y, n), permute(cut_y, X, n)


def gathered_pieces(geo, arrays, others):
    rows = geo.rows
    half = ceil_to(rows // 2, 16)
    found = []
    for core, group in ((0, arrays), (CORE, others)):
        for array, (relative, at, count) in zip(
            group, ((0, 0, rows), (X, 0, rows), (Y, 0, rows), (X + Y, 0, half), (X + Y, half, rows - half))
        ):
            found.append((array, [(z * count, relative + core + 8 * z, None, at, count) for z in range(4)]))
    return found


def gather_any(geo, chunk):
    gathered = lax.all_gather(chunk, AXES, axis=0)
    return [(gathered, [(0, 0, 0, 0, 0)])]


def add(*values):
    total = values[0].astype(F32)
    for value in values[1:]:
        total = total + value.astype(F32)
    return total


def plane_start(geo, keep, came):
    shape = (2, 2, 2, geo.rows, LANES)
    half = ceil_to(geo.rows // 2, 16)
    keep, came = keep.reshape(shape), came.reshape(shape)
    one = (keep[:, :, :, :half], came[:, :, :, :half])
    two = (keep[:, :, :, half:], came[:, :, :, half:])
    to_x = add(*(part[1] for part in one)).astype(BF16)
    to_y = add(*(part[:, 1] for part in two)).astype(BF16)
    return [part[0] for part in one], [part[:, 0] for part in two], to_x, to_y


def plane_next(one, two, from_x, from_y):
    one, two = one + [from_x], two + [from_y]
    to_y = add(*(part[1] for part in one)).astype(BF16)
    to_x = add(*(part[1] for part in two)).astype(BF16)
    return [part[0] for part in one], [part[0] for part in two], to_y, to_x


def plane_end(one, two, from_y, from_x):
    return jnp.concatenate([add(*one, from_y), add(*two, from_x)], 1)


def column_sum(geo, place, upper, lower, table):
    n = geo.devices
    if table:
        row = lax.broadcasted_iota(jnp.int32, (1, geo.rows, 1), 1)
        upper = jnp.where(row < geo.param_rows, upper, lower)
    is_upper = place[3] >= 2
    near = jnp.where(is_upper, upper, lower)
    far = jnp.where(is_upper, lower, upper).astype(BF16)
    return [near[0], permute(near[1].astype(BF16), Z1, n), permute(far[0], Z2, n), permute(far[1], Z3, n)]


def sum_any(chunks):
    return lax.psum_scatter(chunks.astype(F32), AXES, scatter_dimension=0, tiled=True)[0]


def timestep_embed(step_ids):
    half_dim = TD // 2
    freq_base = jnp.exp(jnp.arange(half_dim, dtype=F32) * (-math.log(10000.0) / half_dim))
    angle_grid = step_ids.astype(F32)[:, None] * freq_base[None, :]
    return jnp.concatenate([jnp.sin(angle_grid), jnp.cos(angle_grid)], axis=1)


def body(fast, chars, steps, embed, layer_params, cotangent):
    seqs, length = chars.shape
    tokens = seqs * length
    geo = Geometry(lax.axis_size(AXES), layer_params.shape[1], embed.shape[0])
    index = lax.axis_index(AXES).astype(jnp.int32)
    place = jnp.stack(
        [index, index * geo.shard % LANES, index * geo.embed_shard % LANES, index // 8]
    ).astype(jnp.int32)
    chunks = pack_shards(geo, place, layer_params, embed)
    emb = timestep_embed(steps).astype(BF16)
    emb_rows = jnp.concatenate([emb, jnp.zeros((8 - seqs, TD), BF16)], 0) if seqs < 8 else emb
    emb_t = emb.astype(F32).T
    chars_row, chars_col = chars.reshape(1, tokens), chars.reshape(tokens, 1)
    n = geo.devices

    def up(layer, gathered):
        return unpack(geo, layer, place, gathered)

    def ahead(layer, first_inputs, got):
        w_time, w_qkv, w_out, _, _, vectors = got[:6]
        return ahead_attn(layer, seqs, tokens, first_inputs, emb_rows, (w_time, w_qkv, w_out, vectors))

    def ahead_rest(layer, saved, got):
        x2, a2 = saved[5:]
        stream, gl, slope = ahead_mlp(x2, a2, got[3], got[4], got[5], F32 if layer == 0 else BF16)
        return stream, list(saved[:6]) + [a2, gl, slope]

    def mlp(layer, grad, saved, got):
        kept, weights = saved[5:], (got[3], got[4], got[5])
        return back_mlp(geo, layer, fast, place, grad, kept, weights)

    def attn(layer, grad, saved, got, rest):
        weights = (got[1], got[2], got[5])
        return back_attn(geo, layer, fast, seqs, place, grad, saved[:5], weights, emb_t, rest, chars_row)

    grad = cotangent.reshape(tokens, D)
    if not fast:
        first = up(0, gather_any(geo, chunks[0]))
        stream, saved_first = ahead_rest(0, ahead(0, [chars_col, first[6]], first), first)
        second = up(1, gather_any(geo, chunks[1]))
        stream, saved_second = ahead_rest(1, ahead(1, [stream], second), second)
        grad, rest, upper_second = mlp(1, grad, saved_second, second)
        grad, lower_second = attn(1, grad, saved_second, second, rest)
        grad, rest, upper_first = mlp(0, grad, saved_first, first)
        lower_first, tables = attn(0, grad, saved_first, first, rest)
        firsts = sum_any(jnp.concatenate([lower_first, upper_first], 0))
        seconds = sum_any(jnp.concatenate([lower_second, upper_second], 0))
        grad_params, grad_embed = finish(geo, fast, place, [firsts, seconds, sum_any(tables)])
        return (stream.reshape(seqs, length, D), grad_embed, grad_params)

    gathered, column = gather_both(geo, *chunks)
    sides = gather_sides(geo, column)
    column_other = permute(column, CORE, n)
    first = up(0, gathered)
    saved_first = ahead(0, [chars_col, first[6]], first)
    saved_first, sides, column_other = sync(saved_first, sides, column_other)
    corners = gather_corners(geo, *sides)
    sides_other = [permute(side, CORE, n) for side in sides]
    stream, saved_first = ahead_rest(0, saved_first, first)
    stream, corners, sides_other = sync(stream, corners, sides_other)
    corners_other = [permute(corner, CORE, n) for corner in corners]
    second = up(1, gathered_pieces(geo, [column, *sides, *corners], [column_other, *sides_other, *corners_other]))
    stream, saved_second = ahead_rest(1, ahead(1, [stream], second), second)
    output = stream.reshape(seqs, length, D)

    def cross(to_one, to_two, one, two):
        return permute(to_one, one, n), permute(to_two, two, n)

    grad, rest, keep_u, send_u = mlp(1, grad, saved_second, second)
    came_u = permute(send_u, CORE, n)
    grad, keep_l, send_l = attn(1, grad, saved_second, second, rest)
    grad, keep_u, came_u, keep_l, send_l = sync(grad, keep_u, came_u, keep_l, send_l)
    came_l = permute(send_l, CORE, n)
    one_u, two_u, to_x, to_y = plane_start(geo, keep_u, came_u)
    from_u = cross(to_x, to_y, X, Y)

    grad, rest, keep, send = mlp(0, after(grad, to_x, to_y), saved_first, first)
    grad, rest, keep, send, came_l, from_u = sync(grad, rest, keep, send, came_l, from_u)
    came = permute(send, CORE, n)
    one_u, two_u, to_y, to_x = plane_next(one_u, two_u, *from_u)
    from_u = cross(to_y, to_x, Y, X)
    one_l, two_l, to_x_l, to_y_l = plane_start(geo, keep_l, came_l)
    from_l = cross(to_x_l, to_y_l, X, Y)

    grad = after(grad, to_x, to_y, to_x_l, to_y_l)
    low_keep, low_send = attn(0, grad, saved_first, first, rest)
    low_keep, low_send, keep, came, from_u, from_l = sync(low_keep, low_send, keep, came, from_u, from_l)
    low_came = permute(low_send, CORE, n)
    one_l, two_l, to_y, to_x = plane_next(one_l, two_l, *from_l)
    from_l = cross(to_y, to_x, Y, X)
    one, two, to_x, to_y = plane_start(geo, keep, came)
    from_up = cross(to_x, to_y, X, Y)
    upper = plane_end(one_u, two_u, *from_u)

    low_came, low_keep, upper, _, _ = sync(low_came, low_keep, upper, to_x, to_y)
    low_one, low_two, to_x, to_y = plane_start(geo, low_keep, low_came)
    from_low = cross(to_x, to_y, X, Y)

    from_l, from_up, _, _ = sync(from_l, from_up, to_x, to_y)
    lower = plane_end(one_l, two_l, *from_l)
    seconds = column_sum(geo, place, upper, lower, False)
    one, two, to_y, to_x = plane_next(one, two, *from_up)
    from_up = cross(to_y, to_x, Y, X)

    from_low, _, _ = sync(from_low, to_y, to_x)
    low_one, low_two, to_y, to_x = plane_next(low_one, low_two, *from_low)
    from_low = cross(to_y, to_x, Y, X)

    from_low, from_up = sync(from_low, from_up)
    upper, lower = plane_end(one, two, *from_up), plane_end(low_one, low_two, *from_low)
    firsts = column_sum(geo, place, upper, lower, True)
    grad_params, grad_embed = finish(geo, fast, place, firsts + seconds)
    return (output, grad_embed, grad_params)


def solution(mesh):
    both = P(AXES)
    fast = dict(mesh.shape) == {"dp": 8, "fsdp": 4}
    return jax.shard_map(
        functools.partial(body, fast),
        mesh=mesh,
        in_specs=(P(AXES, None), both, both, P(None, AXES), P(AXES, None, None)),
        out_specs=(P(AXES, None, None), both, P(None, AXES)),
        check_vma=False,
    )
```

```python
import functools
import math

import jax
import jax.numpy as jnp
from jax import lax
from jax.experimental import pallas as pl
from jax.experimental.pallas import tpu as pltpu
from jax.sharding import PartitionSpec as P

D = 512
HEADS = 8
FF = 2048
VOCAB = 27
TD = 128
HD = 64
LANES = 128
EPSILON = 1e-05
AXES = ("dp", "fsdp")
F32 = jnp.float32
BF16 = jnp.bfloat16
VMEM_BYTES = 52 * 2**20

ROW_GAIN_ONE, ROW_BIAS_ONE, ROW_W_TIME, ROW_B_TIME = 0, 4, 8, 520
ROW_QKV, ROW_OUT, ROW_GAIN_TWO, ROW_BIAS_TWO = 524, 6668, 8716, 8720
ROW_UP, ROW_B_UP, ROW_DOWN, ROW_B_DOWN, ROW_END = 8724, 16916, 16932, 25124, 25128
CHUNK_PAD = 832


def ceil_to(value, step):
    return -(-value // step) * step


class Geometry:
    def __init__(self, devices, shard, embed_shard):
        self.devices, self.shard, self.embed_shard = devices, shard, embed_shard
        self.param_rows = max(self.count(d, shard) for d in range(devices))
        self.embed_rows = max(self.count(d, embed_shard) for d in range(devices))
        self.embed_at = ceil_to(self.param_rows, 8)
        self.rows = ceil_to(max(self.embed_at + 8, self.param_rows + 2 * self.embed_rows), 16)

    @staticmethod
    def first(d, size):
        return d * size // LANES

    @staticmethod
    def count(d, size):
        return -(-(d + 1) * size // LANES) - d * size // LANES


def params(flops, nbytes, weight=0):
    flops, nbytes = max(flops * weight, 1000), max(nbytes * weight, 1000)
    return dict(
        compiler_params=pltpu.CompilerParams(vmem_limit_bytes=VMEM_BYTES),
        cost_estimate=pl.CostEstimate(flops=flops, bytes_accessed=nbytes, transcendentals=0),
    )


VM = pl.BlockSpec(memory_space=pltpu.VMEM)
SM = pl.BlockSpec(memory_space=pltpu.SMEM)
HBM = pl.BlockSpec(memory_space=pltpu.HBM)


def nn(left, right):
    return lax.dot_general(left, right, (((1,), (0,)), ((), ())), preferred_element_type=F32)


def nt(left, right):
    return lax.dot_general(left, right, (((1,), (1,)), ((), ())), preferred_element_type=F32)


def tn(left, right):
    return nn(left.T, right)


def shift_in(flat, offset):
    rolled = pltpu.roll(flat, offset, 1)
    above = jnp.concatenate([jnp.zeros((1, LANES), F32), rolled[:-1]], 0)
    lane = lax.broadcasted_iota(jnp.int32, flat.shape, 1)
    return jnp.where(lane >= offset, rolled, above)


def shift_out(flat, offset):
    rolled = pltpu.roll(flat, lax.rem(LANES - offset, LANES), 1)
    below = jnp.concatenate([rolled[1:], jnp.zeros((1, LANES), F32)], 0)
    lane = lax.broadcasted_iota(jnp.int32, flat.shape, 1)
    return jnp.where(lane < LANES - offset, rolled, below)


def pack_kernel(geo, place_ref, layers_ref, embed_ref, first_ref, second_ref):
    main = geo.embed_at
    for layer, out_ref in ((0, first_ref), (1, second_ref)):
        moved = shift_in(layers_ref[layer].astype(F32), place_ref[1])
        if layer == 0:
            tail = shift_in(embed_ref[...].astype(F32), place_ref[2])
            parts = [moved[:main], tail] + ([moved[main + 8 :]] if geo.rows > main + 8 else [])
            moved = jnp.concatenate(parts, 0)
        out_ref[...] = moved.astype(BF16)


def pack_shards(geo, place, layer_params, embed):
    layers = jnp.pad(layer_params, ((0, 0), (0, geo.rows * LANES - geo.shard)))
    table = jnp.pad(embed, (0, 8 * LANES - geo.embed_shard))
    out = jax.ShapeDtypeStruct((geo.rows, LANES), BF16)
    return pl.pallas_call(
        functools.partial(pack_kernel, geo),
        out_shape=(out, out),
        in_specs=[SM, VM, VM],
        out_specs=(VM, VM),
        **params(10**6, geo.rows * 1024),
    )(place, layers.reshape(2, geo.rows, LANES), table.reshape(8, LANES))


def finish_kernel(geo, fast, place_ref, *refs):
    grads_ref, embed_ref, moved = refs[-3:]
    parts = refs[:-3]
    count = 4 if fast else 1
    for layer in range(2):
        total = parts[layer * count][...].astype(F32)
        for part in parts[layer * count + 1 : (layer + 1) * count]:
            total = total + part[...].astype(F32)
        moved[pl.ds(layer * geo.rows, geo.rows), :] = shift_out(total, place_ref[1])
        if fast and layer == 0:
            first, size = geo.param_rows, geo.embed_rows
            lower, upper = total[first : first + size], total[first + size : first + 2 * size]
            tail = jnp.where(place_ref[3] >= 2, upper, lower)
            tail = jnp.concatenate([tail, jnp.zeros((8 - size, LANES), F32)], 0)
    if not fast:
        tail = parts[2][...]
    embed_ref[...] = shift_out(tail, place_ref[2])
    for r in range(ceil_to(geo.shard, LANES) // LANES):
        size = min(LANES, geo.shard - r * LANES)
        grads_ref[:, r * LANES : r * LANES + size] = moved[pl.ds(r, 2, stride=geo.rows), :][:, :size]


def finish(geo, fast, place, operands):
    grads, table = pl.pallas_call(
        functools.partial(finish_kernel, geo, fast),
        out_shape=(
            jax.ShapeDtypeStruct((2, geo.shard), F32),
            jax.ShapeDtypeStruct((8, LANES), F32),
        ),
        in_specs=[SM] + [VM] * len(operands),
        out_specs=(VM, VM),
        scratch_shapes=[pltpu.VMEM((2 * geo.rows, LANES), F32)],
        **params(10**6, geo.rows * 4096),
    )(place, *operands)
    return grads, table.reshape(-1)[: geo.embed_shard]


class Staged:
    def __init__(self, sources, targets, held, sems):
        self.held, self.pending, self.sent = held, {}, []
        self.targets, self.sems = targets, sems
        self.used = len(sources)
        for i, name in enumerate(sources):
            self.pending[name] = pltpu.make_async_copy(sources[name], held[name], sems.at[i])
            self.pending[name].start()

    def get(self, *names):
        for name in names:
            if name in self.pending:
                self.pending.pop(name).wait()
        found = [self.held[name] for name in names]
        return found[0] if len(found) == 1 else found

    def put(self, *names):
        for name in names:
            copy = pltpu.make_async_copy(self.held[name], self.targets[name], self.sems.at[self.used])
            copy.start()
            self.used += 1
            self.sent.append(copy)

    def close(self):
        for copy in list(self.pending.values()) + self.sent:
            copy.wait()


def staged_call(kernel, place, operands, results, scratch, flops, raw=(), semaphores=0, unheld=()):
    names, outs, temps = list(operands), list(results), list(scratch)

    held_outs = [name for name in outs if name not in unheld]

    def whole(place_ref, *refs):
        raws, refs = refs[: len(raw)], refs[len(raw) :]
        sources, refs = dict(zip(names, refs)), refs[len(names) :]
        targets, refs = dict(zip(outs, refs)), refs[len(outs) :]
        held, refs = dict(zip(names + held_outs, refs)), refs[len(names) + len(held_outs) :]
        extra, refs = dict(zip(temps, refs)), refs[len(temps) :]
        staged = Staged(sources, targets, held, refs[0])
        kernel(place_ref, raws, staged, extra, refs[-1])
        staged.close()

    buffers = [pltpu.VMEM(v.shape, v.dtype) for v in (*operands.values(), *(results[name] for name in held_outs))]
    sems = [pltpu.SemaphoreType.DMA((len(names) + len(outs),))]
    if semaphores:
        sems.append(pltpu.SemaphoreType.DMA((semaphores,)))
    found = pl.pallas_call(
        whole,
        out_shape=tuple(results.values()),
        in_specs=[SM] + [HBM] * (len(raw) + len(names)),
        out_specs=(HBM,) * len(outs),
        scratch_shapes=buffers + list(scratch.values()) + sems,
        **params(flops, 2 * 10**7, 1),
    )(place, *raw, *operands.values())
    return dict(zip(outs, found))


def like(dtype, *shape):
    return jax.ShapeDtypeStruct(shape, dtype)


def unpack(geo, layer, plan, me, chunk_refs, held, flat, flat_table, out, sems):
    copies = []
    for source, pieces in zip(chunk_refs, plan):
        for src_at, relative, absolute, dst_at, count in pieces:
            if absolute is None:
                target = held.at[lax.bitwise_xor(me, relative), pl.ds(dst_at, count)]
                origin = source.at[pl.ds(src_at, count)]
            else:
                target, origin = held, source
            copies.append(pltpu.make_async_copy(origin, target, sems.at[len(copies)]))
    for copy in copies:
        copy.start()
    for copy in copies:
        copy.wait()
    for d in range(geo.devices):
        block = held[d].astype(F32)
        start, rows = geo.first(d, geo.shard), geo.count(d, geo.shard)
        split = (d * geo.shard) % LANES != 0
        if split:
            shared = flat[pl.ds(start, 1), :] + block[:1]
        flat[pl.ds(start, rows), :] = block[:rows]
        if split:
            flat[pl.ds(start, 1), :] = shared
        if layer == 0:
            tail = block[geo.embed_at : geo.embed_at + 8]
            start, rows = geo.first(d, geo.embed_shard), geo.count(d, geo.embed_shard)
            split = (d * geo.embed_shard) % LANES != 0
            if split:
                shared = flat_table[pl.ds(start, 1), :] + tail[:1]
            flat_table[pl.ds(start, rows), :] = tail[:rows]
            if split:
                flat_table[pl.ds(start, 1), :] = shared
    vectors = out["vectors"]
    for row, start, width in (
        (0, ROW_GAIN_ONE, 4),
        (1, ROW_BIAS_ONE, 4),
        (2, ROW_B_TIME, 4),
        (3, ROW_GAIN_TWO, 4),
        (4, ROW_BIAS_TWO, 4),
        (5, ROW_B_DOWN, 4),
        (6, ROW_B_UP, 16),
    ):
        for c in range(width):
            vectors[row : row + 1, c * LANES : (c + 1) * LANES] = flat[pl.ds(start + c, 1), :]
    for name, start, rows, width in (
        ("w_time", ROW_W_TIME, TD, 4),
        ("w_qkv", ROW_QKV, D, 12),
        ("w_out", ROW_OUT, D, 4),
        ("w_up", ROW_UP, D, 16),
        ("w_down", ROW_DOWN, FF, 4),
    ):
        for c in range(width):
            out[name][:, c * LANES : (c + 1) * LANES] = flat[pl.ds(start + c, rows, stride=width), :].astype(BF16)
    if layer == 0:
        table = out["table"]
        table[...] = jnp.zeros(table.shape, BF16)
        for c in range(4):
            table[0:VOCAB, c * LANES : (c + 1) * LANES] = flat_table[pl.ds(c, VOCAB, stride=4), :].astype(BF16)


WEIGHTS = {
    "w_qkv": like(BF16, D, 3 * D),
    "w_out": like(BF16, D, D),
    "w_up": like(BF16, D, FF),
    "w_down": like(BF16, FF, D),
    "vectors": like(F32, 8, FF),
}


def unpack_scratch(geo, layer):
    scratch = {
        "chunks": pltpu.VMEM((geo.devices, geo.rows, LANES), BF16),
        "flat": pltpu.VMEM((ROW_END + CHUNK_PAD, LANES), F32),
        "flat_table": pltpu.VMEM((4 * 32, LANES), F32),
        "w_time": pltpu.VMEM((TD, D), BF16),
    }
    if layer == 0:
        scratch["table"] = pltpu.VMEM((32, D), BF16)
    return scratch


def split_gathered(gathered):
    plan = tuple(tuple(pieces) for array, pieces in gathered)
    return [array for array, pieces in gathered], plan, sum(len(pieces) for pieces in plan)


def norm_stats(values):
    mean = jnp.mean(values, -1, keepdims=True)
    centered = values - mean
    variance = jnp.mean(centered * centered, -1, keepdims=True)
    scale = lax.rsqrt(variance + EPSILON)
    return centered * scale, scale


ROW_BLOCK = 64


def norm_ahead(values, gain, bias, out):
    for r in range(0, values.shape[0], ROW_BLOCK):
        rows = slice(r, r + ROW_BLOCK)
        unit, _ = norm_stats(values[rows, :])
        out[rows, :] = (unit * gain + bias).astype(BF16)


def norm_back(grad, values, gain, passed, out):
    grad_gain, grad_bias = jnp.zeros((8, D), F32), jnp.zeros((8, D), F32)
    for r in range(0, values.shape[0], ROW_BLOCK):
        rows = slice(r, r + ROW_BLOCK)
        unit, scale = norm_stats(values[rows, :])
        block = grad[rows, :]
        grad_gain = grad_gain + jnp.sum((block * unit).reshape(-1, 8, D), 0)
        grad_bias = grad_bias + jnp.sum(block.reshape(-1, 8, D), 0)
        inner = block * gain
        shifted = inner - jnp.mean(inner, -1, keepdims=True)
        back = scale * (shifted - unit * jnp.mean(inner * unit, -1, keepdims=True))
        out[rows, :] = passed[rows, :].astype(F32) + back
    return jnp.sum(grad_gain, 0, keepdims=True), jnp.sum(grad_bias, 0, keepdims=True)


def gelu_both(u):
    root = math.sqrt(2.0 / math.pi)
    square = u * u
    t = jnp.tanh(root * (u + 0.044715 * (square * u)))
    half = 0.5 * (1.0 + t)
    slope = half + 0.5 * u * (1.0 - t * t) * (root * (1.0 + 3.0 * 0.044715 * square))
    return u * half, slope


def head_masks(shape, scale):
    lane = lax.broadcasted_iota(jnp.int32, shape, 1)
    one = jnp.where(lane < HD, scale, 0.0).astype(BF16)
    two = jnp.where(lane < HD, 0.0, scale).astype(BF16)
    return one, two


def ahead_attn(seqs, stream, emb, w_time, w_qkv, w_out, vectors, x, a, qkv, prob, o, x2, a2, done):
    tokens = x.shape[0]
    length = tokens // seqs
    time_vec = nn(emb[...], w_time[...]) + vectors[2:3, :D]
    for s in range(seqs):
        x[s * length : (s + 1) * length, :] = stream[s * length : (s + 1) * length] + time_vec[s : s + 1]
    done("x")
    norm_ahead(x, vectors[0:1, :D], vectors[1:2, :D], a)
    done("a")
    for c in range(3):
        part = slice(c * D, (c + 1) * D)
        qkv[:, part] = nn(a[...], w_qkv[:, part]).astype(BF16)
    done("qkv")
    masks = head_masks((length, LANES), 1.0 / math.sqrt(HD))
    for s in range(seqs):
        rows = slice(s * length, (s + 1) * length)
        for pair in range(HEADS // 2):
            cols = [slice(c * D + pair * LANES, c * D + (pair + 1) * LANES) for c in range(3)]
            q, k, v_t = qkv[rows, cols[0]], qkv[rows, cols[1]], qkv[rows, cols[2]].T
            mixed = []
            for h in range(2):
                scores = nt(k * masks[h], q)
                top = jnp.max(scores, 0, keepdims=True)
                expd = jnp.exp(scores - top)
                low = (expd * (1.0 / jnp.sum(expd, 0, keepdims=True))).astype(BF16)
                prob[s * HEADS + 2 * pair + h] = low
                mixed.append(nn(v_t[h * HD : (h + 1) * HD], low))
            o[rows, cols[0]] = jnp.concatenate(mixed, 0).T.astype(BF16)
    done("prob")
    done("o")
    x2[...] = x[...] + nn(o[...], w_out[...])
    done("x2")
    norm_ahead(x2, vectors[3:4, :D], vectors[4:5, :D], a2)
    done("a2")


def ahead_mlp(x2, a2, w_up, w_down, vectors, gl, slope):
    parts = [slice(c * D, (c + 1) * D) for c in range(FF // D)]

    def up(part):
        return nn(a2()[...], w_up()[:, part])

    total, u = None, up(parts[0])
    for c, part in enumerate(parts):
        value, rate = gelu_both(u + vectors()[6:7, part])
        low = value.astype(BF16)
        gl[:, part] = low
        slope[:, part] = rate.astype(BF16)
        if c + 1 < len(parts):
            u = up(parts[c + 1])
        step = nn(low, w_down()[part, :])
        total = step if total is None else total + step
    return x2()[...] + vectors()[5:6, :D] + total


class Chunks:
    def __init__(self, geo, fast, me, held, targets, sems):
        self.geo, self.fast, self.me, self.held, self.targets, self.sems = geo, fast, me, held, targets, sems
        self.copies = []

    def cut(self, d, flat, base, table=None):
        geo, slot = self.geo, d % (self.geo.devices // 2)
        block = flat[pl.ds(geo.first(d, geo.shard) - base, geo.rows), :]
        if table is not None:
            first, size = geo.param_rows, geo.embed_rows
            tails = [
                table[pl.ds(geo.first(e, geo.embed_shard), size), :] for e in (d, d + geo.devices // 2)
            ]
            block = jnp.concatenate([block[:first], *tails, block[first + 2 * size :]], 0)
        self.held[slot] = block.astype(BF16)
        source, sem = self.held.at[slot], self.sems.at[slot]
        if not self.fast:
            self.copies.append(pltpu.make_async_copy(source, self.targets[0].at[slot], sem))
            self.copies[-1].start()
            return
        relative = lax.bitwise_xor(self.me, d)
        row = lax.bitwise_and(relative, 4) + lax.bitwise_and(relative, 2)
        row = row + lax.bitwise_and(lax.shift_right_logical(relative, 3), 1)
        keep, send = (pltpu.make_async_copy(source, target.at[row], sem) for target in self.targets)
        core = lax.bitwise_and(relative, 1)

        @pl.when(core == 0)
        def _():
            keep.start()

        @pl.when(core == 1)
        def _():
            send.start()

        self.copies.append(keep)

    def close(self):
        for copy in self.copies:
            copy.wait()


def back_mlp(geo, chunks, grad_in, x2, a2, gl, slope, w_up, w_down, vectors, grad, rest, flat, base, normed, done):
    grad_low = grad_in()[...].astype(BF16)
    flat[pl.ds(ROW_END - base, CHUNK_PAD), :] = jnp.zeros((CHUNK_PAD, LANES), F32)
    grad_bias = jnp.sum(grad_low.astype(F32), 0, keepdims=True)
    for c in range(4):
        flat[pl.ds(ROW_B_DOWN - base + c, 1), :] = grad_bias[:, c * LANES : (c + 1) * LANES]
    parts = [slice(j * D, (j + 1) * D) for j in range(FF // D)]

    def hidden_grad(part):
        return nt(grad_low, w_down()[part, :])

    total, hidden = None, hidden_grad(parts[0])
    for j, part in enumerate(parts):
        up_grad = (hidden * slope()[:, part].astype(F32)).astype(BF16)
        bias_grad = jnp.sum(up_grad.astype(F32), 0, keepdims=True)
        if j + 1 < len(parts):
            hidden = hidden_grad(parts[j + 1])
        down = tn(gl()[:, part], grad_low)
        for c in range(4):
            cols = slice(c * LANES, (c + 1) * LANES)
            flat[pl.ds(ROW_B_UP - base + 4 * j + c, 1), :] = bias_grad[:, cols]
            flat[pl.ds(ROW_DOWN - base + 4 * D * j + c, D, stride=4), :] = down[:, cols]
        up = tn(a2()[...], up_grad)
        for c in range(4):
            cols = slice(c * LANES, (c + 1) * LANES)
            flat[pl.ds(ROW_UP - base + 4 * j + c, D, stride=16), :] = up[:, cols]
        step = nt(up_grad, w_up()[:, part])
        total = step if total is None else total + step
    normed[...] = total
    for d in range(geo.devices // 2, geo.devices):
        chunks.cut(d, flat, base)
    grad_gain, grad_bias = norm_back(normed, x2(), vectors()[3:4, :D], grad_in(), grad)
    done("grad")
    for c in range(4):
        cols = slice(c * LANES, (c + 1) * LANES)
        flat[pl.ds(ROW_GAIN_TWO - base + c, 1), :] = grad_gain[:, cols]
        flat[pl.ds(ROW_BIAS_TWO - base + c, 1), :] = grad_bias[:, cols]
    rest[...] = flat[pl.ds(ROW_GAIN_TWO - base, rest.shape[0]), :].astype(BF16)
    done("rest")


def back_attn(
    geo, seqs, chunks, table, embed_outs, grad_in, x, a, qkv, prob, o, w_qkv, w_out, vectors, emb_t, rest, total,
    flat, qkv_grad, heads_grad, normed, chars, done,
):
    tokens = normed.shape[0]
    length = tokens // seqs
    grad_low = grad_in()[...].astype(BF16)
    heads_grad[...] = nt(grad_low, w_out()[...]).astype(BF16)
    out_grad = tn(o()[...], grad_low)
    for c in range(4):
        flat[pl.ds(ROW_OUT + c, D, stride=4), :] = out_grad[:, c * LANES : (c + 1) * LANES]
    masks = head_masks((length, LANES), 1.0)
    scale = 1.0 / math.sqrt(HD)
    lane = lax.broadcasted_iota(jnp.int32, (length, LANES), 1)
    qkv, prob = qkv(), prob()
    for s in range(seqs):
        rows = slice(s * length, (s + 1) * length)
        for pair in range(HEADS // 2):
            cols = [slice(c * D + pair * LANES, c * D + (pair + 1) * LANES) for c in range(3)]
            q, k, v = qkv[rows, cols[0]], qkv[rows, cols[1]], qkv[rows, cols[2]]
            go = heads_grad[rows, cols[0]]
            k_t = k.T
            to_q, to_k, to_v = [], [], []
            for h in range(2):
                prob_low = prob[s * HEADS + 2 * pair + h]
                prob_full = prob_low.astype(F32)
                prob_grad = nt(v * masks[h], go)
                weighted = prob_full * prob_grad
                row_dot = jnp.sum(weighted, 0, keepdims=True)
                score_grad = (weighted - prob_full * row_dot).astype(BF16)
                to_q.append(nn(k_t[h * HD : (h + 1) * HD], score_grad))
                to_k.append(nn(score_grad, q))
                to_v.append(nn(prob_low, go))
            qkv_grad[rows, cols[0]] = (jnp.concatenate(to_q, 0).T * scale).astype(BF16)
            qkv_grad[rows, cols[1]] = (jnp.where(lane < HD, to_k[0], to_k[1]) * scale).astype(BF16)
            qkv_grad[rows, cols[2]] = jnp.where(lane < HD, to_v[0], to_v[1]).astype(BF16)
    a_t, steps = a()[...].T, None
    for part in range(3):
        cols = slice(part * D, (part + 1) * D)
        piece = nn(a_t, qkv_grad[:, cols])
        for c in range(4):
            flat[pl.ds(ROW_QKV + 4 * part + c, D, stride=12), :] = piece[:, c * LANES : (c + 1) * LANES]
        step = nt(qkv_grad[:, cols], w_qkv()[:, cols])
        steps = step if steps is None else steps + step
    normed[...] = steps
    flat[pl.ds(ROW_GAIN_TWO, rest().shape[0]), :] = rest()[...].astype(F32)
    middle = geo.devices // 2
    early = [d for d in range(middle) if geo.first(d, geo.shard) >= ROW_QKV] if table is None else []
    for d in early:
        chunks.cut(d, flat, 0)
    grad_gain, grad_bias = norm_back(normed, x(), vectors()[0:1, :D], grad_in(), total)
    done("grad")
    time_grad = [
        jnp.sum(total[s * length : (s + 1) * length, :], 0, keepdims=True).astype(BF16).astype(F32) for s in range(seqs)
    ]
    bias_grad = sum(time_grad[1:], time_grad[0])
    weight_grad = sum(emb_t()[:, s : s + 1] * time_grad[s] for s in range(seqs))
    for c in range(4):
        cols = slice(c * LANES, (c + 1) * LANES)
        flat[pl.ds(ROW_GAIN_ONE + c, 1), :] = grad_gain[:, cols]
        flat[pl.ds(ROW_BIAS_ONE + c, 1), :] = grad_bias[:, cols]
        flat[pl.ds(ROW_B_TIME + c, 1), :] = bias_grad[:, cols]
        flat[pl.ds(ROW_W_TIME + c, TD, stride=4), :] = weight_grad[:, cols]
    if table is not None:
        kind = lax.broadcasted_iota(jnp.int32, (32, tokens), 0)
        table_grad = nn((chars()[...] == kind).astype(BF16), total[...].astype(BF16))
        for c in range(4):
            table[pl.ds(c, 32, stride=4), :] = table_grad[:, c * LANES : (c + 1) * LANES]
    for d in range(middle):
        if d not in early:
            chunks.cut(d, flat, 0, table if chunks.fast else None)
    if table is not None and not chunks.fast:
        for d in range(geo.devices):
            embed_outs[d] = table[pl.ds(geo.first(d, geo.embed_shard), 8), :]


def kept_shapes(seqs, tokens):
    length = tokens // seqs
    return {
        "x": like(F32, tokens, D),
        "a": like(BF16, tokens, D),
        "qkv": like(BF16, tokens, 3 * D),
        "prob": like(BF16, seqs * HEADS, length, length),
        "o": like(BF16, tokens, D),
    }


def rest_rows(geo):
    middle = geo.first(geo.devices // 2, geo.shard)
    return ceil_to(middle + geo.rows - ROW_GAIN_TWO, 16)


def chunk_results(geo, fast):
    if fast:
        shape = like(BF16, geo.devices // 4, geo.rows, LANES)
        return {"keep": shape, "send": shape}
    return {"keep": like(BF16, geo.devices // 2, geo.rows, LANES)}


def chunk_targets(staged, fast):
    return [staged.targets[name] for name in (("keep", "send") if fast else ("keep",))]


def chunk_scratch(geo, tokens):
    return {
        "cuts": pltpu.VMEM((geo.devices // 2, geo.rows, LANES), BF16),
        "cut_sems": pltpu.SemaphoreType.DMA((geo.devices // 2,)),
        "normed": pltpu.VMEM((tokens, D), F32),
    }


def first_ahead(geo, seqs, place, gathered, chars, emb):
    tokens = chars.shape[0]
    arrays, plan, count = split_gathered(gathered)
    results = WEIGHTS | kept_shapes(seqs, tokens) | {"x2": like(F32, tokens, D), "a2": like(BF16, tokens, D)}

    def kernel(place_ref, chunk_refs, staged, extra, sems):
        held = staged.held
        unpack(
            geo, 0, plan, place_ref[0], chunk_refs, extra["chunks"], extra["flat"], extra["flat_table"], held | extra, sems
        )
        staged.put(*WEIGHTS)
        lane = lax.broadcasted_iota(jnp.int32, (tokens, 32), 1)
        stream = nn((staged.get("chars")[...] == lane).astype(BF16), extra["table"][...])
        weights = [extra["w_time"]] + [held[name] for name in ("w_qkv", "w_out", "vectors")]
        outs = [held[name] for name in ("x", "a", "qkv", "prob", "o", "x2", "a2")]
        ahead_attn(seqs, stream, staged.get("emb"), *weights, *outs, staged.put)

    operands = {"chars": chars, "emb": emb}
    scratch = unpack_scratch(geo, 0)
    return staged_call(kernel, place, operands, results, scratch, 4 * 10**9, arrays, count)


def first_ahead_rest(place, found):
    names = ("a2", "w_up", "vectors", "w_down", "x2")
    operands = {name: found[name] for name in names}
    tokens = found["x2"].shape[0]
    results = {"stream": like(F32, tokens, D), "gl": like(BF16, tokens, FF), "slope": like(BF16, tokens, FF)}

    def kernel(place_ref, _, staged, extra, sems):
        late = [functools.partial(staged.get, name) for name in ("x2", "a2", "w_up", "w_down", "vectors")]
        gl, slope, stream = (staged.held[name] for name in ("gl", "slope", "stream"))
        stream[...] = ahead_mlp(*late, gl, slope)
        staged.put("gl", "slope", "stream")

    return found | staged_call(kernel, place, operands, results, {}, 4 * 10**9)


def second_both(geo, fast, seqs, place, gathered, stream, emb, cotangent):
    tokens = stream.shape[0]
    arrays, plan, count = split_gathered(gathered)
    results = {name: WEIGHTS[name] for name in ("w_qkv", "w_out", "vectors")}
    results = results | kept_shapes(seqs, tokens)
    results = results | {
        "output": like(BF16, tokens, D),
        "grad": like(F32, tokens, D),
        "rest": like(BF16, rest_rows(geo), LANES),
    }
    results = results | chunk_results(geo, fast)
    scratch = unpack_scratch(geo, 1)
    scratch["w_up"], scratch["w_down"] = pltpu.VMEM((D, FF), BF16), pltpu.VMEM((FF, D), BF16)
    scratch["x2"], scratch["a2"] = pltpu.VMEM((tokens, D), F32), pltpu.VMEM((tokens, D), BF16)
    scratch["gl"], scratch["slope"] = pltpu.VMEM((tokens, FF), BF16), pltpu.VMEM((tokens, FF), BF16)
    scratch = scratch | chunk_scratch(geo, tokens)

    def kernel(place_ref, chunk_arrays, staged, extra, sems):
        every = staged.held | extra
        unpack(geo, 1, plan, place_ref[0], chunk_arrays, extra["chunks"], extra["flat"], extra["flat_table"], every, sems)
        staged.put("w_qkv", "w_out", "vectors")
        weights = [every[name] for name in ("w_time", "w_qkv", "w_out", "vectors")]
        outs = [every[name] for name in ("x", "a", "qkv", "prob", "o", "x2", "a2")]

        def done(name):
            if name in results:
                staged.put(name)

        ahead_attn(seqs, staged.get("stream")[...], staged.get("emb"), *weights, *outs, done)

        def ready(*names):
            return [functools.partial(every.get, name) for name in names]

        outputs = ahead_mlp(*ready("x2", "a2", "w_up", "w_down", "vectors"), every["gl"], every["slope"])
        every["output"][...] = outputs.astype(BF16)
        done("output")
        chunks = Chunks(geo, fast, place_ref[0], extra["cuts"], chunk_targets(staged, fast), extra["cut_sems"])
        back_mlp(
            geo, chunks, functools.partial(staged.get, "cotangent"),
            *ready("x2", "a2", "gl", "slope", "w_up", "w_down", "vectors"),
            every["grad"], every["rest"], extra["flat"], 0, extra["normed"], done,
        )
        chunks.close()

    operands = {"stream": stream, "emb": emb, "cotangent": cotangent}
    return staged_call(kernel, place, operands, results, scratch, 10**10, arrays, count, ("keep", "send"))


def first_back_mlp(geo, fast, place, grad, found):
    names = ("grad_in", "w_down", "slope", "gl", "a2", "w_up", "x2", "vectors")
    operands = {name: grad if name == "grad_in" else found[name] for name in names}
    tokens = grad.shape[0]
    results = {"grad": like(F32, tokens, D), "rest": like(BF16, rest_rows(geo), LANES)} | chunk_results(geo, fast)
    base = ROW_GAIN_TWO

    def kernel(place_ref, _, staged, extra, sems):
        late = [
            functools.partial(staged.get, name)
            for name in ("grad_in", "x2", "a2", "gl", "slope", "w_up", "w_down", "vectors")
        ]
        chunks = Chunks(geo, fast, place_ref[0], extra["cuts"], chunk_targets(staged, fast), extra["cut_sems"])
        back_mlp(
            geo, chunks, *late, staged.held["grad"], staged.held["rest"], extra["flat"], base, extra["normed"], staged.put
        )
        chunks.close()

    scratch = {"flat": pltpu.VMEM((ROW_END - base + CHUNK_PAD, LANES), F32)} | chunk_scratch(geo, tokens)
    return staged_call(kernel, place, operands, results, scratch, 6 * 10**9, unheld=("keep", "send"))


def both_back_attn(geo, fast, layer, seqs, place, grad, found, emb_t, rest, chars_row):
    names = ("grad_in", "w_out", "o", "qkv", "prob", "a", "w_qkv", "x", "vectors", "emb_t", "rest")
    given = {"grad_in": grad, "emb_t": emb_t, "rest": rest}
    operands = {name: given[name] if name in given else found[name] for name in names}
    tokens = grad.shape[0]
    results = {} if layer == 0 else {"grad": like(F32, tokens, D)}
    results = results | chunk_results(geo, fast)
    scratch = {
        "flat": pltpu.VMEM((ROW_GAIN_TWO + rest.shape[0], LANES), F32),
        "qkv_grad": pltpu.VMEM((tokens, 3 * D), BF16),
        "heads_grad": pltpu.VMEM((tokens, D), BF16),
    } | chunk_scratch(geo, tokens)
    if layer == 0:
        scratch["total"] = pltpu.VMEM((tokens, D), F32)
        operands["chars"] = chars_row
        scratch["table"] = pltpu.VMEM((4 * 32, LANES), F32)
        if not fast:
            results["table_out"] = like(F32, geo.devices, 8, LANES)

    def kernel(place_ref, _, staged, extra, sems):
        late = [functools.partial(staged.get, name) for name in ("grad_in", "x", "a", "qkv", "prob", "o", "w_qkv", "w_out")]
        tail = [functools.partial(staged.get, name) for name in ("vectors", "emb_t", "rest")]
        chunks = Chunks(geo, fast, place_ref[0], extra["cuts"], chunk_targets(staged, fast), extra["cut_sems"])

        def done(name):
            if name in results:
                staged.put(name)

        back_attn(
            geo, seqs, chunks, extra.get("table"), staged.held.get("table_out"), *late, *tail,
            extra["total"] if layer == 0 else staged.held["grad"], extra["flat"], extra["qkv_grad"], extra["heads_grad"],
            extra["normed"], functools.partial(staged.get, "chars"), done,
        )
        done("table_out")
        chunks.close()

    return staged_call(kernel, place, operands, results, scratch, 6 * 10**9, unheld=("keep", "send"))


def permute(value, distance, devices):
    return lax.ppermute(value, AXES, [(d, d ^ distance) for d in range(devices)])


Z1, Z2, Z3, X, Y, CORE = 8, 16, 24, 4, 2, 1


def after(value, *others):
    return lax.optimization_barrier((value, *others))[0]


def sync(*values):
    return lax.optimization_barrier(values)


def gather_both(geo, first, second):
    n, rows = geo.devices, geo.rows
    half = ceil_to(rows // 2, 16)

    def sides(held):
        return permute(held, X, n), permute(held, Y, n)

    def corners(over_x, over_y):
        return permute(over_x[:half], Y, n), permute(over_y[half:], X, n)

    def other(*arrays):
        return permute(jnp.concatenate(arrays, 0), CORE, n)

    near, over = permute(first, Z1, n), permute(first, Z2, n)
    sides_0 = sides(first)
    sides_0 = sync(*sides_0)
    corners_0 = corners(*sides_0)
    near, _ = sync(near, sides_0[0])
    sides_1 = sides(near)
    over, _ = sync(over, near)
    far = permute(over, Z1, n)
    sides_2 = sides(over)
    *sides_1, _ = sync(*sides_1, over)
    corners_1 = corners(*sides_1)
    far, *corners_0 = sync(far, *corners_0, sides_1[0])[:3]
    sides_3 = sides(far)
    other_0 = other(first, *sides_0, *corners_0)
    second, _ = sync(second, far)
    near_b, over_b = permute(second, Z1, n), permute(second, Z2, n)
    *sides_2, _ = sync(*sides_2, far)
    corners_2 = corners(*sides_2)
    *corners_1, _ = sync(*corners_1, sides_2[0])
    other_1 = other(near, *sides_1, *corners_1)
    *sides_3, _ = sync(*sides_3, sides_2[0])
    corners_3 = corners(*sides_3)
    over_b, near_b, _ = sync(over_b, near_b, sides_3[0])
    far_b = permute(over_b, Z1, n)
    *corners_2, _ = sync(*corners_2, sides_3[0])
    other_2 = other(over, *sides_2, *corners_2)
    *corners_3, far_b, _ = sync(*corners_3, far_b, corners_2[0])
    other_3 = other(far, *sides_3, *corners_3)
    column = jnp.concatenate([second, near_b, over_b, far_b], 0)
    found = []
    for z, arrays, packed in (
        (0, (first, *sides_0, *corners_0), other_0),
        (Z1, (near, *sides_1, *corners_1), other_1),
        (Z2, (over, *sides_2, *corners_2), other_2),
        (Z3, (far, *sides_3, *corners_3), other_3),
    ):
        pieces = [
            (0, z, None, 0, rows),
            (rows, z + X, None, 0, rows),
            (2 * rows, z + Y, None, 0, rows),
            (3 * rows, z + X + Y, None, 0, half),
            (3 * rows + half, z + X + Y, None, half, rows - half),
        ]
        for array, (_, relative, _, at, count) in zip(arrays, pieces):
            found.append((array, [(0, relative, None, at, count)]))
        found.append((packed, [(src, rel + CORE, None, at, count) for src, rel, _, at, count in pieces]))
    return found, column


def gather_sides(geo, column):
    return permute(column, X, geo.devices), permute(column, Y, geo.devices)


def gather_corners(geo, over_x, over_y):
    n, rows = geo.devices, geo.rows
    half = ceil_to(rows // 2, 16)
    cut_x = over_x.reshape(4, rows, LANES)[:, :half].reshape(-1, LANES)
    cut_y = over_y.reshape(4, rows, LANES)[:, half:].reshape(-1, LANES)
    return permute(cut_x, Y, n), permute(cut_y, X, n)


def gathered_pieces(geo, arrays, others):
    rows = geo.rows
    half = ceil_to(rows // 2, 16)
    found = []
    for core, group in ((0, arrays), (CORE, others)):
        for array, (relative, at, count) in zip(
            group, ((0, 0, rows), (X, 0, rows), (Y, 0, rows), (X + Y, 0, half), (X + Y, half, rows - half))
        ):
            found.append((array, [(z * count, relative + core + 8 * z, None, at, count) for z in range(4)]))
    return found


def gather_any(geo, chunk):
    gathered = lax.all_gather(chunk, AXES, axis=0)
    return [(gathered, [(0, 0, 0, 0, 0)])]


def add(*values):
    total = values[0].astype(F32)
    for value in values[1:]:
        total = total + value.astype(F32)
    return total


def plane_start(geo, keep, came):
    shape = (2, 2, 2, geo.rows, LANES)
    half = ceil_to(geo.rows // 2, 16)
    keep, came = keep.reshape(shape), came.reshape(shape)
    one = (keep[:, :, :, :half], came[:, :, :, :half])
    two = (keep[:, :, :, half:], came[:, :, :, half:])
    to_x = add(*(part[1] for part in one)).astype(BF16)
    to_y = add(*(part[:, 1] for part in two)).astype(BF16)
    return [part[0] for part in one], [part[:, 0] for part in two], to_x, to_y


def plane_next(one, two, from_x, from_y):
    one, two = one + [from_x], two + [from_y]
    to_y = add(*(part[1] for part in one)).astype(BF16)
    to_x = add(*(part[1] for part in two)).astype(BF16)
    return [part[0] for part in one], [part[0] for part in two], to_y, to_x


def plane_end(one, two, from_y, from_x):
    return jnp.concatenate([add(*one, from_y), add(*two, from_x)], 1)


def column_sum(geo, place, upper, lower, table):
    n = geo.devices
    if table:
        row = lax.broadcasted_iota(jnp.int32, (1, geo.rows, 1), 1)
        upper = jnp.where(row < geo.param_rows, upper, lower)
    is_upper = place[3] >= 2
    near = jnp.where(is_upper, upper, lower)
    far = jnp.where(is_upper, lower, upper).astype(BF16)
    return [near[0], permute(near[1].astype(BF16), Z1, n), permute(far[0], Z2, n), permute(far[1], Z3, n)]


def sum_any(chunks):
    return lax.psum_scatter(chunks.astype(F32), AXES, scatter_dimension=0, tiled=True)[0]


def timestep_embed(step_ids):
    half_dim = TD // 2
    freq_base = jnp.exp(jnp.arange(half_dim, dtype=F32) * (-math.log(10000.0) / half_dim))
    angle_grid = step_ids.astype(F32)[:, None] * freq_base[None, :]
    return jnp.concatenate([jnp.sin(angle_grid), jnp.cos(angle_grid)], axis=1)


def body(fast, chars, steps, embed, layer_params, cotangent):
    seqs, length = chars.shape
    tokens = seqs * length
    geo = Geometry(lax.axis_size(AXES), layer_params.shape[1], embed.shape[0])
    index = lax.axis_index(AXES).astype(jnp.int32)
    place = jnp.stack(
        [index, index * geo.shard % LANES, index * geo.embed_shard % LANES, index // 8]
    ).astype(jnp.int32)
    chunks = pack_shards(geo, place, layer_params, embed)
    emb = timestep_embed(steps).astype(BF16)
    emb_rows = jnp.concatenate([emb, jnp.zeros((8 - seqs, TD), BF16)], 0) if seqs < 8 else emb
    emb_t = emb.astype(F32).T
    chars_row, chars_col = chars.reshape(1, tokens), chars.reshape(tokens, 1)
    n = geo.devices

    cotangent = cotangent.reshape(tokens, D)
    if not fast:
        first = first_ahead(geo, seqs, place, gather_any(geo, chunks[0]), chars_col, emb_rows)
        first = first_ahead_rest(place, first)
        second = second_both(geo, fast, seqs, place, gather_any(geo, chunks[1]), first["stream"], emb_rows, cotangent)
        low_second = both_back_attn(geo, fast, 1, seqs, place, second["grad"], second, emb_t, second["rest"], chars_row)
        up_first = first_back_mlp(geo, fast, place, low_second["grad"], first)
        low_first = both_back_attn(geo, fast, 0, seqs, place, up_first["grad"], first, emb_t, up_first["rest"], chars_row)
        sums = [
            sum_any(jnp.concatenate([low_first["keep"], up_first["keep"]], 0)),
            sum_any(jnp.concatenate([low_second["keep"], second["keep"]], 0)),
            sum_any(low_first["table_out"]),
        ]
        grad_params, grad_embed = finish(geo, fast, place, sums)
        return (second["output"].reshape(seqs, length, D), grad_embed, grad_params)

    gathered, column = gather_both(geo, *chunks)
    sides = gather_sides(geo, column)
    column_other = permute(column, CORE, n)
    first = first_ahead(geo, seqs, place, gathered, chars_col, emb_rows)
    first, sides, column_other = sync(first, sides, column_other)
    corners = gather_corners(geo, *sides)
    sides_other = [permute(side, CORE, n) for side in sides]
    first = first_ahead_rest(place, first)
    first, corners, sides_other = sync(first, corners, sides_other)
    corners_other = [permute(corner, CORE, n) for corner in corners]
    pieces = gathered_pieces(geo, [column, *sides, *corners], [column_other, *sides_other, *corners_other])
    second = second_both(geo, fast, seqs, place, pieces, first["stream"], emb_rows, cotangent)
    output = second["output"].reshape(seqs, length, D)

    def cross(to_one, to_two, one, two):
        return permute(to_one, one, n), permute(to_two, two, n)

    def attn(layer, grad, found, rest):
        got = both_back_attn(geo, fast, layer, seqs, place, grad, found, emb_t, rest, chars_row)
        return (got["keep"], got["send"]) if layer == 0 else (got["grad"], got["keep"], got["send"])

    grad, rest, keep_u, send_u = (second[name] for name in ("grad", "rest", "keep", "send"))
    came_u = permute(send_u, CORE, n)
    grad, keep_l, send_l = attn(1, grad, second, rest)
    grad, keep_u, came_u, keep_l, send_l = sync(grad, keep_u, came_u, keep_l, send_l)
    came_l = permute(send_l, CORE, n)
    one_u, two_u, to_x, to_y = plane_start(geo, keep_u, came_u)
    from_u = cross(to_x, to_y, X, Y)

    got = first_back_mlp(geo, fast, place, after(grad, to_x, to_y), first)
    grad, rest, keep, send = (got[name] for name in ("grad", "rest", "keep", "send"))
    grad, rest, keep, send, came_l, from_u = sync(grad, rest, keep, send, came_l, from_u)
    came = permute(send, CORE, n)
    one_u, two_u, to_y, to_x = plane_next(one_u, two_u, *from_u)
    from_u = cross(to_y, to_x, Y, X)
    one_l, two_l, to_x_l, to_y_l = plane_start(geo, keep_l, came_l)
    from_l = cross(to_x_l, to_y_l, X, Y)

    grad = after(grad, to_x, to_y, to_x_l, to_y_l)
    low_keep, low_send = attn(0, grad, first, rest)
    low_keep, low_send, keep, came, from_u, from_l = sync(low_keep, low_send, keep, came, from_u, from_l)
    low_came = permute(low_send, CORE, n)
    one_l, two_l, to_y, to_x = plane_next(one_l, two_l, *from_l)
    from_l = cross(to_y, to_x, Y, X)
    one, two, to_x, to_y = plane_start(geo, keep, came)
    from_up = cross(to_x, to_y, X, Y)
    upper = plane_end(one_u, two_u, *from_u)

    low_came, low_keep, upper, _, _ = sync(low_came, low_keep, upper, to_x, to_y)
    low_one, low_two, to_x, to_y = plane_start(geo, low_keep, low_came)
    from_low = cross(to_x, to_y, X, Y)

    from_l, from_up, _, _ = sync(from_l, from_up, to_x, to_y)
    lower = plane_end(one_l, two_l, *from_l)
    seconds = column_sum(geo, place, upper, lower, False)
    one, two, to_y, to_x = plane_next(one, two, *from_up)
    from_up = cross(to_y, to_x, Y, X)

    from_low, _, _ = sync(from_low, to_y, to_x)
    low_one, low_two, to_y, to_x = plane_next(low_one, low_two, *from_low)
    from_low = cross(to_y, to_x, Y, X)

    from_low, from_up = sync(from_low, from_up)
    upper, lower = plane_end(one, two, *from_up), plane_end(low_one, low_two, *from_low)
    firsts = column_sum(geo, place, upper, lower, True)
    grad_params, grad_embed = finish(geo, fast, place, firsts + seconds)
    return (output, grad_embed, grad_params)


def solution(mesh):
    both = P(AXES)
    fast = dict(mesh.shape) == {"dp": 8, "fsdp": 4}
    return jax.shard_map(
        functools.partial(body, fast),
        mesh=mesh,
        in_specs=(P(AXES, None), both, both, P(None, AXES), P(AXES, None, None)),
        out_specs=(P(AXES, None, None), both, P(None, AXES)),
        check_vma=False,
    )
```

```python
import functools
import math

import jax
import jax.numpy as jnp
from jax import lax
from jax.experimental import pallas as pl
from jax.experimental.pallas import tpu as pltpu
from jax.sharding import PartitionSpec as P

D = 512
HEADS = 8
FF = 2048
VOCAB = 27
TD = 128
HD = 64
LANES = 128
EPSILON = 1e-05
AXES = ("dp", "fsdp")
F32 = jnp.float32
BF16 = jnp.bfloat16
VMEM_BYTES = 52 * 2**20

(
    N_CHARS, N_EMB, N_W_TIME, N_W_QKV, N_W_OUT, N_W_UP, N_W_DOWN,
    N_VECTORS, N_TABLE, N_X, N_A, N_QKV, N_PROB, N_O,
    N_X2, N_A2, N_GL, N_SLOPE, N_STREAM, N_OUTPUT, N_COTANGENT,
    N_GRAD, N_GRAD_IN, N_REST, N_KEEP, N_SEND, N_TABLE_OUT, N_EMB_T,
    N_CHUNKS, N_FLAT, N_FLAT_TABLE, N_CUTS, N_CUT_SEMS, N_NORMED, N_TOTAL,
    N_QKV_GRAD, N_HEADS_GRAD,
) = range(37)

ROW_GAIN_ONE, ROW_BIAS_ONE, ROW_W_TIME, ROW_B_TIME = 0, 4, 8, 520
ROW_QKV, ROW_OUT, ROW_GAIN_TWO, ROW_BIAS_TWO = 524, 6668, 8716, 8720
ROW_UP, ROW_B_UP, ROW_DOWN, ROW_B_DOWN, ROW_END = 8724, 16916, 16932, 25124, 25128
CHUNK_PAD = 832


def ceil_to(value, step):
    return -(-value // step) * step


class Geometry:
    def __init__(self, devices, shard, embed_shard):
        self.devices, self.shard, self.embed_shard = devices, shard, embed_shard
        self.param_rows = max(self.count(d, shard) for d in range(devices))
        self.embed_rows = max(self.count(d, embed_shard) for d in range(devices))
        self.embed_at = ceil_to(self.param_rows, 8)
        self.rows = ceil_to(max(self.embed_at + 8, self.param_rows + 2 * self.embed_rows), 16)

    @staticmethod
    def first(d, size):
        return d * size // LANES

    @staticmethod
    def count(d, size):
        return -(-(d + 1) * size // LANES) - d * size // LANES


def params(flops, nbytes, weight=0):
    flops, nbytes = max(flops * weight, 1000), max(nbytes * weight, 1000)
    return dict(
        compiler_params=pltpu.CompilerParams(vmem_limit_bytes=VMEM_BYTES),
        cost_estimate=pl.CostEstimate(flops=flops, bytes_accessed=nbytes, transcendentals=0),
    )


VM = pl.BlockSpec(memory_space=pltpu.VMEM)
SM = pl.BlockSpec(memory_space=pltpu.SMEM)
HBM = pl.BlockSpec(memory_space=pltpu.HBM)


def nn(left, right):
    return lax.dot_general(left, right, (((1,), (0,)), ((), ())), preferred_element_type=F32)


def nt(left, right):
    return lax.dot_general(left, right, (((1,), (1,)), ((), ())), preferred_element_type=F32)


def tn(left, right):
    return nn(left.T, right)


def shift_in(flat, offset):
    rolled = pltpu.roll(flat, offset, 1)
    above = jnp.concatenate([jnp.zeros((1, LANES), F32), rolled[:-1]], 0)
    lane = lax.broadcasted_iota(jnp.int32, flat.shape, 1)
    return jnp.where(lane >= offset, rolled, above)


def shift_out(flat, offset):
    rolled = pltpu.roll(flat, lax.rem(LANES - offset, LANES), 1)
    below = jnp.concatenate([rolled[1:], jnp.zeros((1, LANES), F32)], 0)
    lane = lax.broadcasted_iota(jnp.int32, flat.shape, 1)
    return jnp.where(lane < LANES - offset, rolled, below)


def pack_kernel(geo, place_ref, layers_ref, embed_ref, first_ref, second_ref):
    main = geo.embed_at
    for layer, out_ref in ((0, first_ref), (1, second_ref)):
        moved = shift_in(layers_ref[layer].astype(F32), place_ref[1])
        if layer == 0:
            tail = shift_in(embed_ref[...].astype(F32), place_ref[2])
            parts = [moved[:main], tail] + ([moved[main + 8 :]] if geo.rows > main + 8 else [])
            moved = jnp.concatenate(parts, 0)
        out_ref[...] = moved.astype(BF16)


def pack_shards(geo, place, layer_params, embed):
    layers = jnp.pad(layer_params, ((0, 0), (0, geo.rows * LANES - geo.shard)))
    table = jnp.pad(embed, (0, 8 * LANES - geo.embed_shard))
    out = jax.ShapeDtypeStruct((geo.rows, LANES), BF16)
    return pl.pallas_call(
        functools.partial(pack_kernel, geo),
        out_shape=(out, out),
        in_specs=[SM, VM, VM],
        out_specs=(VM, VM),
        **params(10**6, geo.rows * 1024),
    )(place, layers.reshape(2, geo.rows, LANES), table.reshape(8, LANES))


def finish_kernel(geo, fast, place_ref, *refs):
    grads_ref, embed_ref, moved = refs[-3:]
    parts = refs[:-3]
    count = 4 if fast else 1
    for layer in range(2):
        total = parts[layer * count][...].astype(F32)
        for part in parts[layer * count + 1 : (layer + 1) * count]:
            total = total + part[...].astype(F32)
        moved[pl.ds(layer * geo.rows, geo.rows), :] = shift_out(total, place_ref[1])
        if fast and layer == 0:
            first, size = geo.param_rows, geo.embed_rows
            lower, upper = total[first : first + size], total[first + size : first + 2 * size]
            tail = jnp.where(place_ref[3] >= 2, upper, lower)
            tail = jnp.concatenate([tail, jnp.zeros((8 - size, LANES), F32)], 0)
    if not fast:
        tail = parts[2][...]
    embed_ref[...] = shift_out(tail, place_ref[2])
    for r in range(ceil_to(geo.shard, LANES) // LANES):
        size = min(LANES, geo.shard - r * LANES)
        grads_ref[:, r * LANES : r * LANES + size] = moved[pl.ds(r, 2, stride=geo.rows), :][:, :size]


def finish(geo, fast, place, operands):
    grads, table = pl.pallas_call(
        functools.partial(finish_kernel, geo, fast),
        out_shape=(
            jax.ShapeDtypeStruct((2, geo.shard), F32),
            jax.ShapeDtypeStruct((8, LANES), F32),
        ),
        in_specs=[SM] + [VM] * len(operands),
        out_specs=(VM, VM),
        scratch_shapes=[pltpu.VMEM((2 * geo.rows, LANES), F32)],
        **params(10**6, geo.rows * 4096),
    )(place, *operands)
    return grads, table.reshape(-1)[: geo.embed_shard]


class Staged:
    def __init__(self, sources, targets, held, sems):
        self.held, self.pending, self.sent = held, {}, []
        self.targets, self.sems = targets, sems
        self.used = len(sources)
        for i, name in enumerate(sources):
            self.pending[name] = pltpu.make_async_copy(sources[name], held[name], sems.at[i])
            self.pending[name].start()

    def get(self, *names):
        for name in names:
            if name in self.pending:
                self.pending.pop(name).wait()
        found = [self.held[name] for name in names]
        return found[0] if len(found) == 1 else found

    def put(self, *names):
        for name in names:
            copy = pltpu.make_async_copy(self.held[name], self.targets[name], self.sems.at[self.used])
            copy.start()
            self.used += 1
            self.sent.append(copy)

    def close(self):
        for copy in list(self.pending.values()) + self.sent:
            copy.wait()


def staged_call(kernel, place, operands, results, scratch, flops, raw=(), semaphores=0, unheld=()):
    names, outs, temps = list(operands), list(results), list(scratch)

    held_outs = [name for name in outs if name not in unheld]

    def whole(place_ref, *refs):
        raws, refs = refs[: len(raw)], refs[len(raw) :]
        sources, refs = dict(zip(names, refs)), refs[len(names) :]
        targets, refs = dict(zip(outs, refs)), refs[len(outs) :]
        held, refs = dict(zip(names + held_outs, refs)), refs[len(names) + len(held_outs) :]
        extra, refs = dict(zip(temps, refs)), refs[len(temps) :]
        staged = Staged(sources, targets, held, refs[0])
        kernel(place_ref, raws, staged, extra, refs[-1])
        staged.close()

    buffers = [pltpu.VMEM(v.shape, v.dtype) for v in (*operands.values(), *(results[name] for name in held_outs))]
    sems = [pltpu.SemaphoreType.DMA((len(names) + len(outs),))]
    if semaphores:
        sems.append(pltpu.SemaphoreType.DMA((semaphores,)))
    found = pl.pallas_call(
        whole,
        out_shape=tuple(pltpu.HBM(v.shape, v.dtype) for v in results.values()),
        in_specs=[SM] + [HBM] * (len(raw) + len(names)),
        out_specs=(HBM,) * len(outs),
        scratch_shapes=buffers + list(scratch.values()) + sems,
        **params(flops, 2 * 10**7, 1),
    )(place, *(pltpu.with_memory_space_constraint(v, pltpu.HBM) for v in (*raw, *operands.values())))
    return dict(zip(outs, found))


def like(dtype, *shape):
    return jax.ShapeDtypeStruct(shape, dtype)


def unpack(geo, layer, plan, me, chunk_refs, held, flat, flat_table, out, sems):
    copies = []
    for source, pieces in zip(chunk_refs, plan):
        for src_at, relative, absolute, dst_at, count in pieces:
            if absolute is None:
                target = held.at[lax.bitwise_xor(me, relative), pl.ds(dst_at, count)]
                origin = source.at[pl.ds(src_at, count)]
            else:
                target, origin = held, source
            copies.append(pltpu.make_async_copy(origin, target, sems.at[len(copies)]))
    for copy in copies:
        copy.start()
    for copy in copies:
        copy.wait()
    for d in range(geo.devices):
        block = held[d].astype(F32)
        start, rows = geo.first(d, geo.shard), geo.count(d, geo.shard)
        split = (d * geo.shard) % LANES != 0
        if split:
            shared = flat[pl.ds(start, 1), :] + block[:1]
        flat[pl.ds(start, rows), :] = block[:rows]
        if split:
            flat[pl.ds(start, 1), :] = shared
        if layer == 0:
            tail = block[geo.embed_at : geo.embed_at + 8]
            start, rows = geo.first(d, geo.embed_shard), geo.count(d, geo.embed_shard)
            split = (d * geo.embed_shard) % LANES != 0
            if split:
                shared = flat_table[pl.ds(start, 1), :] + tail[:1]
            flat_table[pl.ds(start, rows), :] = tail[:rows]
            if split:
                flat_table[pl.ds(start, 1), :] = shared
    vectors = out[N_VECTORS]
    for row, start, width in (
        (0, ROW_GAIN_ONE, 4),
        (1, ROW_BIAS_ONE, 4),
        (2, ROW_B_TIME, 4),
        (3, ROW_GAIN_TWO, 4),
        (4, ROW_BIAS_TWO, 4),
        (5, ROW_B_DOWN, 4),
        (6, ROW_B_UP, 16),
    ):
        for c in range(width):
            vectors[row : row + 1, c * LANES : (c + 1) * LANES] = flat[pl.ds(start + c, 1), :]
    for name, start, rows, width in (
        (N_W_TIME, ROW_W_TIME, TD, 4),
        (N_W_QKV, ROW_QKV, D, 12),
        (N_W_OUT, ROW_OUT, D, 4),
        (N_W_UP, ROW_UP, D, 16),
        (N_W_DOWN, ROW_DOWN, FF, 4),
    ):
        for c in range(width):
            out[name][:, c * LANES : (c + 1) * LANES] = flat[pl.ds(start + c, rows, stride=width), :].astype(BF16)
    if layer == 0:
        table = out[N_TABLE]
        table[...] = jnp.zeros(table.shape, BF16)
        for c in range(4):
            table[0:VOCAB, c * LANES : (c + 1) * LANES] = flat_table[pl.ds(c, VOCAB, stride=4), :].astype(BF16)


WEIGHTS = {
    N_W_QKV: like(BF16, D, 3 * D),
    N_W_OUT: like(BF16, D, D),
    N_W_UP: like(BF16, D, FF),
    N_W_DOWN: like(BF16, FF, D),
    N_VECTORS: like(F32, 8, FF),
}


def unpack_scratch(geo, layer):
    scratch = {
        N_CHUNKS: pltpu.VMEM((geo.devices, geo.rows, LANES), BF16),
        N_FLAT: pltpu.VMEM((ROW_END + CHUNK_PAD, LANES), F32),
        N_FLAT_TABLE: pltpu.VMEM((4 * 32, LANES), F32),
        N_W_TIME: pltpu.VMEM((TD, D), BF16),
    }
    if layer == 0:
        scratch[N_TABLE] = pltpu.VMEM((32, D), BF16)
    return scratch


def split_gathered(gathered):
    plan = tuple(tuple(pieces) for array, pieces in gathered)
    return [array for array, pieces in gathered], plan, sum(len(pieces) for pieces in plan)


def norm_stats(values):
    mean = jnp.mean(values, -1, keepdims=True)
    centered = values - mean
    variance = jnp.mean(centered * centered, -1, keepdims=True)
    scale = lax.rsqrt(variance + EPSILON)
    return centered * scale, scale


ROW_BLOCK = 64


def norm_ahead(values, gain, bias, out):
    for r in range(0, values.shape[0], ROW_BLOCK):
        rows = slice(r, r + ROW_BLOCK)
        unit, _ = norm_stats(values[rows, :])
        out[rows, :] = (unit * gain + bias).astype(BF16)


def norm_back(grad, values, gain, passed, out):
    grad_gain, grad_bias = jnp.zeros((8, D), F32), jnp.zeros((8, D), F32)
    for r in range(0, values.shape[0], ROW_BLOCK):
        rows = slice(r, r + ROW_BLOCK)
        unit, scale = norm_stats(values[rows, :])
        block = grad[rows, :]
        grad_gain = grad_gain + jnp.sum((block * unit).reshape(-1, 8, D), 0)
        grad_bias = grad_bias + jnp.sum(block.reshape(-1, 8, D), 0)
        inner = block * gain
        shifted = inner - jnp.mean(inner, -1, keepdims=True)
        back = scale * (shifted - unit * jnp.mean(inner * unit, -1, keepdims=True))
        out[rows, :] = passed[rows, :].astype(F32) + back
    return jnp.sum(grad_gain, 0, keepdims=True), jnp.sum(grad_bias, 0, keepdims=True)


def gelu_both(u):
    root = math.sqrt(2.0 / math.pi)
    square = u * u
    t = jnp.tanh(root * (u + 0.044715 * (square * u)))
    half = 0.5 * (1.0 + t)
    slope = half + 0.5 * u * (1.0 - t * t) * (root * (1.0 + 3.0 * 0.044715 * square))
    return u * half, slope


def head_masks(shape, scale):
    lane = lax.broadcasted_iota(jnp.int32, shape, 1)
    one = jnp.where(lane < HD, scale, 0.0).astype(BF16)
    two = jnp.where(lane < HD, 0.0, scale).astype(BF16)
    return one, two


def ahead_attn(seqs, stream, emb, w_time, w_qkv, w_out, vectors, x, a, qkv, prob, o, x2, a2, done):
    tokens = x.shape[0]
    length = tokens // seqs
    time_vec = nn(emb[...], w_time[...]) + vectors[2:3, :D]
    for s in range(seqs):
        x[s * length : (s + 1) * length, :] = stream[s * length : (s + 1) * length] + time_vec[s : s + 1]
    done(N_X)
    norm_ahead(x, vectors[0:1, :D], vectors[1:2, :D], a)
    done(N_A)
    for c in range(3):
        part = slice(c * D, (c + 1) * D)
        qkv[:, part] = nn(a[...], w_qkv[:, part]).astype(BF16)
    done(N_QKV)
    masks = head_masks((length, LANES), 1.0 / math.sqrt(HD))
    for s in range(seqs):
        rows = slice(s * length, (s + 1) * length)
        for pair in range(HEADS // 2):
            cols = [slice(c * D + pair * LANES, c * D + (pair + 1) * LANES) for c in range(3)]
            q, k, v_t = qkv[rows, cols[0]], qkv[rows, cols[1]], qkv[rows, cols[2]].T
            mixed = []
            for h in range(2):
                scores = nt(k * masks[h], q)
                top = jnp.max(scores, 0, keepdims=True)
                expd = jnp.exp(scores - top)
                low = (expd * (1.0 / jnp.sum(expd, 0, keepdims=True))).astype(BF16)
                prob[s * HEADS + 2 * pair + h] = low
                mixed.append(nn(v_t[h * HD : (h + 1) * HD], low))
            o[rows, cols[0]] = jnp.concatenate(mixed, 0).T.astype(BF16)
    done(N_PROB)
    done(N_O)
    x2[...] = x[...] + nn(o[...], w_out[...])
    done(N_X2)
    norm_ahead(x2, vectors[3:4, :D], vectors[4:5, :D], a2)
    done(N_A2)


def ahead_mlp(x2, a2, w_up, w_down, vectors, gl, slope):
    parts = [slice(c * D, (c + 1) * D) for c in range(FF // D)]

    def up(part):
        return nn(a2()[...], w_up()[:, part])

    total, u = None, up(parts[0])
    for c, part in enumerate(parts):
        value, rate = gelu_both(u + vectors()[6:7, part])
        low = value.astype(BF16)
        gl[:, part] = low
        slope[:, part] = rate.astype(BF16)
        if c + 1 < len(parts):
            u = up(parts[c + 1])
        step = nn(low, w_down()[part, :])
        total = step if total is None else total + step
    return x2()[...] + vectors()[5:6, :D] + total


class Chunks:
    def __init__(self, geo, fast, me, held, targets, sems):
        self.geo, self.fast, self.me, self.held, self.targets, self.sems = geo, fast, me, held, targets, sems
        self.copies = []

    def cut(self, d, flat, base, table=None):
        geo, slot = self.geo, d % (self.geo.devices // 2)
        block = flat[pl.ds(geo.first(d, geo.shard) - base, geo.rows), :]
        if table is not None:
            first, size = geo.param_rows, geo.embed_rows
            tails = [
                table[pl.ds(geo.first(e, geo.embed_shard), size), :] for e in (d, d + geo.devices // 2)
            ]
            block = jnp.concatenate([block[:first], *tails, block[first + 2 * size :]], 0)
        self.held[slot] = block.astype(BF16)
        source, sem = self.held.at[slot], self.sems.at[slot]
        if not self.fast:
            self.copies.append(pltpu.make_async_copy(source, self.targets[0].at[slot], sem))
            self.copies[-1].start()
            return
        relative = lax.bitwise_xor(self.me, d)
        row = lax.bitwise_and(relative, 4) + lax.bitwise_and(relative, 2)
        row = row + lax.bitwise_and(lax.shift_right_logical(relative, 3), 1)
        keep, send = (pltpu.make_async_copy(source, target.at[row], sem) for target in self.targets)
        core = lax.bitwise_and(relative, 1)

        @pl.when(core == 0)
        def _():
            keep.start()

        @pl.when(core == 1)
        def _():
            send.start()

        self.copies.append(keep)

    def close(self):
        for copy in self.copies:
            copy.wait()


def back_mlp(geo, chunks, grad_in, x2, a2, gl, slope, w_up, w_down, vectors, grad, rest, flat, base, normed, done):
    grad_low = grad_in()[...].astype(BF16)
    flat[pl.ds(ROW_END - base, CHUNK_PAD), :] = jnp.zeros((CHUNK_PAD, LANES), F32)
    grad_bias = jnp.sum(grad_low.astype(F32), 0, keepdims=True)
    for c in range(4):
        flat[pl.ds(ROW_B_DOWN - base + c, 1), :] = grad_bias[:, c * LANES : (c + 1) * LANES]
    parts = [slice(j * D, (j + 1) * D) for j in range(FF // D)]

    def hidden_grad(part):
        return nt(grad_low, w_down()[part, :])

    total, hidden = None, hidden_grad(parts[0])
    for j, part in enumerate(parts):
        up_grad = (hidden * slope()[:, part].astype(F32)).astype(BF16)
        bias_grad = jnp.sum(up_grad.astype(F32), 0, keepdims=True)
        if j + 1 < len(parts):
            hidden = hidden_grad(parts[j + 1])
        down = tn(gl()[:, part], grad_low)
        for c in range(4):
            cols = slice(c * LANES, (c + 1) * LANES)
            flat[pl.ds(ROW_B_UP - base + 4 * j + c, 1), :] = bias_grad[:, cols]
            flat[pl.ds(ROW_DOWN - base + 4 * D * j + c, D, stride=4), :] = down[:, cols]
        up = tn(a2()[...], up_grad)
        for c in range(4):
            cols = slice(c * LANES, (c + 1) * LANES)
            flat[pl.ds(ROW_UP - base + 4 * j + c, D, stride=16), :] = up[:, cols]
        step = nt(up_grad, w_up()[:, part])
        total = step if total is None else total + step
    normed[...] = total
    for d in range(geo.devices // 2, geo.devices):
        chunks.cut(d, flat, base)
    grad_gain, grad_bias = norm_back(normed, x2(), vectors()[3:4, :D], grad_in(), grad)
    done(N_GRAD)
    for c in range(4):
        cols = slice(c * LANES, (c + 1) * LANES)
        flat[pl.ds(ROW_GAIN_TWO - base + c, 1), :] = grad_gain[:, cols]
        flat[pl.ds(ROW_BIAS_TWO - base + c, 1), :] = grad_bias[:, cols]
    rest[...] = flat[pl.ds(ROW_GAIN_TWO - base, rest.shape[0]), :].astype(BF16)
    done(N_REST)


def back_attn(
    geo, seqs, chunks, table, embed_outs, grad_in, x, a, qkv, prob, o, w_qkv, w_out, vectors, emb_t, rest, total,
    flat, qkv_grad, heads_grad, normed, chars, done,
):
    tokens = normed.shape[0]
    length = tokens // seqs
    grad_low = grad_in()[...].astype(BF16)
    heads_grad[...] = nt(grad_low, w_out()[...]).astype(BF16)
    out_grad = tn(o()[...], grad_low)
    for c in range(4):
        flat[pl.ds(ROW_OUT + c, D, stride=4), :] = out_grad[:, c * LANES : (c + 1) * LANES]
    masks = head_masks((length, LANES), 1.0)
    scale = 1.0 / math.sqrt(HD)
    lane = lax.broadcasted_iota(jnp.int32, (length, LANES), 1)
    qkv, prob = qkv(), prob()
    for s in range(seqs):
        rows = slice(s * length, (s + 1) * length)
        for pair in range(HEADS // 2):
            cols = [slice(c * D + pair * LANES, c * D + (pair + 1) * LANES) for c in range(3)]
            q, k, v = qkv[rows, cols[0]], qkv[rows, cols[1]], qkv[rows, cols[2]]
            go = heads_grad[rows, cols[0]]
            k_t = k.T
            to_q, to_k, to_v = [], [], []
            for h in range(2):
                prob_low = prob[s * HEADS + 2 * pair + h]
                prob_full = prob_low.astype(F32)
                prob_grad = nt(v * masks[h], go)
                weighted = prob_full * prob_grad
                row_dot = jnp.sum(weighted, 0, keepdims=True)
                score_grad = (weighted - prob_full * row_dot).astype(BF16)
                to_q.append(nn(k_t[h * HD : (h + 1) * HD], score_grad))
                to_k.append(nn(score_grad, q))
                to_v.append(nn(prob_low, go))
            qkv_grad[rows, cols[0]] = (jnp.concatenate(to_q, 0).T * scale).astype(BF16)
            qkv_grad[rows, cols[1]] = (jnp.where(lane < HD, to_k[0], to_k[1]) * scale).astype(BF16)
            qkv_grad[rows, cols[2]] = jnp.where(lane < HD, to_v[0], to_v[1]).astype(BF16)
    a_t, steps = a()[...].T, None
    for part in range(3):
        cols = slice(part * D, (part + 1) * D)
        piece = nn(a_t, qkv_grad[:, cols])
        for c in range(4):
            flat[pl.ds(ROW_QKV + 4 * part + c, D, stride=12), :] = piece[:, c * LANES : (c + 1) * LANES]
        step = nt(qkv_grad[:, cols], w_qkv()[:, cols])
        steps = step if steps is None else steps + step
    normed[...] = steps
    flat[pl.ds(ROW_GAIN_TWO, rest().shape[0]), :] = rest()[...].astype(F32)
    middle = geo.devices // 2
    early = [d for d in range(middle) if geo.first(d, geo.shard) >= ROW_QKV] if table is None else []
    for d in early:
        chunks.cut(d, flat, 0)
    grad_gain, grad_bias = norm_back(normed, x(), vectors()[0:1, :D], grad_in(), total)
    done(N_GRAD)
    time_grad = [
        jnp.sum(total[s * length : (s + 1) * length, :], 0, keepdims=True).astype(BF16).astype(F32) for s in range(seqs)
    ]
    bias_grad = sum(time_grad[1:], time_grad[0])
    weight_grad = sum(emb_t()[:, s : s + 1] * time_grad[s] for s in range(seqs))
    for c in range(4):
        cols = slice(c * LANES, (c + 1) * LANES)
        flat[pl.ds(ROW_GAIN_ONE + c, 1), :] = grad_gain[:, cols]
        flat[pl.ds(ROW_BIAS_ONE + c, 1), :] = grad_bias[:, cols]
        flat[pl.ds(ROW_B_TIME + c, 1), :] = bias_grad[:, cols]
        flat[pl.ds(ROW_W_TIME + c, TD, stride=4), :] = weight_grad[:, cols]
    if table is not None:
        kind = lax.broadcasted_iota(jnp.int32, (32, tokens), 0)
        table_grad = nn((chars()[...] == kind).astype(BF16), total[...].astype(BF16))
        for c in range(4):
            table[pl.ds(c, 32, stride=4), :] = table_grad[:, c * LANES : (c + 1) * LANES]
    for d in range(middle):
        if d not in early:
            chunks.cut(d, flat, 0, table if chunks.fast else None)
    if table is not None and not chunks.fast:
        for d in range(geo.devices):
            embed_outs[d] = table[pl.ds(geo.first(d, geo.embed_shard), 8), :]


def kept_shapes(seqs, tokens):
    length = tokens // seqs
    return {
        N_X: like(F32, tokens, D),
        N_A: like(BF16, tokens, D),
        N_QKV: like(BF16, tokens, 3 * D),
        N_PROB: like(BF16, seqs * HEADS, length, length),
        N_O: like(BF16, tokens, D),
    }


def rest_rows(geo):
    middle = geo.first(geo.devices // 2, geo.shard)
    return ceil_to(middle + geo.rows - ROW_GAIN_TWO, 16)


def chunk_results(geo, fast):
    if fast:
        shape = like(BF16, geo.devices // 4, geo.rows, LANES)
        return {N_KEEP: shape, N_SEND: shape}
    return {N_KEEP: like(BF16, geo.devices // 2, geo.rows, LANES)}


def chunk_targets(staged, fast):
    return [staged.targets[name] for name in ((N_KEEP, N_SEND) if fast else (N_KEEP,))]


def chunk_scratch(geo, tokens):
    return {
        N_CUTS: pltpu.VMEM((geo.devices // 2, geo.rows, LANES), BF16),
        N_CUT_SEMS: pltpu.SemaphoreType.DMA((geo.devices // 2,)),
        N_NORMED: pltpu.VMEM((tokens, D), F32),
    }


def first_ahead(geo, seqs, place, gathered, chars, emb):
    tokens = chars.shape[0]
    arrays, plan, count = split_gathered(gathered)
    results = WEIGHTS | kept_shapes(seqs, tokens) | {N_X2: like(F32, tokens, D), N_A2: like(BF16, tokens, D)}

    def kernel(place_ref, chunk_refs, staged, extra, sems):
        held = staged.held
        unpack(
            geo, 0, plan, place_ref[0], chunk_refs, extra[N_CHUNKS], extra[N_FLAT], extra[N_FLAT_TABLE], held | extra, sems
        )
        staged.put(*WEIGHTS)
        lane = lax.broadcasted_iota(jnp.int32, (tokens, 32), 1)
        stream = nn((staged.get(N_CHARS)[...] == lane).astype(BF16), extra[N_TABLE][...])
        weights = [extra[N_W_TIME]] + [held[name] for name in (N_W_QKV, N_W_OUT, N_VECTORS)]
        outs = [held[name] for name in (N_X, N_A, N_QKV, N_PROB, N_O, N_X2, N_A2)]
        ahead_attn(seqs, stream, staged.get(N_EMB), *weights, *outs, staged.put)

    operands = {N_CHARS: chars, N_EMB: emb}
    scratch = unpack_scratch(geo, 0)
    return staged_call(kernel, place, operands, results, scratch, 4 * 10**9, arrays, count)


def first_ahead_rest(place, found):
    names = (N_A2, N_W_UP, N_VECTORS, N_W_DOWN, N_X2)
    operands = {name: found[name] for name in names}
    tokens = found[N_X2].shape[0]
    results = {N_STREAM: like(F32, tokens, D), N_GL: like(BF16, tokens, FF), N_SLOPE: like(BF16, tokens, FF)}

    def kernel(place_ref, _, staged, extra, sems):
        late = [functools.partial(staged.get, name) for name in (N_X2, N_A2, N_W_UP, N_W_DOWN, N_VECTORS)]
        gl, slope, stream = (staged.held[name] for name in (N_GL, N_SLOPE, N_STREAM))
        stream[...] = ahead_mlp(*late, gl, slope)
        staged.put(N_GL, N_SLOPE, N_STREAM)

    return found | staged_call(kernel, place, operands, results, {}, 4 * 10**9)


def second_both(geo, fast, seqs, place, gathered, stream, emb, cotangent):
    tokens = stream.shape[0]
    arrays, plan, count = split_gathered(gathered)
    results = {name: WEIGHTS[name] for name in (N_W_QKV, N_W_OUT, N_VECTORS)}
    results = results | kept_shapes(seqs, tokens)
    results = results | {
        N_OUTPUT: like(BF16, tokens, D),
        N_GRAD: like(F32, tokens, D),
        N_REST: like(BF16, rest_rows(geo), LANES),
    }
    results = results | chunk_results(geo, fast)
    scratch = unpack_scratch(geo, 1)
    scratch[N_W_UP], scratch[N_W_DOWN] = pltpu.VMEM((D, FF), BF16), pltpu.VMEM((FF, D), BF16)
    scratch[N_X2], scratch[N_A2] = pltpu.VMEM((tokens, D), F32), pltpu.VMEM((tokens, D), BF16)
    scratch[N_GL], scratch[N_SLOPE] = pltpu.VMEM((tokens, FF), BF16), pltpu.VMEM((tokens, FF), BF16)
    scratch = scratch | chunk_scratch(geo, tokens)

    def kernel(place_ref, chunk_arrays, staged, extra, sems):
        every = staged.held | extra
        unpack(geo, 1, plan, place_ref[0], chunk_arrays, extra[N_CHUNKS], extra[N_FLAT], extra[N_FLAT_TABLE], every, sems)
        staged.put(N_W_QKV, N_W_OUT, N_VECTORS)
        weights = [every[name] for name in (N_W_TIME, N_W_QKV, N_W_OUT, N_VECTORS)]
        outs = [every[name] for name in (N_X, N_A, N_QKV, N_PROB, N_O, N_X2, N_A2)]

        def done(name):
            if name in results:
                staged.put(name)

        ahead_attn(seqs, staged.get(N_STREAM)[...], staged.get(N_EMB), *weights, *outs, done)

        def ready(*names):
            return [functools.partial(every.get, name) for name in names]

        outputs = ahead_mlp(*ready(N_X2, N_A2, N_W_UP, N_W_DOWN, N_VECTORS), every[N_GL], every[N_SLOPE])
        every[N_OUTPUT][...] = outputs.astype(BF16)
        done(N_OUTPUT)
        chunks = Chunks(geo, fast, place_ref[0], extra[N_CUTS], chunk_targets(staged, fast), extra[N_CUT_SEMS])
        back_mlp(
            geo, chunks, functools.partial(staged.get, N_COTANGENT),
            *ready(N_X2, N_A2, N_GL, N_SLOPE, N_W_UP, N_W_DOWN, N_VECTORS),
            every[N_GRAD], every[N_REST], extra[N_FLAT], 0, extra[N_NORMED], done,
        )
        chunks.close()

    operands = {N_STREAM: stream, N_EMB: emb, N_COTANGENT: cotangent}
    return staged_call(kernel, place, operands, results, scratch, 10**10, arrays, count, (N_KEEP, N_SEND))


def first_back_mlp(geo, fast, place, grad, found):
    names = (N_GRAD_IN, N_W_DOWN, N_SLOPE, N_GL, N_A2, N_W_UP, N_X2, N_VECTORS)
    operands = {name: grad if name == N_GRAD_IN else found[name] for name in names}
    tokens = grad.shape[0]
    results = {N_GRAD: like(F32, tokens, D), N_REST: like(BF16, rest_rows(geo), LANES)} | chunk_results(geo, fast)
    base = ROW_GAIN_TWO

    def kernel(place_ref, _, staged, extra, sems):
        late = [
            functools.partial(staged.get, name)
            for name in (N_GRAD_IN, N_X2, N_A2, N_GL, N_SLOPE, N_W_UP, N_W_DOWN, N_VECTORS)
        ]
        chunks = Chunks(geo, fast, place_ref[0], extra[N_CUTS], chunk_targets(staged, fast), extra[N_CUT_SEMS])
        back_mlp(
            geo, chunks, *late, staged.held[N_GRAD], staged.held[N_REST], extra[N_FLAT], base, extra[N_NORMED], staged.put
        )
        chunks.close()

    scratch = {N_FLAT: pltpu.VMEM((ROW_END - base + CHUNK_PAD, LANES), F32)} | chunk_scratch(geo, tokens)
    return staged_call(kernel, place, operands, results, scratch, 6 * 10**9, unheld=(N_KEEP, N_SEND))


def both_back_attn(geo, fast, layer, seqs, place, grad, found, emb_t, rest, chars_row):
    names = (N_GRAD_IN, N_W_OUT, N_O, N_QKV, N_PROB, N_A, N_W_QKV, N_X, N_VECTORS, N_EMB_T, N_REST)
    given = {N_GRAD_IN: grad, N_EMB_T: emb_t, N_REST: rest}
    operands = {name: given[name] if name in given else found[name] for name in names}
    tokens = grad.shape[0]
    results = {} if layer == 0 else {N_GRAD: like(F32, tokens, D)}
    results = results | chunk_results(geo, fast)
    scratch = {
        N_FLAT: pltpu.VMEM((ROW_GAIN_TWO + rest.shape[0], LANES), F32),
        N_QKV_GRAD: pltpu.VMEM((tokens, 3 * D), BF16),
        N_HEADS_GRAD: pltpu.VMEM((tokens, D), BF16),
    } | chunk_scratch(geo, tokens)
    if layer == 0:
        scratch[N_TOTAL] = pltpu.VMEM((tokens, D), F32)
        operands[N_CHARS] = chars_row
        scratch[N_TABLE] = pltpu.VMEM((4 * 32, LANES), F32)
        if not fast:
            results[N_TABLE_OUT] = like(F32, geo.devices, 8, LANES)

    def kernel(place_ref, _, staged, extra, sems):
        late = [functools.partial(staged.get, name) for name in (N_GRAD_IN, N_X, N_A, N_QKV, N_PROB, N_O, N_W_QKV, N_W_OUT)]
        tail = [functools.partial(staged.get, name) for name in (N_VECTORS, N_EMB_T, N_REST)]
        chunks = Chunks(geo, fast, place_ref[0], extra[N_CUTS], chunk_targets(staged, fast), extra[N_CUT_SEMS])

        def done(name):
            if name in results:
                staged.put(name)

        back_attn(
            geo, seqs, chunks, extra.get(N_TABLE), staged.held.get(N_TABLE_OUT), *late, *tail,
            extra[N_TOTAL] if layer == 0 else staged.held[N_GRAD], extra[N_FLAT], extra[N_QKV_GRAD], extra[N_HEADS_GRAD],
            extra[N_NORMED], functools.partial(staged.get, N_CHARS), done,
        )
        done(N_TABLE_OUT)
        chunks.close()

    return staged_call(kernel, place, operands, results, scratch, 6 * 10**9, unheld=(N_KEEP, N_SEND))


def permute(value, distance, devices):
    return lax.ppermute(value, AXES, [(d, d ^ distance) for d in range(devices)])


Z1, Z2, Z3, X, Y, CORE = 8, 16, 24, 4, 2, 1


def after(value, *others):
    return lax.optimization_barrier((value, *others))[0]


def sync(*values):
    return lax.optimization_barrier(values)


def gather_both(geo, first, second):
    n, rows = geo.devices, geo.rows
    half = ceil_to(rows // 2, 16)

    def sides(held):
        return permute(held, X, n), permute(held, Y, n)

    def corners(over_x, over_y):
        return permute(over_x[:half], Y, n), permute(over_y[half:], X, n)

    def other(*arrays):
        return permute(jnp.concatenate(arrays, 0), CORE, n)

    near, over = permute(first, Z1, n), permute(first, Z2, n)
    sides_0 = sides(first)
    sides_0 = sync(*sides_0)
    corners_0 = corners(*sides_0)
    near, _ = sync(near, sides_0[0])
    sides_1 = sides(near)
    over, _ = sync(over, near)
    far = permute(over, Z1, n)
    sides_2 = sides(over)
    *sides_1, _ = sync(*sides_1, over)
    corners_1 = corners(*sides_1)
    far, *corners_0 = sync(far, *corners_0, sides_1[0])[:3]
    sides_3 = sides(far)
    other_0 = other(first, *sides_0, *corners_0)
    second, _ = sync(second, far)
    near_b, over_b = permute(second, Z1, n), permute(second, Z2, n)
    *sides_2, _ = sync(*sides_2, far)
    corners_2 = corners(*sides_2)
    *corners_1, _ = sync(*corners_1, sides_2[0])
    other_1 = other(near, *sides_1, *corners_1)
    *sides_3, _ = sync(*sides_3, sides_2[0])
    corners_3 = corners(*sides_3)
    over_b, near_b, _ = sync(over_b, near_b, sides_3[0])
    far_b = permute(over_b, Z1, n)
    *corners_2, _ = sync(*corners_2, sides_3[0])
    other_2 = other(over, *sides_2, *corners_2)
    *corners_3, far_b, _ = sync(*corners_3, far_b, corners_2[0])
    other_3 = other(far, *sides_3, *corners_3)
    column = jnp.concatenate([second, near_b, over_b, far_b], 0)
    found = []
    for z, arrays, packed in (
        (0, (first, *sides_0, *corners_0), other_0),
        (Z1, (near, *sides_1, *corners_1), other_1),
        (Z2, (over, *sides_2, *corners_2), other_2),
        (Z3, (far, *sides_3, *corners_3), other_3),
    ):
        pieces = [
            (0, z, None, 0, rows),
            (rows, z + X, None, 0, rows),
            (2 * rows, z + Y, None, 0, rows),
            (3 * rows, z + X + Y, None, 0, half),
            (3 * rows + half, z + X + Y, None, half, rows - half),
        ]
        for array, (_, relative, _, at, count) in zip(arrays, pieces):
            found.append((array, [(0, relative, None, at, count)]))
        found.append((packed, [(src, rel + CORE, None, at, count) for src, rel, _, at, count in pieces]))
    return found, column


def gather_sides(geo, column):
    return permute(column, X, geo.devices), permute(column, Y, geo.devices)


def gather_corners(geo, over_x, over_y):
    n, rows = geo.devices, geo.rows
    half = ceil_to(rows // 2, 16)
    cut_x = over_x.reshape(4, rows, LANES)[:, :half].reshape(-1, LANES)
    cut_y = over_y.reshape(4, rows, LANES)[:, half:].reshape(-1, LANES)
    return permute(cut_x, Y, n), permute(cut_y, X, n)


def gathered_pieces(geo, arrays, others):
    rows = geo.rows
    half = ceil_to(rows // 2, 16)
    found = []
    for core, group in ((0, arrays), (CORE, others)):
        for array, (relative, at, count) in zip(
            group, ((0, 0, rows), (X, 0, rows), (Y, 0, rows), (X + Y, 0, half), (X + Y, half, rows - half))
        ):
            found.append((array, [(z * count, relative + core + 8 * z, None, at, count) for z in range(4)]))
    return found


def gather_any(geo, chunk):
    gathered = lax.all_gather(chunk, AXES, axis=0)
    return [(gathered, [(0, 0, 0, 0, 0)])]


def add(*values):
    total = values[0].astype(F32)
    for value in values[1:]:
        total = total + value.astype(F32)
    return total


def plane_start(geo, keep, came):
    shape = (2, 2, 2, geo.rows, LANES)
    half = ceil_to(geo.rows // 2, 16)
    keep, came = keep.reshape(shape), came.reshape(shape)
    one = (keep[:, :, :, :half], came[:, :, :, :half])
    two = (keep[:, :, :, half:], came[:, :, :, half:])
    to_x = add(*(part[1] for part in one)).astype(BF16)
    to_y = add(*(part[:, 1] for part in two)).astype(BF16)
    return [part[0] for part in one], [part[:, 0] for part in two], to_x, to_y


def plane_next(one, two, from_x, from_y):
    one, two = one + [from_x], two + [from_y]
    to_y = add(*(part[1] for part in one)).astype(BF16)
    to_x = add(*(part[1] for part in two)).astype(BF16)
    return [part[0] for part in one], [part[0] for part in two], to_y, to_x


def plane_end(one, two, from_y, from_x):
    return jnp.concatenate([add(*one, from_y), add(*two, from_x)], 1)


def column_sum(geo, place, upper, lower, table):
    n = geo.devices
    if table:
        row = lax.broadcasted_iota(jnp.int32, (1, geo.rows, 1), 1)
        upper = jnp.where(row < geo.param_rows, upper, lower)
    is_upper = place[3] >= 2
    near = jnp.where(is_upper, upper, lower)
    far = jnp.where(is_upper, lower, upper).astype(BF16)
    return [near[0], permute(near[1].astype(BF16), Z1, n), permute(far[0], Z2, n), permute(far[1], Z3, n)]


def sum_any(chunks):
    return lax.psum_scatter(chunks.astype(F32), AXES, scatter_dimension=0, tiled=True)[0]


def timestep_embed(step_ids):
    half_dim = TD // 2
    freq_base = jnp.exp(jnp.arange(half_dim, dtype=F32) * (-math.log(10000.0) / half_dim))
    angle_grid = step_ids.astype(F32)[:, None] * freq_base[None, :]
    return jnp.concatenate([jnp.sin(angle_grid), jnp.cos(angle_grid)], axis=1)


def body(fast, chars, steps, embed, layer_params, cotangent):
    seqs, length = chars.shape
    tokens = seqs * length
    geo = Geometry(lax.axis_size(AXES), layer_params.shape[1], embed.shape[0])
    index = lax.axis_index(AXES).astype(jnp.int32)
    place = jnp.stack(
        [index, index * geo.shard % LANES, index * geo.embed_shard % LANES, index // 8]
    ).astype(jnp.int32)
    chunks = pack_shards(geo, place, layer_params, embed)
    emb = timestep_embed(steps).astype(BF16)
    emb_rows = jnp.concatenate([emb, jnp.zeros((8 - seqs, TD), BF16)], 0) if seqs < 8 else emb
    emb_t = emb.astype(F32).T
    chars_row, chars_col = chars.reshape(1, tokens), chars.reshape(tokens, 1)
    n = geo.devices

    cotangent = cotangent.reshape(tokens, D)
    if not fast:
        first = first_ahead(geo, seqs, place, gather_any(geo, chunks[0]), chars_col, emb_rows)
        first = first_ahead_rest(place, first)
        second = second_both(geo, fast, seqs, place, gather_any(geo, chunks[1]), first[N_STREAM], emb_rows, cotangent)
        low_second = both_back_attn(geo, fast, 1, seqs, place, second[N_GRAD], second, emb_t, second[N_REST], chars_row)
        up_first = first_back_mlp(geo, fast, place, low_second[N_GRAD], first)
        low_first = both_back_attn(geo, fast, 0, seqs, place, up_first[N_GRAD], first, emb_t, up_first[N_REST], chars_row)
        sums = [
            sum_any(jnp.concatenate([low_first[N_KEEP], up_first[N_KEEP]], 0)),
            sum_any(jnp.concatenate([low_second[N_KEEP], second[N_KEEP]], 0)),
            sum_any(low_first[N_TABLE_OUT]),
        ]
        grad_params, grad_embed = finish(geo, fast, place, sums)
        return (second[N_OUTPUT].reshape(seqs, length, D), grad_embed, grad_params)

    gathered, column = gather_both(geo, *chunks)
    sides = gather_sides(geo, column)
    column_other = permute(column, CORE, n)
    first = first_ahead(geo, seqs, place, gathered, chars_col, emb_rows)
    first, sides, column_other = sync(first, sides, column_other)
    corners = gather_corners(geo, *sides)
    sides_other = [permute(side, CORE, n) for side in sides]
    first = first_ahead_rest(place, first)
    first, corners, sides_other = sync(first, corners, sides_other)
    corners_other = [permute(corner, CORE, n) for corner in corners]
    pieces = gathered_pieces(geo, [column, *sides, *corners], [column_other, *sides_other, *corners_other])
    second = second_both(geo, fast, seqs, place, pieces, first[N_STREAM], emb_rows, cotangent)
    output = second[N_OUTPUT].reshape(seqs, length, D)

    def cross(to_one, to_two, one, two):
        return permute(to_one, one, n), permute(to_two, two, n)

    def attn(layer, grad, found, rest):
        got = both_back_attn(geo, fast, layer, seqs, place, grad, found, emb_t, rest, chars_row)
        return (got[N_KEEP], got[N_SEND]) if layer == 0 else (got[N_GRAD], got[N_KEEP], got[N_SEND])

    grad, rest, keep_u, send_u = (second[name] for name in (N_GRAD, N_REST, N_KEEP, N_SEND))
    came_u = permute(send_u, CORE, n)
    grad, keep_l, send_l = attn(1, grad, second, rest)
    grad, keep_u, came_u, keep_l, send_l = sync(grad, keep_u, came_u, keep_l, send_l)
    came_l = permute(send_l, CORE, n)
    one_u, two_u, to_x, to_y = plane_start(geo, keep_u, came_u)
    from_u = cross(to_x, to_y, X, Y)

    got = first_back_mlp(geo, fast, place, after(grad, to_x, to_y), first)
    grad, rest, keep, send = (got[name] for name in (N_GRAD, N_REST, N_KEEP, N_SEND))
    grad, rest, keep, send, came_l, from_u = sync(grad, rest, keep, send, came_l, from_u)
    came = permute(send, CORE, n)
    one_u, two_u, to_y, to_x = plane_next(one_u, two_u, *from_u)
    from_u = cross(to_y, to_x, Y, X)
    one_l, two_l, to_x_l, to_y_l = plane_start(geo, keep_l, came_l)
    from_l = cross(to_x_l, to_y_l, X, Y)

    grad = after(grad, to_x, to_y, to_x_l, to_y_l)
    low_keep, low_send = attn(0, grad, first, rest)
    low_keep, low_send, keep, came, from_u, from_l = sync(low_keep, low_send, keep, came, from_u, from_l)
    low_came = permute(low_send, CORE, n)
    one_l, two_l, to_y, to_x = plane_next(one_l, two_l, *from_l)
    from_l = cross(to_y, to_x, Y, X)
    one, two, to_x, to_y = plane_start(geo, keep, came)
    from_up = cross(to_x, to_y, X, Y)
    upper = plane_end(one_u, two_u, *from_u)

    low_came, low_keep, upper, _, _ = sync(low_came, low_keep, upper, to_x, to_y)
    low_one, low_two, to_x, to_y = plane_start(geo, low_keep, low_came)
    from_low = cross(to_x, to_y, X, Y)

    from_l, from_up, _, _ = sync(from_l, from_up, to_x, to_y)
    lower = plane_end(one_l, two_l, *from_l)
    seconds = column_sum(geo, place, upper, lower, False)
    one, two, to_y, to_x = plane_next(one, two, *from_up)
    from_up = cross(to_y, to_x, Y, X)

    from_low, _, _ = sync(from_low, to_y, to_x)
    low_one, low_two, to_y, to_x = plane_next(low_one, low_two, *from_low)
    from_low = cross(to_y, to_x, Y, X)

    from_low, from_up = sync(from_low, from_up)
    upper, lower = plane_end(one, two, *from_up), plane_end(low_one, low_two, *from_low)
    firsts = column_sum(geo, place, upper, lower, True)
    grad_params, grad_embed = finish(geo, fast, place, firsts + seconds)
    return (output, grad_embed, grad_params)


def solution(mesh):
    both = P(AXES)
    fast = dict(mesh.shape) == {"dp": 8, "fsdp": 4}
    return jax.shard_map(
        functools.partial(body, fast),
        mesh=mesh,
        in_specs=(P(AXES, None), both, both, P(None, AXES), P(AXES, None, None)),
        out_specs=(P(AXES, None, None), both, P(None, AXES)),
        check_vma=False,
    )
```

```python
import functools
import math

import jax
import jax.numpy as jnp
from jax import lax
from jax.experimental import pallas as pl
from jax.experimental.pallas import tpu as pltpu
from jax.sharding import PartitionSpec as P

D = 512
HEADS = 8
FF = 2048
VOCAB = 27
TD = 128
HD = 64
LANES = 128
EPSILON = 1e-05
AXES = ("dp", "fsdp")
F32 = jnp.float32
BF16 = jnp.bfloat16
VMEM_BYTES = 52 * 2**20

(
    N_CHARS, N_EMB, N_W_TIME, N_W_QKV, N_W_OUT, N_W_UP, N_W_DOWN,
    N_VECTORS, N_TABLE, N_X, N_A, N_QKV, N_PROB, N_O,
    N_X2, N_A2, N_GL, N_SLOPE, N_STREAM, N_OUTPUT, N_COTANGENT,
    N_GRAD, N_GRAD_IN, N_REST, N_KEEP, N_SEND, N_TABLE_OUT, N_EMB_T,
    N_CHUNKS, N_FLAT, N_FLAT_TABLE, N_CUTS, N_CUT_SEMS, N_NORMED, N_TOTAL,
    N_QKV_GRAD, N_HEADS_GRAD,
) = range(37)

ROW_GAIN_ONE, ROW_BIAS_ONE, ROW_W_TIME, ROW_B_TIME = 0, 4, 8, 520
ROW_QKV, ROW_OUT, ROW_GAIN_TWO, ROW_BIAS_TWO = 524, 6668, 8716, 8720
ROW_UP, ROW_B_UP, ROW_DOWN, ROW_B_DOWN, ROW_END = 8724, 16916, 16932, 25124, 25128
CHUNK_PAD = 832


def ceil_to(value, step):
    return -(-value // step) * step


class Geometry:
    def __init__(self, devices, shard, embed_shard):
        self.devices, self.shard, self.embed_shard = devices, shard, embed_shard
        self.param_rows = max(self.count(d, shard) for d in range(devices))
        self.embed_rows = max(self.count(d, embed_shard) for d in range(devices))
        self.embed_at = ceil_to(self.param_rows, 8)
        self.rows = ceil_to(max(self.embed_at + 8, self.param_rows + 2 * self.embed_rows), 16)

    @staticmethod
    def first(d, size):
        return d * size // LANES

    @staticmethod
    def count(d, size):
        return -(-(d + 1) * size // LANES) - d * size // LANES


def params(flops, nbytes, weight=0):
    flops, nbytes = max(flops * weight, 1000), max(nbytes * weight, 1000)
    return dict(
        compiler_params=pltpu.CompilerParams(vmem_limit_bytes=VMEM_BYTES),
        cost_estimate=pl.CostEstimate(flops=flops, bytes_accessed=nbytes, transcendentals=0),
    )


VM = pl.BlockSpec(memory_space=pltpu.VMEM)
SM = pl.BlockSpec(memory_space=pltpu.SMEM)
HBM = pl.BlockSpec(memory_space=pltpu.HBM)


def nn(left, right):
    return lax.dot_general(left, right, (((1,), (0,)), ((), ())), preferred_element_type=F32)


def nt(left, right):
    return lax.dot_general(left, right, (((1,), (1,)), ((), ())), preferred_element_type=F32)


def tn(left, right):
    return nn(left.T, right)


def shift_in(flat, offset):
    rolled = pltpu.roll(flat, offset, 1)
    above = jnp.concatenate([jnp.zeros((1, LANES), F32), rolled[:-1]], 0)
    lane = lax.broadcasted_iota(jnp.int32, flat.shape, 1)
    return jnp.where(lane >= offset, rolled, above)


def shift_out(flat, offset):
    rolled = pltpu.roll(flat, lax.rem(LANES - offset, LANES), 1)
    below = jnp.concatenate([rolled[1:], jnp.zeros((1, LANES), F32)], 0)
    lane = lax.broadcasted_iota(jnp.int32, flat.shape, 1)
    return jnp.where(lane < LANES - offset, rolled, below)


def pack_kernel(geo, place_ref, layers_ref, embed_ref, first_ref, second_ref):
    main = geo.embed_at
    for layer, out_ref in ((0, first_ref), (1, second_ref)):
        moved = shift_in(layers_ref[layer].astype(F32), place_ref[1])
        if layer == 0:
            tail = shift_in(embed_ref[...].astype(F32), place_ref[2])
            parts = [moved[:main], tail] + ([moved[main + 8 :]] if geo.rows > main + 8 else [])
            moved = jnp.concatenate(parts, 0)
        out_ref[...] = moved.astype(BF16)


def pack_shards(geo, place, layer_params, embed):
    layers = jnp.pad(layer_params, ((0, 0), (0, geo.rows * LANES - geo.shard)))
    table = jnp.pad(embed, (0, 8 * LANES - geo.embed_shard))
    out = jax.ShapeDtypeStruct((geo.rows, LANES), BF16)
    return pl.pallas_call(
        functools.partial(pack_kernel, geo),
        out_shape=(out, out),
        in_specs=[SM, VM, VM],
        out_specs=(VM, VM),
        **params(10**6, geo.rows * 1024),
    )(place, layers.reshape(2, geo.rows, LANES), table.reshape(8, LANES))


def finish_kernel(geo, fast, place_ref, *refs):
    grads_ref, embed_ref, moved = refs[-3:]
    parts = refs[:-3]
    count = 4 if fast else 1
    for layer in range(2):
        total = parts[layer * count][...].astype(F32)
        for part in parts[layer * count + 1 : (layer + 1) * count]:
            total = total + part[...].astype(F32)
        moved[pl.ds(layer * geo.rows, geo.rows), :] = shift_out(total, place_ref[1])
        if fast and layer == 0:
            first, size = geo.param_rows, geo.embed_rows
            lower, upper = total[first : first + size], total[first + size : first + 2 * size]
            tail = jnp.where(place_ref[3] >= 2, upper, lower)
            tail = jnp.concatenate([tail, jnp.zeros((8 - size, LANES), F32)], 0)
    if not fast:
        tail = parts[2][...]
    embed_ref[...] = shift_out(tail, place_ref[2])
    for r in range(ceil_to(geo.shard, LANES) // LANES):
        size = min(LANES, geo.shard - r * LANES)
        grads_ref[:, r * LANES : r * LANES + size] = moved[pl.ds(r, 2, stride=geo.rows), :][:, :size]


def finish(geo, fast, place, operands):
    grads, table = pl.pallas_call(
        functools.partial(finish_kernel, geo, fast),
        out_shape=(
            jax.ShapeDtypeStruct((2, geo.shard), F32),
            jax.ShapeDtypeStruct((8, LANES), F32),
        ),
        in_specs=[SM] + [VM] * len(operands),
        out_specs=(VM, VM),
        scratch_shapes=[pltpu.VMEM((2 * geo.rows, LANES), F32)],
        **params(10**6, geo.rows * 4096),
    )(place, *operands)
    return grads, table.reshape(-1)[: geo.embed_shard]


PARTS = {N_W_UP: (1, 4), N_W_DOWN: (0, 4), N_GL: (1, 4), N_SLOPE: (1, 4), N_PROB: (0, 2), N_QKV: (0, 2)}


def parts_of(name, parted):
    return range(PARTS[name][1]) if name in parted else range(1)


def part_of(ref, name, part, parted):
    if name not in parted:
        return ref
    dim, count = PARTS[name]
    size = ref.shape[dim] // count
    index = [slice(None)] * len(ref.shape)
    index[dim] = pl.ds(part * size, size)
    return ref.at[tuple(index)]


class Staged:
    def __init__(self, sources, targets, held, sems, parted):
        self.held, self.pending, self.sent, self.parted = held, {}, [], parted
        self.targets, self.sems = targets, sems
        order = sorted((part, place, name) for place, name in enumerate(sources) for part in parts_of(name, parted))
        for part, _, name in order:
            copy = pltpu.make_async_copy(
                part_of(sources[name], name, part, parted), part_of(held[name], name, part, parted), sems.at[len(self.pending)]
            )
            copy.start()
            self.pending[name, part] = copy
        self.used = len(order)

    def get(self, name, part=None):
        for one in parts_of(name, self.parted) if part is None or name not in self.parted else [part]:
            if (name, one) in self.pending:
                self.pending.pop((name, one)).wait()
        return self.held[name]

    def put(self, name, part=None):
        for one in parts_of(name, self.parted) if part is None else [part]:
            copy = pltpu.make_async_copy(
                part_of(self.held[name], name, one, self.parted), part_of(self.targets[name], name, one, self.parted), self.sems.at[self.used]
            )
            copy.start()
            self.used += 1
            self.sent.append(copy)

    def close(self):
        for copy in list(self.pending.values()) + self.sent:
            copy.wait()


def staged_call(kernel, place, operands, results, scratch, flops, raw=(), semaphores=0, unheld=(), parted=()):
    names, outs, temps = list(operands), list(results), list(scratch)

    held_outs = [name for name in outs if name not in unheld]

    def whole(place_ref, *refs):
        raws, refs = refs[: len(raw)], refs[len(raw) :]
        sources, refs = dict(zip(names, refs)), refs[len(names) :]
        targets, refs = dict(zip(outs, refs)), refs[len(outs) :]
        held, refs = dict(zip(names + held_outs, refs)), refs[len(names) + len(held_outs) :]
        extra, refs = dict(zip(temps, refs)), refs[len(temps) :]
        staged = Staged(sources, targets, held, refs[0], parted)
        kernel(place_ref, raws, staged, extra, refs[-1])
        staged.close()

    buffers = [pltpu.VMEM(v.shape, v.dtype) for v in (*operands.values(), *(results[name] for name in held_outs))]
    sems = [pltpu.SemaphoreType.DMA((sum(len(parts_of(name, parted)) for name in names + held_outs),))]
    if semaphores:
        sems.append(pltpu.SemaphoreType.DMA((semaphores,)))
    found = pl.pallas_call(
        whole,
        out_shape=tuple(pltpu.HBM(v.shape, v.dtype) for v in results.values()),
        in_specs=[SM] + [HBM] * (len(raw) + len(names)),
        out_specs=(HBM,) * len(outs),
        scratch_shapes=buffers + list(scratch.values()) + sems,
        **params(flops, 2 * 10**7, 1),
    )(place, *(pltpu.with_memory_space_constraint(v, pltpu.HBM) for v in (*raw, *operands.values())))
    return dict(zip(outs, found))


def like(dtype, *shape):
    return jax.ShapeDtypeStruct(shape, dtype)


def unpack(geo, layer, plan, me, chunk_refs, held, flat, flat_table, out, sems):
    copies = []
    for source, pieces in zip(chunk_refs, plan):
        for src_at, relative, absolute, dst_at, count in pieces:
            if absolute is None:
                target = held.at[lax.bitwise_xor(me, relative), pl.ds(dst_at, count)]
                origin = source.at[pl.ds(src_at, count)]
            else:
                target, origin = held, source
            copies.append(pltpu.make_async_copy(origin, target, sems.at[len(copies)]))
    for copy in copies:
        copy.start()
    for copy in copies:
        copy.wait()
    for d in range(geo.devices):
        block = held[d].astype(F32)
        start, rows = geo.first(d, geo.shard), geo.count(d, geo.shard)
        split = (d * geo.shard) % LANES != 0
        if split:
            shared = flat[pl.ds(start, 1), :] + block[:1]
        flat[pl.ds(start, rows), :] = block[:rows]
        if split:
            flat[pl.ds(start, 1), :] = shared
        if layer == 0:
            tail = block[geo.embed_at : geo.embed_at + 8]
            start, rows = geo.first(d, geo.embed_shard), geo.count(d, geo.embed_shard)
            split = (d * geo.embed_shard) % LANES != 0
            if split:
                shared = flat_table[pl.ds(start, 1), :] + tail[:1]
            flat_table[pl.ds(start, rows), :] = tail[:rows]
            if split:
                flat_table[pl.ds(start, 1), :] = shared
    vectors = out[N_VECTORS]
    for row, start, width in (
        (0, ROW_GAIN_ONE, 4),
        (1, ROW_BIAS_ONE, 4),
        (2, ROW_B_TIME, 4),
        (3, ROW_GAIN_TWO, 4),
        (4, ROW_BIAS_TWO, 4),
        (5, ROW_B_DOWN, 4),
        (6, ROW_B_UP, 16),
    ):
        for c in range(width):
            vectors[row : row + 1, c * LANES : (c + 1) * LANES] = flat[pl.ds(start + c, 1), :]
    for name, start, rows, width in (
        (N_W_TIME, ROW_W_TIME, TD, 4),
        (N_W_QKV, ROW_QKV, D, 12),
        (N_W_OUT, ROW_OUT, D, 4),
        (N_W_UP, ROW_UP, D, 16),
        (N_W_DOWN, ROW_DOWN, FF, 4),
    ):
        for c in range(width):
            out[name][:, c * LANES : (c + 1) * LANES] = flat[pl.ds(start + c, rows, stride=width), :].astype(BF16)
    if layer == 0:
        table = out[N_TABLE]
        table[...] = jnp.zeros(table.shape, BF16)
        for c in range(4):
            table[0:VOCAB, c * LANES : (c + 1) * LANES] = flat_table[pl.ds(c, VOCAB, stride=4), :].astype(BF16)


WEIGHTS = {
    N_W_QKV: like(BF16, D, 3 * D),
    N_W_OUT: like(BF16, D, D),
    N_W_UP: like(BF16, D, FF),
    N_W_DOWN: like(BF16, FF, D),
    N_VECTORS: like(F32, 8, FF),
}


def unpack_scratch(geo, layer):
    scratch = {
        N_CHUNKS: pltpu.VMEM((geo.devices, geo.rows, LANES), BF16),
        N_FLAT: pltpu.VMEM((ROW_END + CHUNK_PAD, LANES), F32),
        N_FLAT_TABLE: pltpu.VMEM((4 * 32, LANES), F32),
        N_W_TIME: pltpu.VMEM((TD, D), BF16),
    }
    if layer == 0:
        scratch[N_TABLE] = pltpu.VMEM((32, D), BF16)
    return scratch


def split_gathered(gathered):
    plan = tuple(tuple(pieces) for array, pieces in gathered)
    return [array for array, pieces in gathered], plan, sum(len(pieces) for pieces in plan)


def norm_stats(values):
    mean = jnp.mean(values, -1, keepdims=True)
    centered = values - mean
    variance = jnp.mean(centered * centered, -1, keepdims=True)
    scale = lax.rsqrt(variance + EPSILON)
    return centered * scale, scale


ROW_BLOCK = 64


def norm_ahead(values, gain, bias, out):
    for r in range(0, values.shape[0], ROW_BLOCK):
        rows = slice(r, r + ROW_BLOCK)
        unit, _ = norm_stats(values[rows, :])
        out[rows, :] = (unit * gain + bias).astype(BF16)


def norm_back(grad, values, gain, passed, out):
    grad_gain, grad_bias = jnp.zeros((8, D), F32), jnp.zeros((8, D), F32)
    for r in range(0, values.shape[0], ROW_BLOCK):
        rows = slice(r, r + ROW_BLOCK)
        unit, scale = norm_stats(values[rows, :])
        block = grad[rows, :]
        grad_gain = grad_gain + jnp.sum((block * unit).reshape(-1, 8, D), 0)
        grad_bias = grad_bias + jnp.sum(block.reshape(-1, 8, D), 0)
        inner = block * gain
        shifted = inner - jnp.mean(inner, -1, keepdims=True)
        back = scale * (shifted - unit * jnp.mean(inner * unit, -1, keepdims=True))
        out[rows, :] = passed[rows, :].astype(F32) + back
    return jnp.sum(grad_gain, 0, keepdims=True), jnp.sum(grad_bias, 0, keepdims=True)


def gelu_both(u):
    root = math.sqrt(2.0 / math.pi)
    square = u * u
    t = jnp.tanh(root * (u + 0.044715 * (square * u)))
    half = 0.5 * (1.0 + t)
    slope = half + 0.5 * u * (1.0 - t * t) * (root * (1.0 + 3.0 * 0.044715 * square))
    return u * half, slope


def head_masks(shape, scale):
    lane = lax.broadcasted_iota(jnp.int32, shape, 1)
    one = jnp.where(lane < HD, scale, 0.0).astype(BF16)
    two = jnp.where(lane < HD, 0.0, scale).astype(BF16)
    return one, two


def ahead_attn(seqs, stream, emb, w_time, w_qkv, w_out, vectors, x, a, qkv, prob, o, x2, a2, done):
    tokens = x.shape[0]
    length = tokens // seqs
    time_vec = nn(emb[...], w_time[...]) + vectors[2:3, :D]
    for s in range(seqs):
        x[s * length : (s + 1) * length, :] = stream[s * length : (s + 1) * length] + time_vec[s : s + 1]
    done(N_X)
    norm_ahead(x, vectors[0:1, :D], vectors[1:2, :D], a)
    done(N_A)
    for c in range(3):
        part = slice(c * D, (c + 1) * D)
        qkv[:, part] = nn(a[...], w_qkv[:, part]).astype(BF16)
    done(N_QKV)
    masks = head_masks((length, LANES), 1.0 / math.sqrt(HD))
    heads = [(s, pair, h) for s in range(seqs) for pair in range(HEADS // 2) for h in range(2)]

    def cut(s, pair, c):
        return qkv[s * length : (s + 1) * length, c * D + pair * LANES : c * D + (pair + 1) * LANES]

    def scores_of(s, pair, h):
        return nt(cut(s, pair, 1) * masks[h], cut(s, pair, 0))

    ahead = [scores_of(*heads[i]) for i in range(4)]
    mixed = []
    for i, (s, pair, h) in enumerate(heads):
        scores = ahead.pop(0)
        if i + 4 < len(heads):
            ahead.append(scores_of(*heads[i + 4]))
        top = jnp.max(scores, 0, keepdims=True)
        expd = jnp.exp(scores - top)
        low = (expd * (1.0 / jnp.sum(expd, 0, keepdims=True))).astype(BF16)
        prob[s * HEADS + 2 * pair + h] = low
        v_t = cut(s, pair, 2).T
        mixed.append(nn(v_t[h * HD : (h + 1) * HD], low))
        if h == 1:
            rows = slice(s * length, (s + 1) * length)
            o[rows, pair * LANES : (pair + 1) * LANES] = jnp.concatenate(mixed, 0).T.astype(BF16)
            mixed = []
    done(N_PROB)
    done(N_O)
    x2[...] = x[...] + nn(o[...], w_out[...])
    done(N_X2)
    norm_ahead(x2, vectors[3:4, :D], vectors[4:5, :D], a2)
    done(N_A2)


def ahead_mlp(x2, a2, w_up, w_down, vectors, gl, slope, done):
    parts = [slice(c * D, (c + 1) * D) for c in range(FF // D)]

    def up(c):
        return nn(a2()[...], w_up(c)[:, parts[c]])

    total, u = None, up(0)
    for c, part in enumerate(parts):
        value, rate = gelu_both(u + vectors()[6:7, part])
        low = value.astype(BF16)
        gl[:, part] = low
        slope[:, part] = rate.astype(BF16)
        done(N_GL, c)
        done(N_SLOPE, c)
        if c + 1 < len(parts):
            u = up(c + 1)
        step = nn(low, w_down(c)[part, :])
        total = step if total is None else total + step
    return x2()[...] + vectors()[5:6, :D] + total


class Chunks:
    def __init__(self, geo, fast, me, held, targets, sems):
        self.geo, self.fast, self.me, self.held, self.targets, self.sems = geo, fast, me, held, targets, sems
        self.copies = []

    def cut(self, d, flat, base, table=None):
        geo, slot = self.geo, d % (self.geo.devices // 2)
        block = flat[pl.ds(geo.first(d, geo.shard) - base, geo.rows), :]
        if table is not None:
            first, size = geo.param_rows, geo.embed_rows
            tails = [
                table[pl.ds(geo.first(e, geo.embed_shard), size), :] for e in (d, d + geo.devices // 2)
            ]
            block = jnp.concatenate([block[:first], *tails, block[first + 2 * size :]], 0)
        self.held[slot] = block.astype(BF16)
        source, sem = self.held.at[slot], self.sems.at[slot]
        if not self.fast:
            self.copies.append(pltpu.make_async_copy(source, self.targets[0].at[slot], sem))
            self.copies[-1].start()
            return
        relative = lax.bitwise_xor(self.me, d)
        row = lax.bitwise_and(relative, 4) + lax.bitwise_and(relative, 2)
        row = row + lax.bitwise_and(lax.shift_right_logical(relative, 3), 1)
        keep, send = (pltpu.make_async_copy(source, target.at[row], sem) for target in self.targets)
        core = lax.bitwise_and(relative, 1)

        @pl.when(core == 0)
        def _():
            keep.start()

        @pl.when(core == 1)
        def _():
            send.start()

        self.copies.append(keep)

    def close(self):
        for copy in self.copies:
            copy.wait()


def back_mlp(geo, chunks, grad_in, x2, a2, gl, slope, w_up, w_down, vectors, grad, rest, flat, base, normed, done):
    grad_low = grad_in()[...].astype(BF16)
    flat[pl.ds(ROW_END - base, CHUNK_PAD), :] = jnp.zeros((CHUNK_PAD, LANES), F32)
    grad_bias = jnp.sum(grad_low.astype(F32), 0, keepdims=True)
    for c in range(4):
        flat[pl.ds(ROW_B_DOWN - base + c, 1), :] = grad_bias[:, c * LANES : (c + 1) * LANES]
    parts = [slice(j * D, (j + 1) * D) for j in range(FF // D)]

    def hidden_grad(j):
        return nt(grad_low, w_down(j)[parts[j], :])

    total, hidden = None, hidden_grad(0)
    for j, part in enumerate(parts):
        up_grad = (hidden * slope(j)[:, part].astype(F32)).astype(BF16)
        bias_grad = jnp.sum(up_grad.astype(F32), 0, keepdims=True)
        if j + 1 < len(parts):
            hidden = hidden_grad(j + 1)
        down = tn(gl(j)[:, part], grad_low)
        for c in range(4):
            cols = slice(c * LANES, (c + 1) * LANES)
            flat[pl.ds(ROW_B_UP - base + 4 * j + c, 1), :] = bias_grad[:, cols]
            flat[pl.ds(ROW_DOWN - base + 4 * D * j + c, D, stride=4), :] = down[:, cols]
        up = tn(a2()[...], up_grad)
        for c in range(4):
            cols = slice(c * LANES, (c + 1) * LANES)
            flat[pl.ds(ROW_UP - base + 4 * j + c, D, stride=16), :] = up[:, cols]
        step = nt(up_grad, w_up(j)[:, part])
        total = step if total is None else total + step
    normed[...] = total
    for d in range(geo.devices // 2, geo.devices):
        chunks.cut(d, flat, base)
    grad_gain, grad_bias = norm_back(normed, x2(), vectors()[3:4, :D], grad_in(), grad)
    done(N_GRAD)
    for c in range(4):
        cols = slice(c * LANES, (c + 1) * LANES)
        flat[pl.ds(ROW_GAIN_TWO - base + c, 1), :] = grad_gain[:, cols]
        flat[pl.ds(ROW_BIAS_TWO - base + c, 1), :] = grad_bias[:, cols]
    rest[...] = flat[pl.ds(ROW_GAIN_TWO - base, rest.shape[0]), :].astype(BF16)
    done(N_REST)


def back_attn(
    geo, seqs, chunks, table, embed_outs, grad_in, x, a, qkv, prob, o, w_qkv, w_out, vectors, emb_t, rest, total,
    flat, qkv_grad, heads_grad, normed, chars, done,
):
    tokens = normed.shape[0]
    length = tokens // seqs
    grad_low = grad_in()[...].astype(BF16)
    heads_grad[...] = nt(grad_low, w_out()[...]).astype(BF16)
    out_grad = tn(o()[...], grad_low)
    for c in range(4):
        flat[pl.ds(ROW_OUT + c, D, stride=4), :] = out_grad[:, c * LANES : (c + 1) * LANES]
    masks = head_masks((length, LANES), 1.0)
    scale = 1.0 / math.sqrt(HD)
    lane = lax.broadcasted_iota(jnp.int32, (length, LANES), 1)
    qkv, prob = qkv(), prob()
    heads = [(s, pair, h) for s in range(seqs) for pair in range(HEADS // 2) for h in range(2)]

    def cut(s, pair, c):
        return qkv[s * length : (s + 1) * length, c * D + pair * LANES : c * D + (pair + 1) * LANES]

    def go_of(s, pair):
        return heads_grad[s * length : (s + 1) * length, pair * LANES : (pair + 1) * LANES]

    def prob_grad_of(s, pair, h):
        return nt(cut(s, pair, 2) * masks[h], go_of(s, pair))

    ahead = [prob_grad_of(*heads[i]) for i in range(4)]
    to_q, to_k, to_v = [], [], []
    for i, (s, pair, h) in enumerate(heads):
        prob_grad = ahead.pop(0)
        if i + 4 < len(heads):
            ahead.append(prob_grad_of(*heads[i + 4]))
        prob_low = prob[s * HEADS + 2 * pair + h]
        prob_full = prob_low.astype(F32)
        weighted = prob_full * prob_grad
        row_dot = jnp.sum(weighted, 0, keepdims=True)
        score_grad = (weighted - prob_full * row_dot).astype(BF16)
        to_v.append(nn(prob_low, go_of(s, pair)))
        k_t = cut(s, pair, 1).T
        to_q.append(nn(k_t[h * HD : (h + 1) * HD], score_grad))
        to_k.append(nn(score_grad, cut(s, pair, 0)))
        if h == 1:
            rows = slice(s * length, (s + 1) * length)
            cols = [slice(c * D + pair * LANES, c * D + (pair + 1) * LANES) for c in range(3)]
            qkv_grad[rows, cols[0]] = (jnp.concatenate(to_q, 0).T * scale).astype(BF16)
            qkv_grad[rows, cols[1]] = (jnp.where(lane < HD, to_k[0], to_k[1]) * scale).astype(BF16)
            qkv_grad[rows, cols[2]] = jnp.where(lane < HD, to_v[0], to_v[1]).astype(BF16)
            to_q, to_k, to_v = [], [], []
    a_t, steps = a()[...].T, None
    for part in range(3):
        cols = slice(part * D, (part + 1) * D)
        piece = nn(a_t, qkv_grad[:, cols])
        for c in range(4):
            flat[pl.ds(ROW_QKV + 4 * part + c, D, stride=12), :] = piece[:, c * LANES : (c + 1) * LANES]
        step = nt(qkv_grad[:, cols], w_qkv()[:, cols])
        steps = step if steps is None else steps + step
    normed[...] = steps
    flat[pl.ds(ROW_GAIN_TWO, rest().shape[0]), :] = rest()[...].astype(F32)
    middle = geo.devices // 2
    early = [d for d in range(middle) if geo.first(d, geo.shard) >= ROW_QKV] if table is None else []
    for d in early:
        chunks.cut(d, flat, 0)
    grad_gain, grad_bias = norm_back(normed, x(), vectors()[0:1, :D], grad_in(), total)
    done(N_GRAD)
    time_grad = [
        jnp.sum(total[s * length : (s + 1) * length, :], 0, keepdims=True).astype(BF16).astype(F32) for s in range(seqs)
    ]
    bias_grad = sum(time_grad[1:], time_grad[0])
    weight_grad = sum(emb_t()[:, s : s + 1] * time_grad[s] for s in range(seqs))
    for c in range(4):
        cols = slice(c * LANES, (c + 1) * LANES)
        flat[pl.ds(ROW_GAIN_ONE + c, 1), :] = grad_gain[:, cols]
        flat[pl.ds(ROW_BIAS_ONE + c, 1), :] = grad_bias[:, cols]
        flat[pl.ds(ROW_B_TIME + c, 1), :] = bias_grad[:, cols]
        flat[pl.ds(ROW_W_TIME + c, TD, stride=4), :] = weight_grad[:, cols]
    if table is not None:
        kind = lax.broadcasted_iota(jnp.int32, (32, tokens), 0)
        table_grad = nn((chars()[...] == kind).astype(BF16), total[...].astype(BF16))
        for c in range(4):
            table[pl.ds(c, 32, stride=4), :] = table_grad[:, c * LANES : (c + 1) * LANES]
    for d in range(middle):
        if d not in early:
            chunks.cut(d, flat, 0, table if chunks.fast else None)
    if table is not None and not chunks.fast:
        for d in range(geo.devices):
            embed_outs[d] = table[pl.ds(geo.first(d, geo.embed_shard), 8), :]


def kept_shapes(seqs, tokens):
    length = tokens // seqs
    return {
        N_X: like(F32, tokens, D),
        N_A: like(BF16, tokens, D),
        N_QKV: like(BF16, tokens, 3 * D),
        N_PROB: like(BF16, seqs * HEADS, length, length),
        N_O: like(BF16, tokens, D),
    }


def rest_rows(geo):
    middle = geo.first(geo.devices // 2, geo.shard)
    return ceil_to(middle + geo.rows - ROW_GAIN_TWO, 16)


def chunk_results(geo, fast):
    if fast:
        shape = like(BF16, geo.devices // 4, geo.rows, LANES)
        return {N_KEEP: shape, N_SEND: shape}
    return {N_KEEP: like(BF16, geo.devices // 2, geo.rows, LANES)}


def chunk_targets(staged, fast):
    return [staged.targets[name] for name in ((N_KEEP, N_SEND) if fast else (N_KEEP,))]


def chunk_scratch(geo, tokens):
    return {
        N_CUTS: pltpu.VMEM((geo.devices // 2, geo.rows, LANES), BF16),
        N_CUT_SEMS: pltpu.SemaphoreType.DMA((geo.devices // 2,)),
        N_NORMED: pltpu.VMEM((tokens, D), F32),
    }


def first_ahead(geo, seqs, place, gathered, chars, emb):
    tokens = chars.shape[0]
    arrays, plan, count = split_gathered(gathered)
    results = WEIGHTS | kept_shapes(seqs, tokens) | {N_X2: like(F32, tokens, D), N_A2: like(BF16, tokens, D)}

    def kernel(place_ref, chunk_refs, staged, extra, sems):
        held = staged.held
        unpack(
            geo, 0, plan, place_ref[0], chunk_refs, extra[N_CHUNKS], extra[N_FLAT], extra[N_FLAT_TABLE], held | extra, sems
        )
        for name in WEIGHTS:
            staged.put(name)
        lane = lax.broadcasted_iota(jnp.int32, (tokens, 32), 1)
        stream = nn((staged.get(N_CHARS)[...] == lane).astype(BF16), extra[N_TABLE][...])
        weights = [extra[N_W_TIME]] + [held[name] for name in (N_W_QKV, N_W_OUT, N_VECTORS)]
        outs = [held[name] for name in (N_X, N_A, N_QKV, N_PROB, N_O, N_X2, N_A2)]
        ahead_attn(seqs, stream, staged.get(N_EMB), *weights, *outs, staged.put)

    operands = {N_CHARS: chars, N_EMB: emb}
    scratch = unpack_scratch(geo, 0)
    return staged_call(kernel, place, operands, results, scratch, 4 * 10**9, arrays, count, parted=())


def first_ahead_rest(place, found):
    names = (N_A2, N_W_UP, N_VECTORS, N_W_DOWN, N_X2)
    operands = {name: found[name] for name in names}
    tokens = found[N_X2].shape[0]
    results = {N_STREAM: like(F32, tokens, D), N_GL: like(BF16, tokens, FF), N_SLOPE: like(BF16, tokens, FF)}

    def kernel(place_ref, _, staged, extra, sems):
        late = [functools.partial(staged.get, name) for name in (N_X2, N_A2, N_W_UP, N_W_DOWN, N_VECTORS)]
        gl, slope, stream = (staged.held[name] for name in (N_GL, N_SLOPE, N_STREAM))
        stream[...] = ahead_mlp(*late, gl, slope, staged.put)
        staged.put(N_STREAM)

    return found | staged_call(kernel, place, operands, results, {}, 4 * 10**9, parted=(N_W_UP, N_W_DOWN, N_GL, N_SLOPE))


def second_both(geo, fast, seqs, place, gathered, stream, emb, cotangent):
    tokens = stream.shape[0]
    arrays, plan, count = split_gathered(gathered)
    results = {name: WEIGHTS[name] for name in (N_W_QKV, N_W_OUT, N_VECTORS)}
    results = results | kept_shapes(seqs, tokens)
    results = results | {
        N_OUTPUT: like(BF16, tokens, D),
        N_GRAD: like(F32, tokens, D),
        N_REST: like(BF16, rest_rows(geo), LANES),
    }
    results = results | chunk_results(geo, fast)
    scratch = unpack_scratch(geo, 1)
    scratch[N_W_UP], scratch[N_W_DOWN] = pltpu.VMEM((D, FF), BF16), pltpu.VMEM((FF, D), BF16)
    scratch[N_X2], scratch[N_A2] = pltpu.VMEM((tokens, D), F32), pltpu.VMEM((tokens, D), BF16)
    scratch[N_GL], scratch[N_SLOPE] = pltpu.VMEM((tokens, FF), BF16), pltpu.VMEM((tokens, FF), BF16)
    scratch = scratch | chunk_scratch(geo, tokens)

    def kernel(place_ref, chunk_arrays, staged, extra, sems):
        every = staged.held | extra
        unpack(geo, 1, plan, place_ref[0], chunk_arrays, extra[N_CHUNKS], extra[N_FLAT], extra[N_FLAT_TABLE], every, sems)
        for name in (N_W_QKV, N_W_OUT, N_VECTORS):
            staged.put(name)
        weights = [every[name] for name in (N_W_TIME, N_W_QKV, N_W_OUT, N_VECTORS)]
        outs = [every[name] for name in (N_X, N_A, N_QKV, N_PROB, N_O, N_X2, N_A2)]

        def done(name, part=None):
            if name in results:
                staged.put(name, part)

        ahead_attn(seqs, staged.get(N_STREAM)[...], staged.get(N_EMB), *weights, *outs, done)

        def ready(*names):
            return [lambda part=None, ref=every[name]: ref for name in names]

        outputs = ahead_mlp(*ready(N_X2, N_A2, N_W_UP, N_W_DOWN, N_VECTORS), every[N_GL], every[N_SLOPE], done)
        every[N_OUTPUT][...] = outputs.astype(BF16)
        done(N_OUTPUT)
        chunks = Chunks(geo, fast, place_ref[0], extra[N_CUTS], chunk_targets(staged, fast), extra[N_CUT_SEMS])
        back_mlp(
            geo, chunks, functools.partial(staged.get, N_COTANGENT),
            *ready(N_X2, N_A2, N_GL, N_SLOPE, N_W_UP, N_W_DOWN, N_VECTORS),
            every[N_GRAD], every[N_REST], extra[N_FLAT], 0, extra[N_NORMED], done,
        )
        chunks.close()

    operands = {N_STREAM: stream, N_EMB: emb, N_COTANGENT: cotangent}
    return staged_call(kernel, place, operands, results, scratch, 10**10, arrays, count, (N_KEEP, N_SEND))


def first_back_mlp(geo, fast, place, grad, found):
    names = (N_GRAD_IN, N_W_DOWN, N_SLOPE, N_GL, N_A2, N_W_UP, N_X2, N_VECTORS)
    operands = {name: grad if name == N_GRAD_IN else found[name] for name in names}
    tokens = grad.shape[0]
    results = {N_GRAD: like(F32, tokens, D), N_REST: like(BF16, rest_rows(geo), LANES)} | chunk_results(geo, fast)
    base = ROW_GAIN_TWO

    def kernel(place_ref, _, staged, extra, sems):
        late = [
            functools.partial(staged.get, name)
            for name in (N_GRAD_IN, N_X2, N_A2, N_GL, N_SLOPE, N_W_UP, N_W_DOWN, N_VECTORS)
        ]
        chunks = Chunks(geo, fast, place_ref[0], extra[N_CUTS], chunk_targets(staged, fast), extra[N_CUT_SEMS])
        back_mlp(
            geo, chunks, *late, staged.held[N_GRAD], staged.held[N_REST], extra[N_FLAT], base, extra[N_NORMED], staged.put
        )
        chunks.close()

    scratch = {N_FLAT: pltpu.VMEM((ROW_END - base + CHUNK_PAD, LANES), F32)} | chunk_scratch(geo, tokens)
    return staged_call(kernel, place, operands, results, scratch, 6 * 10**9, unheld=(N_KEEP, N_SEND))


def both_back_attn(geo, fast, layer, seqs, place, grad, found, emb_t, rest, chars_row):
    names = (N_GRAD_IN, N_W_OUT, N_O, N_QKV, N_PROB, N_A, N_W_QKV, N_X, N_VECTORS, N_EMB_T, N_REST)
    given = {N_GRAD_IN: grad, N_EMB_T: emb_t, N_REST: rest}
    operands = {name: given[name] if name in given else found[name] for name in names}
    tokens = grad.shape[0]
    results = {} if layer == 0 else {N_GRAD: like(F32, tokens, D)}
    results = results | chunk_results(geo, fast)
    scratch = {
        N_FLAT: pltpu.VMEM((ROW_GAIN_TWO + rest.shape[0], LANES), F32),
        N_QKV_GRAD: pltpu.VMEM((tokens, 3 * D), BF16),
        N_HEADS_GRAD: pltpu.VMEM((tokens, D), BF16),
    } | chunk_scratch(geo, tokens)
    if layer == 0:
        scratch[N_TOTAL] = pltpu.VMEM((tokens, D), F32)
        operands[N_CHARS] = chars_row
        scratch[N_TABLE] = pltpu.VMEM((4 * 32, LANES), F32)
        if not fast:
            results[N_TABLE_OUT] = like(F32, geo.devices, 8, LANES)

    def kernel(place_ref, _, staged, extra, sems):
        late = [functools.partial(staged.get, name) for name in (N_GRAD_IN, N_X, N_A, N_QKV, N_PROB, N_O, N_W_QKV, N_W_OUT)]
        tail = [functools.partial(staged.get, name) for name in (N_VECTORS, N_EMB_T, N_REST)]
        chunks = Chunks(geo, fast, place_ref[0], extra[N_CUTS], chunk_targets(staged, fast), extra[N_CUT_SEMS])

        def done(name, part=None):
            if name in results:
                staged.put(name, part)

        back_attn(
            geo, seqs, chunks, extra.get(N_TABLE), staged.held.get(N_TABLE_OUT), *late, *tail,
            extra[N_TOTAL] if layer == 0 else staged.held[N_GRAD], extra[N_FLAT], extra[N_QKV_GRAD], extra[N_HEADS_GRAD],
            extra[N_NORMED], functools.partial(staged.get, N_CHARS), done,
        )
        done(N_TABLE_OUT)
        chunks.close()

    return staged_call(kernel, place, operands, results, scratch, 6 * 10**9, unheld=(N_KEEP, N_SEND))


def permute(value, distance, devices):
    return lax.ppermute(value, AXES, [(d, d ^ distance) for d in range(devices)])


Z1, Z2, Z3, X, Y, CORE = 8, 16, 24, 4, 2, 1


def after(value, *others):
    return lax.optimization_barrier((value, *others))[0]


def sync(*values):
    return lax.optimization_barrier(values)


def gather_both(geo, first, second):
    n, rows = geo.devices, geo.rows
    half = ceil_to(rows // 2, 16)

    def sides(held):
        return permute(held, X, n), permute(held, Y, n)

    def corners(over_x, over_y):
        return permute(over_x[:half], Y, n), permute(over_y[half:], X, n)

    def other(*arrays):
        return permute(jnp.concatenate(arrays, 0), CORE, n)

    near, over = permute(first, Z1, n), permute(first, Z2, n)
    sides_0 = sides(first)
    sides_0 = sync(*sides_0)
    corners_0 = corners(*sides_0)
    near, _ = sync(near, sides_0[0])
    sides_1 = sides(near)
    over, _ = sync(over, near)
    far = permute(over, Z1, n)
    sides_2 = sides(over)
    *sides_1, _ = sync(*sides_1, over)
    corners_1 = corners(*sides_1)
    far, *corners_0 = sync(far, *corners_0, sides_1[0])[:3]
    sides_3 = sides(far)
    other_0 = other(first, *sides_0, *corners_0)
    second, _ = sync(second, far)
    near_b, over_b = permute(second, Z1, n), permute(second, Z2, n)
    *sides_2, _ = sync(*sides_2, far)
    corners_2 = corners(*sides_2)
    *corners_1, _ = sync(*corners_1, sides_2[0])
    other_1 = other(near, *sides_1, *corners_1)
    *sides_3, _ = sync(*sides_3, sides_2[0])
    corners_3 = corners(*sides_3)
    over_b, near_b, _ = sync(over_b, near_b, sides_3[0])
    far_b = permute(over_b, Z1, n)
    *corners_2, _ = sync(*corners_2, sides_3[0])
    other_2 = other(over, *sides_2, *corners_2)
    *corners_3, far_b, _ = sync(*corners_3, far_b, corners_2[0])
    other_3 = other(far, *sides_3, *corners_3)
    column = jnp.concatenate([second, near_b, over_b, far_b], 0)
    found = []
    for z, arrays, packed in (
        (0, (first, *sides_0, *corners_0), other_0),
        (Z1, (near, *sides_1, *corners_1), other_1),
        (Z2, (over, *sides_2, *corners_2), other_2),
        (Z3, (far, *sides_3, *corners_3), other_3),
    ):
        pieces = [
            (0, z, None, 0, rows),
            (rows, z + X, None, 0, rows),
            (2 * rows, z + Y, None, 0, rows),
            (3 * rows, z + X + Y, None, 0, half),
            (3 * rows + half, z + X + Y, None, half, rows - half),
        ]
        for array, (_, relative, _, at, count) in zip(arrays, pieces):
            found.append((array, [(0, relative, None, at, count)]))
        found.append((packed, [(src, rel + CORE, None, at, count) for src, rel, _, at, count in pieces]))
    return found, column


def gather_sides(geo, column):
    return permute(column, X, geo.devices), permute(column, Y, geo.devices)


def gather_corners(geo, over_x, over_y):
    n, rows = geo.devices, geo.rows
    half = ceil_to(rows // 2, 16)
    cut_x = over_x.reshape(4, rows, LANES)[:, :half].reshape(-1, LANES)
    cut_y = over_y.reshape(4, rows, LANES)[:, half:].reshape(-1, LANES)
    return permute(cut_x, Y, n), permute(cut_y, X, n)


def gathered_pieces(geo, arrays, others):
    rows = geo.rows
    half = ceil_to(rows // 2, 16)
    found = []
    for core, group in ((0, arrays), (CORE, others)):
        for array, (relative, at, count) in zip(
            group, ((0, 0, rows), (X, 0, rows), (Y, 0, rows), (X + Y, 0, half), (X + Y, half, rows - half))
        ):
            found.append((array, [(z * count, relative + core + 8 * z, None, at, count) for z in range(4)]))
    return found


def gather_any(geo, chunk):
    gathered = lax.all_gather(chunk, AXES, axis=0)
    return [(gathered, [(0, 0, 0, 0, 0)])]


def add(*values):
    total = values[0].astype(F32)
    for value in values[1:]:
        total = total + value.astype(F32)
    return total


def plane_start(geo, keep, came):
    shape = (2, 2, 2, geo.rows, LANES)
    half = ceil_to(geo.rows // 2, 16)
    keep, came = keep.reshape(shape), came.reshape(shape)
    one = (keep[:, :, :, :half], came[:, :, :, :half])
    two = (keep[:, :, :, half:], came[:, :, :, half:])
    to_x = add(*(part[1] for part in one)).astype(BF16)
    to_y = add(*(part[:, 1] for part in two)).astype(BF16)
    return [part[0] for part in one], [part[:, 0] for part in two], to_x, to_y


def plane_next(one, two, from_x, from_y):
    one, two = one + [from_x], two + [from_y]
    to_y = add(*(part[1] for part in one)).astype(BF16)
    to_x = add(*(part[1] for part in two)).astype(BF16)
    return [part[0] for part in one], [part[0] for part in two], to_y, to_x


def plane_end(one, two, from_y, from_x):
    return jnp.concatenate([add(*one, from_y), add(*two, from_x)], 1)


def column_sum(geo, place, upper, lower, table):
    n = geo.devices
    if table:
        row = lax.broadcasted_iota(jnp.int32, (1, geo.rows, 1), 1)
        upper = jnp.where(row < geo.param_rows, upper, lower)
    is_upper = place[3] >= 2
    near = jnp.where(is_upper, upper, lower)
    far = jnp.where(is_upper, lower, upper).astype(BF16)
    return [near[0], permute(near[1].astype(BF16), Z1, n), permute(far[0], Z2, n), permute(far[1], Z3, n)]


def sum_any(chunks):
    return lax.psum_scatter(chunks.astype(F32), AXES, scatter_dimension=0, tiled=True)[0]


def timestep_embed(step_ids):
    half_dim = TD // 2
    freq_base = jnp.exp(jnp.arange(half_dim, dtype=F32) * (-math.log(10000.0) / half_dim))
    angle_grid = step_ids.astype(F32)[:, None] * freq_base[None, :]
    return jnp.concatenate([jnp.sin(angle_grid), jnp.cos(angle_grid)], axis=1)


def body(fast, chars, steps, embed, layer_params, cotangent):
    seqs, length = chars.shape
    tokens = seqs * length
    geo = Geometry(lax.axis_size(AXES), layer_params.shape[1], embed.shape[0])
    index = lax.axis_index(AXES).astype(jnp.int32)
    place = jnp.stack(
        [index, index * geo.shard % LANES, index * geo.embed_shard % LANES, index // 8]
    ).astype(jnp.int32)
    chunks = pack_shards(geo, place, layer_params, embed)
    emb = timestep_embed(steps).astype(BF16)
    emb_rows = jnp.concatenate([emb, jnp.zeros((8 - seqs, TD), BF16)], 0) if seqs < 8 else emb
    emb_t = emb.astype(F32).T
    chars_row, chars_col = chars.reshape(1, tokens), chars.reshape(tokens, 1)
    n = geo.devices

    cotangent = cotangent.reshape(tokens, D)
    if not fast:
        first = first_ahead(geo, seqs, place, gather_any(geo, chunks[0]), chars_col, emb_rows)
        first = first_ahead_rest(place, first)
        second = second_both(geo, fast, seqs, place, gather_any(geo, chunks[1]), first[N_STREAM], emb_rows, cotangent)
        low_second = both_back_attn(geo, fast, 1, seqs, place, second[N_GRAD], second, emb_t, second[N_REST], chars_row)
        up_first = first_back_mlp(geo, fast, place, low_second[N_GRAD], first)
        low_first = both_back_attn(geo, fast, 0, seqs, place, up_first[N_GRAD], first, emb_t, up_first[N_REST], chars_row)
        sums = [
            sum_any(jnp.concatenate([low_first[N_KEEP], up_first[N_KEEP]], 0)),
            sum_any(jnp.concatenate([low_second[N_KEEP], second[N_KEEP]], 0)),
            sum_any(low_first[N_TABLE_OUT]),
        ]
        grad_params, grad_embed = finish(geo, fast, place, sums)
        return (second[N_OUTPUT].reshape(seqs, length, D), grad_embed, grad_params)

    gathered, column = gather_both(geo, *chunks)
    sides = gather_sides(geo, column)
    column_other = permute(column, CORE, n)
    first = first_ahead(geo, seqs, place, gathered, chars_col, emb_rows)
    first, sides, column_other = sync(first, sides, column_other)
    corners = gather_corners(geo, *sides)
    sides_other = [permute(side, CORE, n) for side in sides]
    first = first_ahead_rest(place, first)
    first, corners, sides_other = sync(first, corners, sides_other)
    corners_other = [permute(corner, CORE, n) for corner in corners]
    pieces = gathered_pieces(geo, [column, *sides, *corners], [column_other, *sides_other, *corners_other])
    second = second_both(geo, fast, seqs, place, pieces, first[N_STREAM], emb_rows, cotangent)
    output = second[N_OUTPUT].reshape(seqs, length, D)

    def cross(to_one, to_two, one, two):
        return permute(to_one, one, n), permute(to_two, two, n)

    def attn(layer, grad, found, rest):
        got = both_back_attn(geo, fast, layer, seqs, place, grad, found, emb_t, rest, chars_row)
        return (got[N_KEEP], got[N_SEND]) if layer == 0 else (got[N_GRAD], got[N_KEEP], got[N_SEND])

    grad, rest, keep_u, send_u = (second[name] for name in (N_GRAD, N_REST, N_KEEP, N_SEND))
    came_u = permute(send_u, CORE, n)
    grad, keep_l, send_l = attn(1, grad, second, rest)
    grad, keep_u, came_u, keep_l, send_l = sync(grad, keep_u, came_u, keep_l, send_l)
    came_l = permute(send_l, CORE, n)
    one_u, two_u, to_x, to_y = plane_start(geo, keep_u, came_u)
    from_u = cross(to_x, to_y, X, Y)

    got = first_back_mlp(geo, fast, place, after(grad, to_x, to_y), first)
    grad, rest, keep, send = (got[name] for name in (N_GRAD, N_REST, N_KEEP, N_SEND))
    grad, rest, keep, send, came_l, from_u = sync(grad, rest, keep, send, came_l, from_u)
    came = permute(send, CORE, n)
    one_u, two_u, to_y, to_x = plane_next(one_u, two_u, *from_u)
    from_u = cross(to_y, to_x, Y, X)
    one_l, two_l, to_x_l, to_y_l = plane_start(geo, keep_l, came_l)
    from_l = cross(to_x_l, to_y_l, X, Y)

    grad = after(grad, to_x, to_y, to_x_l, to_y_l)
    low_keep, low_send = attn(0, grad, first, rest)
    low_keep, low_send, keep, came, from_u, from_l = sync(low_keep, low_send, keep, came, from_u, from_l)
    low_came = permute(low_send, CORE, n)
    one_l, two_l, to_y, to_x = plane_next(one_l, two_l, *from_l)
    from_l = cross(to_y, to_x, Y, X)
    one, two, to_x, to_y = plane_start(geo, keep, came)
    from_up = cross(to_x, to_y, X, Y)
    upper = plane_end(one_u, two_u, *from_u)

    low_came, low_keep, upper, _, _ = sync(low_came, low_keep, upper, to_x, to_y)
    low_one, low_two, to_x, to_y = plane_start(geo, low_keep, low_came)
    from_low = cross(to_x, to_y, X, Y)

    from_l, from_up, _, _ = sync(from_l, from_up, to_x, to_y)
    lower = plane_end(one_l, two_l, *from_l)
    seconds = column_sum(geo, place, upper, lower, False)
    one, two, to_y, to_x = plane_next(one, two, *from_up)
    from_up = cross(to_y, to_x, Y, X)

    from_low, _, _ = sync(from_low, to_y, to_x)
    low_one, low_two, to_y, to_x = plane_next(low_one, low_two, *from_low)
    from_low = cross(to_y, to_x, Y, X)

    from_low, from_up = sync(from_low, from_up)
    upper, lower = plane_end(one, two, *from_up), plane_end(low_one, low_two, *from_low)
    firsts = column_sum(geo, place, upper, lower, True)
    grad_params, grad_embed = finish(geo, fast, place, firsts + seconds)
    return (output, grad_embed, grad_params)


def solution(mesh):
    both = P(AXES)
    fast = dict(mesh.shape) == {"dp": 8, "fsdp": 4}
    return jax.shard_map(
        functools.partial(body, fast),
        mesh=mesh,
        in_specs=(P(AXES, None), both, both, P(None, AXES), P(AXES, None, None)),
        out_specs=(P(AXES, None, None), both, P(None, AXES)),
        check_vma=False,
    )
```

```python
import functools
import math

import jax
import jax.numpy as jnp
from jax import lax
from jax.experimental import pallas as pl
from jax.experimental.pallas import tpu as pltpu
from jax.sharding import PartitionSpec as P

D = 512
HEADS = 8
FF = 2048
VOCAB = 27
TD = 128
HD = 64
LANES = 128
EPSILON = 1e-05
AXES = ("dp", "fsdp")
F32 = jnp.float32
BF16 = jnp.bfloat16
VMEM_BYTES = 52 * 2**20

(
    N_CHARS, N_EMB, N_W_TIME, N_W_QKV, N_W_OUT, N_W_UP, N_W_DOWN,
    N_VECTORS, N_TABLE, N_X, N_A, N_QKV, N_PROB, N_O,
    N_X2, N_A2, N_GL, N_SLOPE, N_STREAM, N_OUTPUT, N_COTANGENT,
    N_GRAD, N_GRAD_IN, N_REST, N_KEEP, N_SEND, N_TABLE_OUT, N_EMB_T,
    N_CHUNKS, N_FLAT, N_FLAT_TABLE, N_CUTS, N_CUT_SEMS, N_NORMED, N_TOTAL,
    N_QKV_GRAD, N_HEADS_GRAD,
) = range(37)

ROW_GAIN_ONE, ROW_BIAS_ONE, ROW_W_TIME, ROW_B_TIME = 0, 4, 8, 520
ROW_QKV, ROW_OUT, ROW_GAIN_TWO, ROW_BIAS_TWO = 524, 6668, 8716, 8720
ROW_UP, ROW_B_UP, ROW_DOWN, ROW_B_DOWN, ROW_END = 8724, 16916, 16932, 25124, 25128
CHUNK_PAD = 832


def ceil_to(value, step):
    return -(-value // step) * step


class Geometry:
    def __init__(self, devices, shard, embed_shard):
        self.devices, self.shard, self.embed_shard = devices, shard, embed_shard
        self.param_rows = max(self.count(d, shard) for d in range(devices))
        self.embed_rows = max(self.count(d, embed_shard) for d in range(devices))
        self.embed_at = ceil_to(self.param_rows, 8)
        self.rows = ceil_to(max(self.embed_at + 8, self.param_rows + 2 * self.embed_rows), 16)

    @staticmethod
    def first(d, size):
        return d * size // LANES

    @staticmethod
    def count(d, size):
        return -(-(d + 1) * size // LANES) - d * size // LANES


def params(flops, nbytes, weight=0):
    flops, nbytes = max(flops * weight, 1000), max(nbytes * weight, 1000)
    return dict(
        compiler_params=pltpu.CompilerParams(vmem_limit_bytes=VMEM_BYTES),
        cost_estimate=pl.CostEstimate(flops=flops, bytes_accessed=nbytes, transcendentals=0),
    )


VM = pl.BlockSpec(memory_space=pltpu.VMEM)
SM = pl.BlockSpec(memory_space=pltpu.SMEM)
HBM = pl.BlockSpec(memory_space=pltpu.HBM)


def nn(left, right):
    return lax.dot_general(left, right, (((1,), (0,)), ((), ())), preferred_element_type=F32)


def nt(left, right):
    return lax.dot_general(left, right, (((1,), (1,)), ((), ())), preferred_element_type=F32)


def tn(left, right):
    return nn(left.T, right)


def shift_in(flat, offset):
    rolled = pltpu.roll(flat, offset, 1)
    above = jnp.concatenate([jnp.zeros((1, LANES), F32), rolled[:-1]], 0)
    lane = lax.broadcasted_iota(jnp.int32, flat.shape, 1)
    return jnp.where(lane >= offset, rolled, above)


def shift_out(flat, offset):
    rolled = pltpu.roll(flat, lax.rem(LANES - offset, LANES), 1)
    below = jnp.concatenate([rolled[1:], jnp.zeros((1, LANES), F32)], 0)
    lane = lax.broadcasted_iota(jnp.int32, flat.shape, 1)
    return jnp.where(lane < LANES - offset, rolled, below)


def pack_kernel(geo, place_ref, layers_ref, embed_ref, first_ref, second_ref):
    main = geo.embed_at
    for layer, out_ref in ((0, first_ref), (1, second_ref)):
        moved = shift_in(layers_ref[layer].astype(F32), place_ref[1])
        if layer == 0:
            tail = shift_in(embed_ref[...].astype(F32), place_ref[2])
            parts = [moved[:main], tail] + ([moved[main + 8 :]] if geo.rows > main + 8 else [])
            moved = jnp.concatenate(parts, 0)
        out_ref[...] = moved.astype(BF16)


def pack_shards(geo, place, layer_params, embed):
    layers = jnp.pad(layer_params, ((0, 0), (0, geo.rows * LANES - geo.shard)))
    table = jnp.pad(embed, (0, 8 * LANES - geo.embed_shard))
    out = jax.ShapeDtypeStruct((geo.rows, LANES), BF16)
    return pl.pallas_call(
        functools.partial(pack_kernel, geo),
        out_shape=(out, out),
        in_specs=[SM, VM, VM],
        out_specs=(VM, VM),
        **params(10**6, geo.rows * 1024),
    )(place, layers.reshape(2, geo.rows, LANES), table.reshape(8, LANES))


def finish_kernel(geo, fast, place_ref, *refs):
    grads_ref, embed_ref, moved = refs[-3:]
    parts = refs[:-3]
    count = 4 if fast else 1
    for layer in range(2):
        total = parts[layer * count][...].astype(F32)
        for part in parts[layer * count + 1 : (layer + 1) * count]:
            total = total + part[...].astype(F32)
        moved[pl.ds(layer * geo.rows, geo.rows), :] = shift_out(total, place_ref[1])
        if fast and layer == 0:
            first, size = geo.param_rows, geo.embed_rows
            lower, upper = total[first : first + size], total[first + size : first + 2 * size]
            tail = jnp.where(place_ref[3] >= 2, upper, lower)
            tail = jnp.concatenate([tail, jnp.zeros((8 - size, LANES), F32)], 0)
    if not fast:
        tail = parts[2][...]
    embed_ref[...] = shift_out(tail, place_ref[2])
    for r in range(ceil_to(geo.shard, LANES) // LANES):
        size = min(LANES, geo.shard - r * LANES)
        grads_ref[:, r * LANES : r * LANES + size] = moved[pl.ds(r, 2, stride=geo.rows), :][:, :size]


def finish(geo, fast, place, operands):
    grads, table = pl.pallas_call(
        functools.partial(finish_kernel, geo, fast),
        out_shape=(
            jax.ShapeDtypeStruct((2, geo.shard), F32),
            jax.ShapeDtypeStruct((8, LANES), F32),
        ),
        in_specs=[SM] + [VM] * len(operands),
        out_specs=(VM, VM),
        scratch_shapes=[pltpu.VMEM((2 * geo.rows, LANES), F32)],
        **params(10**6, geo.rows * 4096),
    )(place, *operands)
    return grads, table.reshape(-1)[: geo.embed_shard]


PARTS = {N_W_UP: (1, 4), N_W_DOWN: (0, 4), N_GL: (1, 4), N_SLOPE: (1, 4), N_PROB: (0, 2), N_QKV: (0, 2)}


def parts_of(name, parted):
    return range(PARTS[name][1]) if name in parted else range(1)


def part_of(ref, name, part, parted):
    if name not in parted:
        return ref
    dim, count = PARTS[name]
    size = ref.shape[dim] // count
    index = [slice(None)] * len(ref.shape)
    index[dim] = pl.ds(part * size, size)
    return ref.at[tuple(index)]


class Staged:
    def __init__(self, sources, targets, held, sems, parted):
        self.held, self.pending, self.sent, self.parted = held, {}, [], parted
        self.targets, self.sems = targets, sems
        order = sorted((part, place, name) for place, name in enumerate(sources) for part in parts_of(name, parted))
        for part, _, name in order:
            copy = pltpu.make_async_copy(
                part_of(sources[name], name, part, parted), part_of(held[name], name, part, parted), sems.at[len(self.pending)]
            )
            copy.start()
            self.pending[name, part] = copy
        self.used = len(order)

    def get(self, name, part=None):
        for one in parts_of(name, self.parted) if part is None or name not in self.parted else [part]:
            if (name, one) in self.pending:
                self.pending.pop((name, one)).wait()
        return self.held[name]

    def put(self, name, part=None):
        for one in parts_of(name, self.parted) if part is None else [part]:
            copy = pltpu.make_async_copy(
                part_of(self.held[name], name, one, self.parted), part_of(self.targets[name], name, one, self.parted), self.sems.at[self.used]
            )
            copy.start()
            self.used += 1
            self.sent.append(copy)

    def close(self):
        for copy in list(self.pending.values()) + self.sent:
            copy.wait()


def staged_call(kernel, place, operands, results, scratch, flops, raw=(), semaphores=0, unheld=(), parted=()):
    names, outs, temps = list(operands), list(results), list(scratch)

    held_outs = [name for name in outs if name not in unheld]

    def whole(place_ref, *refs):
        raws, refs = refs[: len(raw)], refs[len(raw) :]
        sources, refs = dict(zip(names, refs)), refs[len(names) :]
        targets, refs = dict(zip(outs, refs)), refs[len(outs) :]
        held, refs = dict(zip(names + held_outs, refs)), refs[len(names) + len(held_outs) :]
        extra, refs = dict(zip(temps, refs)), refs[len(temps) :]
        staged = Staged(sources, targets, held, refs[0], parted)
        kernel(place_ref, raws, staged, extra, refs[-1])
        staged.close()

    buffers = [pltpu.VMEM(v.shape, v.dtype) for v in (*operands.values(), *(results[name] for name in held_outs))]
    sems = [pltpu.SemaphoreType.DMA((sum(len(parts_of(name, parted)) for name in names + held_outs),))]
    if semaphores:
        sems.append(pltpu.SemaphoreType.DMA((semaphores,)))
    found = pl.pallas_call(
        whole,
        out_shape=tuple(results.values()),
        in_specs=[SM] + [HBM] * (len(raw) + len(names)),
        out_specs=(HBM,) * len(outs),
        scratch_shapes=buffers + list(scratch.values()) + sems,
        **params(flops, 2 * 10**7, 1),
    )(place, *raw, *operands.values())
    return dict(zip(outs, found))


def like(dtype, *shape):
    return jax.ShapeDtypeStruct(shape, dtype)


def unpack(geo, layer, plan, me, chunk_refs, held, flat, flat_table, out, sems):
    copies = []
    for source, pieces in zip(chunk_refs, plan):
        for src_at, relative, absolute, dst_at, count in pieces:
            if absolute is None:
                target = held.at[lax.bitwise_xor(me, relative), pl.ds(dst_at, count)]
                origin = source.at[pl.ds(src_at, count)]
            else:
                target, origin = held, source
            copies.append(pltpu.make_async_copy(origin, target, sems.at[len(copies)]))
    for copy in copies:
        copy.start()
    for copy in copies:
        copy.wait()
    for d in range(geo.devices):
        block = held[d].astype(F32)
        start, rows = geo.first(d, geo.shard), geo.count(d, geo.shard)
        split = (d * geo.shard) % LANES != 0
        if split:
            shared = flat[pl.ds(start, 1), :] + block[:1]
        flat[pl.ds(start, rows), :] = block[:rows]
        if split:
            flat[pl.ds(start, 1), :] = shared
        if layer == 0:
            tail = block[geo.embed_at : geo.embed_at + 8]
            start, rows = geo.first(d, geo.embed_shard), geo.count(d, geo.embed_shard)
            split = (d * geo.embed_shard) % LANES != 0
            if split:
                shared = flat_table[pl.ds(start, 1), :] + tail[:1]
            flat_table[pl.ds(start, rows), :] = tail[:rows]
            if split:
                flat_table[pl.ds(start, 1), :] = shared
    vectors = out[N_VECTORS]
    for row, start, width in (
        (0, ROW_GAIN_ONE, 4),
        (1, ROW_BIAS_ONE, 4),
        (2, ROW_B_TIME, 4),
        (3, ROW_GAIN_TWO, 4),
        (4, ROW_BIAS_TWO, 4),
        (5, ROW_B_DOWN, 4),
        (6, ROW_B_UP, 16),
    ):
        for c in range(width):
            vectors[row : row + 1, c * LANES : (c + 1) * LANES] = flat[pl.ds(start + c, 1), :]
    for name, start, rows, width in (
        (N_W_TIME, ROW_W_TIME, TD, 4),
        (N_W_QKV, ROW_QKV, D, 12),
        (N_W_OUT, ROW_OUT, D, 4),
        (N_W_UP, ROW_UP, D, 16),
        (N_W_DOWN, ROW_DOWN, FF, 4),
    ):
        for c in range(width):
            out[name][:, c * LANES : (c + 1) * LANES] = flat[pl.ds(start + c, rows, stride=width), :].astype(BF16)
    if layer == 0:
        table = out[N_TABLE]
        table[...] = jnp.zeros(table.shape, BF16)
        for c in range(4):
            table[0:VOCAB, c * LANES : (c + 1) * LANES] = flat_table[pl.ds(c, VOCAB, stride=4), :].astype(BF16)


WEIGHTS = {
    N_W_QKV: like(BF16, D, 3 * D),
    N_W_OUT: like(BF16, D, D),
    N_W_UP: like(BF16, D, FF),
    N_W_DOWN: like(BF16, FF, D),
    N_VECTORS: like(F32, 8, FF),
}


def unpack_scratch(geo, layer):
    scratch = {
        N_CHUNKS: pltpu.VMEM((geo.devices, geo.rows, LANES), BF16),
        N_FLAT: pltpu.VMEM((ROW_END + CHUNK_PAD, LANES), F32),
        N_FLAT_TABLE: pltpu.VMEM((4 * 32, LANES), F32),
        N_W_TIME: pltpu.VMEM((TD, D), BF16),
    }
    if layer == 0:
        scratch[N_TABLE] = pltpu.VMEM((32, D), BF16)
    return scratch


def split_gathered(gathered):
    plan = tuple(tuple(pieces) for array, pieces in gathered)
    return [array for array, pieces in gathered], plan, sum(len(pieces) for pieces in plan)


def norm_stats(values):
    mean = jnp.mean(values, -1, keepdims=True)
    centered = values - mean
    variance = jnp.mean(centered * centered, -1, keepdims=True)
    scale = lax.rsqrt(variance + EPSILON)
    return centered * scale, scale


ROW_BLOCK = 64


def norm_ahead(values, gain, bias, out):
    for r in range(0, values.shape[0], ROW_BLOCK):
        rows = slice(r, r + ROW_BLOCK)
        unit, _ = norm_stats(values[rows, :])
        out[rows, :] = (unit * gain + bias).astype(BF16)


def norm_back(grad, values, gain, passed, out):
    grad_gain, grad_bias = jnp.zeros((8, D), F32), jnp.zeros((8, D), F32)
    for r in range(0, values.shape[0], ROW_BLOCK):
        rows = slice(r, r + ROW_BLOCK)
        unit, scale = norm_stats(values[rows, :])
        block = grad[rows, :]
        grad_gain = grad_gain + jnp.sum((block * unit).reshape(-1, 8, D), 0)
        grad_bias = grad_bias + jnp.sum(block.reshape(-1, 8, D), 0)
        inner = block * gain
        shifted = inner - jnp.mean(inner, -1, keepdims=True)
        back = scale * (shifted - unit * jnp.mean(inner * unit, -1, keepdims=True))
        out[rows, :] = passed[rows, :].astype(F32) + back
    return jnp.sum(grad_gain, 0, keepdims=True), jnp.sum(grad_bias, 0, keepdims=True)


def gelu_both(u):
    root = math.sqrt(2.0 / math.pi)
    square = u * u
    t = jnp.tanh(root * (u + 0.044715 * (square * u)))
    half = 0.5 * (1.0 + t)
    slope = half + 0.5 * u * (1.0 - t * t) * (root * (1.0 + 3.0 * 0.044715 * square))
    return u * half, slope


def head_masks(shape, scale):
    lane = lax.broadcasted_iota(jnp.int32, shape, 1)
    one = jnp.where(lane < HD, scale, 0.0).astype(BF16)
    two = jnp.where(lane < HD, 0.0, scale).astype(BF16)
    return one, two


def ahead_attn(seqs, stream, emb, w_time, w_qkv, w_out, vectors, x, a, qkv, prob, o, x2, a2, done):
    tokens = x.shape[0]
    length = tokens // seqs
    time_vec = nn(emb[...], w_time[...]) + vectors[2:3, :D]
    for s in range(seqs):
        x[s * length : (s + 1) * length, :] = stream[s * length : (s + 1) * length] + time_vec[s : s + 1]
    done(N_X)
    norm_ahead(x, vectors[0:1, :D], vectors[1:2, :D], a)
    done(N_A)
    for c in range(3):
        part = slice(c * D, (c + 1) * D)
        qkv[:, part] = nn(a[...], w_qkv[:, part]).astype(BF16)
    done(N_QKV)
    masks = head_masks((length, LANES), 1.0 / math.sqrt(HD))
    heads = [(s, pair, h) for s in range(seqs) for pair in range(HEADS // 2) for h in range(2)]

    def cut(s, pair, c):
        return qkv[s * length : (s + 1) * length, c * D + pair * LANES : c * D + (pair + 1) * LANES]

    def scores_of(s, pair, h):
        return nt(cut(s, pair, 1) * masks[h], cut(s, pair, 0))

    ahead = [scores_of(*heads[i]) for i in range(4)]
    mixed = []
    for i, (s, pair, h) in enumerate(heads):
        scores = ahead.pop(0)
        if i + 4 < len(heads):
            ahead.append(scores_of(*heads[i + 4]))
        top = jnp.max(scores, 0, keepdims=True)
        expd = jnp.exp(scores - top)
        low = (expd * (1.0 / jnp.sum(expd, 0, keepdims=True))).astype(BF16)
        prob[s * HEADS + 2 * pair + h] = low
        v_t = cut(s, pair, 2).T
        mixed.append(nn(v_t[h * HD : (h + 1) * HD], low))
        if h == 1:
            rows = slice(s * length, (s + 1) * length)
            o[rows, pair * LANES : (pair + 1) * LANES] = jnp.concatenate(mixed, 0).T.astype(BF16)
            mixed = []
    done(N_PROB)
    done(N_O)
    x2[...] = x[...] + nn(o[...], w_out[...])
    done(N_X2)
    norm_ahead(x2, vectors[3:4, :D], vectors[4:5, :D], a2)
    done(N_A2)


def ahead_mlp(x2, a2, w_up, w_down, vectors, gl, slope, done):
    parts = [slice(c * D, (c + 1) * D) for c in range(FF // D)]

    def up(c):
        return nn(a2()[...], w_up(c)[:, parts[c]])

    total, u = None, up(0)
    for c, part in enumerate(parts):
        value, rate = gelu_both(u + vectors()[6:7, part])
        low = value.astype(BF16)
        gl[:, part] = low
        slope[:, part] = rate.astype(BF16)
        done(N_GL, c)
        done(N_SLOPE, c)
        if c + 1 < len(parts):
            u = up(c + 1)
        step = nn(low, w_down(c)[part, :])
        total = step if total is None else total + step
    return x2()[...] + vectors()[5:6, :D] + total


class Chunks:
    def __init__(self, geo, fast, me, held, targets, sems):
        self.geo, self.fast, self.me, self.held, self.targets, self.sems = geo, fast, me, held, targets, sems
        self.copies = []

    def cut(self, d, flat, base, table=None):
        geo, slot = self.geo, d % (self.geo.devices // 2)
        block = flat[pl.ds(geo.first(d, geo.shard) - base, geo.rows), :]
        if table is not None:
            first, size = geo.param_rows, geo.embed_rows
            tails = [
                table[pl.ds(geo.first(e, geo.embed_shard), size), :] for e in (d, d + geo.devices // 2)
            ]
            block = jnp.concatenate([block[:first], *tails, block[first + 2 * size :]], 0)
        self.held[slot] = block.astype(BF16)
        source, sem = self.held.at[slot], self.sems.at[slot]
        if not self.fast:
            self.copies.append(pltpu.make_async_copy(source, self.targets[0].at[slot], sem))
            self.copies[-1].start()
            return
        relative = lax.bitwise_xor(self.me, d)
        row = lax.bitwise_and(relative, 4) + lax.bitwise_and(relative, 2)
        row = row + lax.bitwise_and(lax.shift_right_logical(relative, 3), 1)
        keep, send = (pltpu.make_async_copy(source, target.at[row], sem) for target in self.targets)
        core = lax.bitwise_and(relative, 1)

        @pl.when(core == 0)
        def _():
            keep.start()

        @pl.when(core == 1)
        def _():
            send.start()

        self.copies.append(keep)

    def close(self):
        for copy in self.copies:
            copy.wait()


def back_mlp(geo, chunks, grad_in, x2, a2, gl, slope, w_up, w_down, vectors, grad, rest, flat, base, normed, done):
    grad_low = grad_in()[...].astype(BF16)
    flat[pl.ds(ROW_END - base, CHUNK_PAD), :] = jnp.zeros((CHUNK_PAD, LANES), F32)
    grad_bias = jnp.sum(grad_low.astype(F32), 0, keepdims=True)
    for c in range(4):
        flat[pl.ds(ROW_B_DOWN - base + c, 1), :] = grad_bias[:, c * LANES : (c + 1) * LANES]
    parts = [slice(j * D, (j + 1) * D) for j in range(FF // D)]

    def hidden_grad(j):
        return nt(grad_low, w_down(j)[parts[j], :])

    total, hidden = None, hidden_grad(0)
    for j, part in enumerate(parts):
        up_grad = (hidden * slope(j)[:, part].astype(F32)).astype(BF16)
        bias_grad = jnp.sum(up_grad.astype(F32), 0, keepdims=True)
        if j + 1 < len(parts):
            hidden = hidden_grad(j + 1)
        down = tn(gl(j)[:, part], grad_low)
        for c in range(4):
            cols = slice(c * LANES, (c + 1) * LANES)
            flat[pl.ds(ROW_B_UP - base + 4 * j + c, 1), :] = bias_grad[:, cols]
            flat[pl.ds(ROW_DOWN - base + 4 * D * j + c, D, stride=4), :] = down[:, cols]
        up = tn(a2()[...], up_grad)
        for c in range(4):
            cols = slice(c * LANES, (c + 1) * LANES)
            flat[pl.ds(ROW_UP - base + 4 * j + c, D, stride=16), :] = up[:, cols]
        step = nt(up_grad, w_up(j)[:, part])
        total = step if total is None else total + step
    normed[...] = total
    for d in range(geo.devices // 2, geo.devices):
        chunks.cut(d, flat, base)
    grad_gain, grad_bias = norm_back(normed, x2(), vectors()[3:4, :D], grad_in(), grad)
    done(N_GRAD)
    for c in range(4):
        cols = slice(c * LANES, (c + 1) * LANES)
        flat[pl.ds(ROW_GAIN_TWO - base + c, 1), :] = grad_gain[:, cols]
        flat[pl.ds(ROW_BIAS_TWO - base + c, 1), :] = grad_bias[:, cols]
    rest[...] = flat[pl.ds(ROW_GAIN_TWO - base, rest.shape[0]), :].astype(BF16)
    done(N_REST)


def back_attn(
    geo, seqs, chunks, table, embed_outs, grad_in, x, a, qkv, prob, o, w_qkv, w_out, vectors, emb_t, rest, total,
    flat, qkv_grad, heads_grad, normed, chars, done,
):
    tokens = normed.shape[0]
    length = tokens // seqs
    grad_low = grad_in()[...].astype(BF16)
    heads_grad[...] = nt(grad_low, w_out()[...]).astype(BF16)
    out_grad = tn(o()[...], grad_low)
    for c in range(4):
        flat[pl.ds(ROW_OUT + c, D, stride=4), :] = out_grad[:, c * LANES : (c + 1) * LANES]
    masks = head_masks((length, LANES), 1.0)
    scale = 1.0 / math.sqrt(HD)
    lane = lax.broadcasted_iota(jnp.int32, (length, LANES), 1)
    qkv, prob = qkv(), prob()
    heads = [(s, pair, h) for s in range(seqs) for pair in range(HEADS // 2) for h in range(2)]

    def cut(s, pair, c):
        return qkv[s * length : (s + 1) * length, c * D + pair * LANES : c * D + (pair + 1) * LANES]

    def go_of(s, pair):
        return heads_grad[s * length : (s + 1) * length, pair * LANES : (pair + 1) * LANES]

    def prob_grad_of(s, pair, h):
        return nt(cut(s, pair, 2) * masks[h], go_of(s, pair))

    ahead = [prob_grad_of(*heads[i]) for i in range(4)]
    to_q, to_k, to_v = [], [], []
    for i, (s, pair, h) in enumerate(heads):
        prob_grad = ahead.pop(0)
        if i + 4 < len(heads):
            ahead.append(prob_grad_of(*heads[i + 4]))
        prob_low = prob[s * HEADS + 2 * pair + h]
        prob_full = prob_low.astype(F32)
        weighted = prob_full * prob_grad
        row_dot = jnp.sum(weighted, 0, keepdims=True)
        score_grad = (weighted - prob_full * row_dot).astype(BF16)
        to_v.append(nn(prob_low, go_of(s, pair)))
        k_t = cut(s, pair, 1).T
        to_q.append(nn(k_t[h * HD : (h + 1) * HD], score_grad))
        to_k.append(nn(score_grad, cut(s, pair, 0)))
        if h == 1:
            rows = slice(s * length, (s + 1) * length)
            cols = [slice(c * D + pair * LANES, c * D + (pair + 1) * LANES) for c in range(3)]
            qkv_grad[rows, cols[0]] = (jnp.concatenate(to_q, 0).T * scale).astype(BF16)
            qkv_grad[rows, cols[1]] = (jnp.where(lane < HD, to_k[0], to_k[1]) * scale).astype(BF16)
            qkv_grad[rows, cols[2]] = jnp.where(lane < HD, to_v[0], to_v[1]).astype(BF16)
            to_q, to_k, to_v = [], [], []
    a_t, steps = a()[...].T, None
    for part in range(3):
        cols = slice(part * D, (part + 1) * D)
        piece = nn(a_t, qkv_grad[:, cols])
        for c in range(4):
            flat[pl.ds(ROW_QKV + 4 * part + c, D, stride=12), :] = piece[:, c * LANES : (c + 1) * LANES]
        step = nt(qkv_grad[:, cols], w_qkv()[:, cols])
        steps = step if steps is None else steps + step
    normed[...] = steps
    flat[pl.ds(ROW_GAIN_TWO, rest().shape[0]), :] = rest()[...].astype(F32)
    middle = geo.devices // 2
    early = [d for d in range(middle) if geo.first(d, geo.shard) >= ROW_QKV] if table is None else []
    for d in early:
        chunks.cut(d, flat, 0)
    grad_gain, grad_bias = norm_back(normed, x(), vectors()[0:1, :D], grad_in(), total)
    done(N_GRAD)
    time_grad = [
        jnp.sum(total[s * length : (s + 1) * length, :], 0, keepdims=True).astype(BF16).astype(F32) for s in range(seqs)
    ]
    bias_grad = sum(time_grad[1:], time_grad[0])
    weight_grad = sum(emb_t()[:, s : s + 1] * time_grad[s] for s in range(seqs))
    for c in range(4):
        cols = slice(c * LANES, (c + 1) * LANES)
        flat[pl.ds(ROW_GAIN_ONE + c, 1), :] = grad_gain[:, cols]
        flat[pl.ds(ROW_BIAS_ONE + c, 1), :] = grad_bias[:, cols]
        flat[pl.ds(ROW_B_TIME + c, 1), :] = bias_grad[:, cols]
        flat[pl.ds(ROW_W_TIME + c, TD, stride=4), :] = weight_grad[:, cols]
    if table is not None:
        kind = lax.broadcasted_iota(jnp.int32, (32, tokens), 0)
        table_grad = nn((chars()[...] == kind).astype(BF16), total[...].astype(BF16))
        for c in range(4):
            table[pl.ds(c, 32, stride=4), :] = table_grad[:, c * LANES : (c + 1) * LANES]
    for d in range(middle):
        if d not in early:
            chunks.cut(d, flat, 0, table if chunks.fast else None)
    if table is not None and not chunks.fast:
        for d in range(geo.devices):
            embed_outs[d] = table[pl.ds(geo.first(d, geo.embed_shard), 8), :]


def kept_shapes(seqs, tokens):
    length = tokens // seqs
    return {
        N_X: like(F32, tokens, D),
        N_A: like(BF16, tokens, D),
        N_QKV: like(BF16, tokens, 3 * D),
        N_PROB: like(BF16, seqs * HEADS, length, length),
        N_O: like(BF16, tokens, D),
    }


def rest_rows(geo):
    middle = geo.first(geo.devices // 2, geo.shard)
    return ceil_to(middle + geo.rows - ROW_GAIN_TWO, 16)


def chunk_results(geo, fast):
    if fast:
        shape = like(BF16, geo.devices // 4, geo.rows, LANES)
        return {N_KEEP: shape, N_SEND: shape}
    return {N_KEEP: like(BF16, geo.devices // 2, geo.rows, LANES)}


def chunk_targets(staged, fast):
    return [staged.targets[name] for name in ((N_KEEP, N_SEND) if fast else (N_KEEP,))]


def chunk_scratch(geo, tokens):
    return {
        N_CUTS: pltpu.VMEM((geo.devices // 2, geo.rows, LANES), BF16),
        N_CUT_SEMS: pltpu.SemaphoreType.DMA((geo.devices // 2,)),
        N_NORMED: pltpu.VMEM((tokens, D), F32),
    }


def first_ahead(geo, seqs, place, gathered, chars, emb):
    tokens = chars.shape[0]
    arrays, plan, count = split_gathered(gathered)
    results = WEIGHTS | kept_shapes(seqs, tokens) | {N_X2: like(F32, tokens, D), N_A2: like(BF16, tokens, D)}

    def kernel(place_ref, chunk_refs, staged, extra, sems):
        held = staged.held
        unpack(
            geo, 0, plan, place_ref[0], chunk_refs, extra[N_CHUNKS], extra[N_FLAT], extra[N_FLAT_TABLE], held | extra, sems
        )
        for name in WEIGHTS:
            staged.put(name)
        lane = lax.broadcasted_iota(jnp.int32, (tokens, 32), 1)
        stream = nn((staged.get(N_CHARS)[...] == lane).astype(BF16), extra[N_TABLE][...])
        weights = [extra[N_W_TIME]] + [held[name] for name in (N_W_QKV, N_W_OUT, N_VECTORS)]
        outs = [held[name] for name in (N_X, N_A, N_QKV, N_PROB, N_O, N_X2, N_A2)]
        ahead_attn(seqs, stream, staged.get(N_EMB), *weights, *outs, staged.put)

    operands = {N_CHARS: chars, N_EMB: emb}
    scratch = unpack_scratch(geo, 0)
    return staged_call(kernel, place, operands, results, scratch, 4 * 10**9, arrays, count, parted=())


def first_ahead_rest(place, found):
    names = (N_A2, N_W_UP, N_VECTORS, N_W_DOWN, N_X2)
    operands = {name: found[name] for name in names}
    tokens = found[N_X2].shape[0]
    results = {N_STREAM: like(F32, tokens, D), N_GL: like(BF16, tokens, FF), N_SLOPE: like(BF16, tokens, FF)}

    def kernel(place_ref, _, staged, extra, sems):
        late = [functools.partial(staged.get, name) for name in (N_X2, N_A2, N_W_UP, N_W_DOWN, N_VECTORS)]
        gl, slope, stream = (staged.held[name] for name in (N_GL, N_SLOPE, N_STREAM))
        stream[...] = ahead_mlp(*late, gl, slope, staged.put)
        staged.put(N_STREAM)

    return found | staged_call(kernel, place, operands, results, {}, 4 * 10**9, parted=(N_W_UP, N_W_DOWN, N_GL, N_SLOPE))


def second_both(geo, fast, seqs, place, gathered, stream, emb, cotangent):
    tokens = stream.shape[0]
    arrays, plan, count = split_gathered(gathered)
    results = {name: WEIGHTS[name] for name in (N_W_QKV, N_W_OUT, N_VECTORS)}
    results = results | kept_shapes(seqs, tokens)
    results = results | {
        N_OUTPUT: like(BF16, tokens, D),
        N_GRAD: like(F32, tokens, D),
        N_REST: like(BF16, rest_rows(geo), LANES),
    }
    results = results | chunk_results(geo, fast)
    scratch = unpack_scratch(geo, 1)
    scratch[N_W_UP], scratch[N_W_DOWN] = pltpu.VMEM((D, FF), BF16), pltpu.VMEM((FF, D), BF16)
    scratch[N_X2], scratch[N_A2] = pltpu.VMEM((tokens, D), F32), pltpu.VMEM((tokens, D), BF16)
    scratch[N_GL], scratch[N_SLOPE] = pltpu.VMEM((tokens, FF), BF16), pltpu.VMEM((tokens, FF), BF16)
    scratch = scratch | chunk_scratch(geo, tokens)

    def kernel(place_ref, chunk_arrays, staged, extra, sems):
        every = staged.held | extra
        unpack(geo, 1, plan, place_ref[0], chunk_arrays, extra[N_CHUNKS], extra[N_FLAT], extra[N_FLAT_TABLE], every, sems)
        for name in (N_W_QKV, N_W_OUT, N_VECTORS):
            staged.put(name)
        weights = [every[name] for name in (N_W_TIME, N_W_QKV, N_W_OUT, N_VECTORS)]
        outs = [every[name] for name in (N_X, N_A, N_QKV, N_PROB, N_O, N_X2, N_A2)]

        def done(name, part=None):
            if name in results:
                staged.put(name, part)

        ahead_attn(seqs, staged.get(N_STREAM)[...], staged.get(N_EMB), *weights, *outs, done)

        def ready(*names):
            return [lambda part=None, ref=every[name]: ref for name in names]

        outputs = ahead_mlp(*ready(N_X2, N_A2, N_W_UP, N_W_DOWN, N_VECTORS), every[N_GL], every[N_SLOPE], done)
        every[N_OUTPUT][...] = outputs.astype(BF16)
        done(N_OUTPUT)
        chunks = Chunks(geo, fast, place_ref[0], extra[N_CUTS], chunk_targets(staged, fast), extra[N_CUT_SEMS])
        back_mlp(
            geo, chunks, functools.partial(staged.get, N_COTANGENT),
            *ready(N_X2, N_A2, N_GL, N_SLOPE, N_W_UP, N_W_DOWN, N_VECTORS),
            every[N_GRAD], every[N_REST], extra[N_FLAT], 0, extra[N_NORMED], done,
        )
        chunks.close()

    operands = {N_STREAM: stream, N_EMB: emb, N_COTANGENT: cotangent}
    return staged_call(kernel, place, operands, results, scratch, 10**10, arrays, count, (N_KEEP, N_SEND))


def first_back_mlp(geo, fast, place, grad, found):
    names = (N_GRAD_IN, N_W_DOWN, N_SLOPE, N_GL, N_A2, N_W_UP, N_X2, N_VECTORS)
    operands = {name: grad if name == N_GRAD_IN else found[name] for name in names}
    tokens = grad.shape[0]
    results = {N_GRAD: like(F32, tokens, D), N_REST: like(BF16, rest_rows(geo), LANES)} | chunk_results(geo, fast)
    base = ROW_GAIN_TWO

    def kernel(place_ref, _, staged, extra, sems):
        late = [
            functools.partial(staged.get, name)
            for name in (N_GRAD_IN, N_X2, N_A2, N_GL, N_SLOPE, N_W_UP, N_W_DOWN, N_VECTORS)
        ]
        chunks = Chunks(geo, fast, place_ref[0], extra[N_CUTS], chunk_targets(staged, fast), extra[N_CUT_SEMS])
        back_mlp(
            geo, chunks, *late, staged.held[N_GRAD], staged.held[N_REST], extra[N_FLAT], base, extra[N_NORMED], staged.put
        )
        chunks.close()

    scratch = {N_FLAT: pltpu.VMEM((ROW_END - base + CHUNK_PAD, LANES), F32)} | chunk_scratch(geo, tokens)
    return staged_call(kernel, place, operands, results, scratch, 6 * 10**9, unheld=(N_KEEP, N_SEND))


def both_back_attn(geo, fast, layer, seqs, place, grad, found, emb_t, rest, chars_row):
    names = (N_GRAD_IN, N_W_OUT, N_O, N_QKV, N_PROB, N_A, N_W_QKV, N_X, N_VECTORS, N_EMB_T, N_REST)
    given = {N_GRAD_IN: grad, N_EMB_T: emb_t, N_REST: rest}
    operands = {name: given[name] if name in given else found[name] for name in names}
    tokens = grad.shape[0]
    results = {} if layer == 0 else {N_GRAD: like(F32, tokens, D)}
    results = results | chunk_results(geo, fast)
    scratch = {
        N_FLAT: pltpu.VMEM((ROW_GAIN_TWO + rest.shape[0], LANES), F32),
        N_QKV_GRAD: pltpu.VMEM((tokens, 3 * D), BF16),
        N_HEADS_GRAD: pltpu.VMEM((tokens, D), BF16),
    } | chunk_scratch(geo, tokens)
    if layer == 0:
        scratch[N_TOTAL] = pltpu.VMEM((tokens, D), F32)
        operands[N_CHARS] = chars_row
        scratch[N_TABLE] = pltpu.VMEM((4 * 32, LANES), F32)
        if not fast:
            results[N_TABLE_OUT] = like(F32, geo.devices, 8, LANES)

    def kernel(place_ref, _, staged, extra, sems):
        late = [functools.partial(staged.get, name) for name in (N_GRAD_IN, N_X, N_A, N_QKV, N_PROB, N_O, N_W_QKV, N_W_OUT)]
        tail = [functools.partial(staged.get, name) for name in (N_VECTORS, N_EMB_T, N_REST)]
        chunks = Chunks(geo, fast, place_ref[0], extra[N_CUTS], chunk_targets(staged, fast), extra[N_CUT_SEMS])

        def done(name, part=None):
            if name in results:
                staged.put(name, part)

        back_attn(
            geo, seqs, chunks, extra.get(N_TABLE), staged.held.get(N_TABLE_OUT), *late, *tail,
            extra[N_TOTAL] if layer == 0 else staged.held[N_GRAD], extra[N_FLAT], extra[N_QKV_GRAD], extra[N_HEADS_GRAD],
            extra[N_NORMED], functools.partial(staged.get, N_CHARS), done,
        )
        done(N_TABLE_OUT)
        chunks.close()

    return staged_call(kernel, place, operands, results, scratch, 6 * 10**9, unheld=(N_KEEP, N_SEND))


def permute(value, distance, devices):
    return lax.ppermute(value, AXES, [(d, d ^ distance) for d in range(devices)])


Z1, Z2, Z3, X, Y, CORE = 8, 16, 24, 4, 2, 1


def after(value, *others):
    return lax.optimization_barrier((value, *others))[0]


def sync(*values):
    return lax.optimization_barrier(values)


def gather_both(geo, first, second):
    n, rows = geo.devices, geo.rows
    half = ceil_to(rows // 2, 16)

    def sides(held):
        return permute(held, X, n), permute(held, Y, n)

    def corners(over_x, over_y):
        return permute(over_x[:half], Y, n), permute(over_y[half:], X, n)

    def other(*arrays):
        return permute(jnp.concatenate(arrays, 0), CORE, n)

    near, over = permute(first, Z1, n), permute(first, Z2, n)
    sides_0 = sides(first)
    sides_0 = sync(*sides_0)
    corners_0 = corners(*sides_0)
    near, _ = sync(near, sides_0[0])
    sides_1 = sides(near)
    over, _ = sync(over, near)
    far = permute(over, Z1, n)
    sides_2 = sides(over)
    *sides_1, _ = sync(*sides_1, over)
    corners_1 = corners(*sides_1)
    far, *corners_0 = sync(far, *corners_0, sides_1[0])[:3]
    sides_3 = sides(far)
    other_0 = other(first, *sides_0, *corners_0)
    second, _ = sync(second, far)
    near_b, over_b = permute(second, Z1, n), permute(second, Z2, n)
    *sides_2, _ = sync(*sides_2, far)
    corners_2 = corners(*sides_2)
    *corners_1, _ = sync(*corners_1, sides_2[0])
    other_1 = other(near, *sides_1, *corners_1)
    *sides_3, _ = sync(*sides_3, sides_2[0])
    corners_3 = corners(*sides_3)
    over_b, near_b, _ = sync(over_b, near_b, sides_3[0])
    far_b = permute(over_b, Z1, n)
    *corners_2, _ = sync(*corners_2, sides_3[0])
    other_2 = other(over, *sides_2, *corners_2)
    *corners_3, far_b, _ = sync(*corners_3, far_b, corners_2[0])
    other_3 = other(far, *sides_3, *corners_3)
    column = jnp.concatenate([second, near_b, over_b, far_b], 0)
    found = []
    for z, arrays, packed in (
        (0, (first, *sides_0, *corners_0), other_0),
        (Z1, (near, *sides_1, *corners_1), other_1),
        (Z2, (over, *sides_2, *corners_2), other_2),
        (Z3, (far, *sides_3, *corners_3), other_3),
    ):
        pieces = [
            (0, z, None, 0, rows),
            (rows, z + X, None, 0, rows),
            (2 * rows, z + Y, None, 0, rows),
            (3 * rows, z + X + Y, None, 0, half),
            (3 * rows + half, z + X + Y, None, half, rows - half),
        ]
        for array, (_, relative, _, at, count) in zip(arrays, pieces):
            found.append((array, [(0, relative, None, at, count)]))
        found.append((packed, [(src, rel + CORE, None, at, count) for src, rel, _, at, count in pieces]))
    return found, column


def gather_sides(geo, column):
    return permute(column, X, geo.devices), permute(column, Y, geo.devices)


def gather_corners(geo, over_x, over_y):
    n, rows = geo.devices, geo.rows
    half = ceil_to(rows // 2, 16)
    cut_x = over_x.reshape(4, rows, LANES)[:, :half].reshape(-1, LANES)
    cut_y = over_y.reshape(4, rows, LANES)[:, half:].reshape(-1, LANES)
    return permute(cut_x, Y, n), permute(cut_y, X, n)


def gathered_pieces(geo, arrays, others):
    rows = geo.rows
    half = ceil_to(rows // 2, 16)
    found = []
    for core, group in ((0, arrays), (CORE, others)):
        for array, (relative, at, count) in zip(
            group, ((0, 0, rows), (X, 0, rows), (Y, 0, rows), (X + Y, 0, half), (X + Y, half, rows - half))
        ):
            found.append((array, [(z * count, relative + core + 8 * z, None, at, count) for z in range(4)]))
    return found


def gather_any(geo, chunk):
    gathered = lax.all_gather(chunk, AXES, axis=0)
    return [(gathered, [(0, 0, 0, 0, 0)])]


def add(*values):
    total = values[0].astype(F32)
    for value in values[1:]:
        total = total + value.astype(F32)
    return total


def plane_start(geo, keep, came):
    shape = (2, 2, 2, geo.rows, LANES)
    half = ceil_to(geo.rows // 2, 16)
    keep, came = keep.reshape(shape), came.reshape(shape)
    one = (keep[:, :, :, :half], came[:, :, :, :half])
    two = (keep[:, :, :, half:], came[:, :, :, half:])
    to_x = add(*(part[1] for part in one)).astype(BF16)
    to_y = add(*(part[:, 1] for part in two)).astype(BF16)
    return [part[0] for part in one], [part[:, 0] for part in two], to_x, to_y


def plane_next(one, two, from_x, from_y):
    one, two = one + [from_x], two + [from_y]
    to_y = add(*(part[1] for part in one)).astype(BF16)
    to_x = add(*(part[1] for part in two)).astype(BF16)
    return [part[0] for part in one], [part[0] for part in two], to_y, to_x


def plane_end(one, two, from_y, from_x):
    return jnp.concatenate([add(*one, from_y), add(*two, from_x)], 1)


def column_sum(geo, place, upper, lower, table):
    n = geo.devices
    if table:
        row = lax.broadcasted_iota(jnp.int32, (1, geo.rows, 1), 1)
        upper = jnp.where(row < geo.param_rows, upper, lower)
    is_upper = place[3] >= 2
    near = jnp.where(is_upper, upper, lower)
    far = jnp.where(is_upper, lower, upper).astype(BF16)
    return [near[0], permute(near[1].astype(BF16), Z1, n), permute(far[0], Z2, n), permute(far[1], Z3, n)]


def sum_any(chunks):
    return lax.psum_scatter(chunks.astype(F32), AXES, scatter_dimension=0, tiled=True)[0]


def timestep_embed(step_ids):
    half_dim = TD // 2
    freq_base = jnp.exp(jnp.arange(half_dim, dtype=F32) * (-math.log(10000.0) / half_dim))
    angle_grid = step_ids.astype(F32)[:, None] * freq_base[None, :]
    return jnp.concatenate([jnp.sin(angle_grid), jnp.cos(angle_grid)], axis=1)


def body(fast, chars, steps, embed, layer_params, cotangent):
    seqs, length = chars.shape
    tokens = seqs * length
    geo = Geometry(lax.axis_size(AXES), layer_params.shape[1], embed.shape[0])
    index = lax.axis_index(AXES).astype(jnp.int32)
    place = jnp.stack(
        [index, index * geo.shard % LANES, index * geo.embed_shard % LANES, index // 8]
    ).astype(jnp.int32)
    chunks = pack_shards(geo, place, layer_params, embed)
    emb = timestep_embed(steps).astype(BF16)
    emb_rows = jnp.concatenate([emb, jnp.zeros((8 - seqs, TD), BF16)], 0) if seqs < 8 else emb
    emb_t = emb.astype(F32).T
    chars_row, chars_col = chars.reshape(1, tokens), chars.reshape(tokens, 1)
    n = geo.devices

    cotangent = cotangent.reshape(tokens, D)
    if not fast:
        first = first_ahead(geo, seqs, place, gather_any(geo, chunks[0]), chars_col, emb_rows)
        first = first_ahead_rest(place, first)
        second = second_both(geo, fast, seqs, place, gather_any(geo, chunks[1]), first[N_STREAM], emb_rows, cotangent)
        low_second = both_back_attn(geo, fast, 1, seqs, place, second[N_GRAD], second, emb_t, second[N_REST], chars_row)
        up_first = first_back_mlp(geo, fast, place, low_second[N_GRAD], first)
        low_first = both_back_attn(geo, fast, 0, seqs, place, up_first[N_GRAD], first, emb_t, up_first[N_REST], chars_row)
        sums = [
            sum_any(jnp.concatenate([low_first[N_KEEP], up_first[N_KEEP]], 0)),
            sum_any(jnp.concatenate([low_second[N_KEEP], second[N_KEEP]], 0)),
            sum_any(low_first[N_TABLE_OUT]),
        ]
        grad_params, grad_embed = finish(geo, fast, place, sums)
        return (second[N_OUTPUT].reshape(seqs, length, D), grad_embed, grad_params)

    gathered, column = gather_both(geo, *chunks)
    sides = gather_sides(geo, column)
    column_other = permute(column, CORE, n)
    first = first_ahead(geo, seqs, place, gathered, chars_col, emb_rows)
    first, sides, column_other = sync(first, sides, column_other)
    corners = gather_corners(geo, *sides)
    sides_other = [permute(side, CORE, n) for side in sides]
    first = first_ahead_rest(place, first)
    first, corners, sides_other = sync(first, corners, sides_other)
    corners_other = [permute(corner, CORE, n) for corner in corners]
    pieces = gathered_pieces(geo, [column, *sides, *corners], [column_other, *sides_other, *corners_other])
    second = second_both(geo, fast, seqs, place, pieces, first[N_STREAM], emb_rows, cotangent)
    output = second[N_OUTPUT].reshape(seqs, length, D)

    def cross(to_one, to_two, one, two):
        return permute(to_one, one, n), permute(to_two, two, n)

    def attn(layer, grad, found, rest):
        got = both_back_attn(geo, fast, layer, seqs, place, grad, found, emb_t, rest, chars_row)
        return (got[N_KEEP], got[N_SEND]) if layer == 0 else (got[N_GRAD], got[N_KEEP], got[N_SEND])

    grad, rest, keep_u, send_u = (second[name] for name in (N_GRAD, N_REST, N_KEEP, N_SEND))
    came_u = permute(send_u, CORE, n)
    grad, keep_l, send_l = attn(1, grad, second, rest)
    grad, keep_u, came_u, keep_l, send_l = sync(grad, keep_u, came_u, keep_l, send_l)
    came_l = permute(send_l, CORE, n)
    one_u, two_u, to_x, to_y = plane_start(geo, keep_u, came_u)
    from_u = cross(to_x, to_y, X, Y)

    got = first_back_mlp(geo, fast, place, after(grad, to_x, to_y), first)
    grad, rest, keep, send = (got[name] for name in (N_GRAD, N_REST, N_KEEP, N_SEND))
    grad, rest, keep, send, came_l, from_u = sync(grad, rest, keep, send, came_l, from_u)
    came = permute(send, CORE, n)
    one_u, two_u, to_y, to_x = plane_next(one_u, two_u, *from_u)
    from_u = cross(to_y, to_x, Y, X)
    one_l, two_l, to_x_l, to_y_l = plane_start(geo, keep_l, came_l)
    from_l = cross(to_x_l, to_y_l, X, Y)

    grad = after(grad, to_x, to_y, to_x_l, to_y_l)
    low_keep, low_send = attn(0, grad, first, rest)
    low_keep, low_send, keep, came, from_u, from_l = sync(low_keep, low_send, keep, came, from_u, from_l)
    low_came = permute(low_send, CORE, n)
    one_l, two_l, to_y, to_x = plane_next(one_l, two_l, *from_l)
    from_l = cross(to_y, to_x, Y, X)
    one, two, to_x, to_y = plane_start(geo, keep, came)
    from_up = cross(to_x, to_y, X, Y)
    upper = plane_end(one_u, two_u, *from_u)

    low_came, low_keep, upper, _, _ = sync(low_came, low_keep, upper, to_x, to_y)
    low_one, low_two, to_x, to_y = plane_start(geo, low_keep, low_came)
    from_low = cross(to_x, to_y, X, Y)

    from_l, from_up, _, _ = sync(from_l, from_up, to_x, to_y)
    lower = plane_end(one_l, two_l, *from_l)
    seconds = column_sum(geo, place, upper, lower, False)
    one, two, to_y, to_x = plane_next(one, two, *from_up)
    from_up = cross(to_y, to_x, Y, X)

    from_low, _, _ = sync(from_low, to_y, to_x)
    low_one, low_two, to_y, to_x = plane_next(low_one, low_two, *from_low)
    from_low = cross(to_y, to_x, Y, X)

    from_low, from_up = sync(from_low, from_up)
    upper, lower = plane_end(one, two, *from_up), plane_end(low_one, low_two, *from_low)
    firsts = column_sum(geo, place, upper, lower, True)
    grad_params, grad_embed = finish(geo, fast, place, firsts + seconds)
    return (output, grad_embed, grad_params)


def solution(mesh):
    both = P(AXES)
    fast = dict(mesh.shape) == {"dp": 8, "fsdp": 4}
    return jax.shard_map(
        functools.partial(body, fast),
        mesh=mesh,
        in_specs=(P(AXES, None), both, both, P(None, AXES), P(AXES, None, None)),
        out_specs=(P(AXES, None, None), both, P(None, AXES)),
        check_vma=False,
    )
```

```python
import functools
import math

import jax
import jax.numpy as jnp
from jax import lax
from jax.experimental import pallas as pl
from jax.experimental.pallas import tpu as pltpu
from jax.sharding import PartitionSpec as P

D = 512
HEADS = 8
FF = 2048
VOCAB = 27
TD = 128
HD = 64
LANES = 128
EPSILON = 1e-05
AXES = ("dp", "fsdp")
F32 = jnp.float32
BF16 = jnp.bfloat16
VMEM_BYTES = 52 * 2**20

(
    N_CHARS, N_EMB, N_W_TIME, N_W_QKV, N_W_OUT, N_W_UP, N_W_DOWN,
    N_VECTORS, N_TABLE, N_X, N_A, N_QKV, N_PROB, N_O,
    N_X2, N_A2, N_GL, N_SLOPE, N_STREAM, N_OUTPUT, N_COTANGENT,
    N_GRAD, N_GRAD_IN, N_REST, N_KEEP, N_SEND, N_TABLE_OUT, N_EMB_T,
    N_CHUNKS, N_FLAT, N_FLAT_TABLE, N_CUTS, N_CUT_SEMS, N_NORMED, N_TOTAL,
    N_QKV_GRAD, N_HEADS_GRAD,
) = range(37)

ROW_GAIN_ONE, ROW_BIAS_ONE, ROW_W_TIME, ROW_B_TIME = 0, 4, 8, 520
ROW_QKV, ROW_OUT, ROW_GAIN_TWO, ROW_BIAS_TWO = 524, 6668, 8716, 8720
ROW_UP, ROW_B_UP, ROW_DOWN, ROW_B_DOWN, ROW_END = 8724, 16916, 16932, 25124, 25128
CHUNK_PAD = 832


def ceil_to(value, step):
    return -(-value // step) * step


class Geometry:
    def __init__(self, devices, shard, embed_shard):
        self.devices, self.shard, self.embed_shard = devices, shard, embed_shard
        self.param_rows = max(self.count(d, shard) for d in range(devices))
        self.embed_rows = max(self.count(d, embed_shard) for d in range(devices))
        self.embed_at = ceil_to(self.param_rows, 8)
        self.rows = ceil_to(max(self.embed_at + 8, self.param_rows + 2 * self.embed_rows), 16)

    @staticmethod
    def first(d, size):
        return d * size // LANES

    @staticmethod
    def count(d, size):
        return -(-(d + 1) * size // LANES) - d * size // LANES


def params(flops, nbytes, weight=0):
    flops, nbytes = max(flops * weight, 1000), max(nbytes * weight, 1000)
    return dict(
        compiler_params=pltpu.CompilerParams(vmem_limit_bytes=VMEM_BYTES),
        cost_estimate=pl.CostEstimate(flops=flops, bytes_accessed=nbytes, transcendentals=0),
    )


VM = pl.BlockSpec(memory_space=pltpu.VMEM)
SM = pl.BlockSpec(memory_space=pltpu.SMEM)
HBM = pl.BlockSpec(memory_space=pltpu.HBM)


def nn(left, right):
    return lax.dot_general(left, right, (((1,), (0,)), ((), ())), preferred_element_type=F32)


def nt(left, right):
    return lax.dot_general(left, right, (((1,), (1,)), ((), ())), preferred_element_type=F32)


def tn(left, right):
    return nn(left.T, right)


def shift_in(flat, offset):
    rolled = pltpu.roll(flat, offset, 1)
    above = jnp.concatenate([jnp.zeros((1, LANES), F32), rolled[:-1]], 0)
    lane = lax.broadcasted_iota(jnp.int32, flat.shape, 1)
    return jnp.where(lane >= offset, rolled, above)


def shift_out(flat, offset):
    rolled = pltpu.roll(flat, lax.rem(LANES - offset, LANES), 1)
    below = jnp.concatenate([rolled[1:], jnp.zeros((1, LANES), F32)], 0)
    lane = lax.broadcasted_iota(jnp.int32, flat.shape, 1)
    return jnp.where(lane < LANES - offset, rolled, below)


def pack_kernel(geo, place_ref, layers_ref, embed_ref, first_ref, second_ref):
    main = geo.embed_at
    for layer, out_ref in ((0, first_ref), (1, second_ref)):
        moved = shift_in(layers_ref[layer].astype(F32), place_ref[1])
        if layer == 0:
            tail = shift_in(embed_ref[...].astype(F32), place_ref[2])
            parts = [moved[:main], tail] + ([moved[main + 8 :]] if geo.rows > main + 8 else [])
            moved = jnp.concatenate(parts, 0)
        out_ref[...] = moved.astype(BF16)


def pack_shards(geo, place, layer_params, embed):
    layers = jnp.pad(layer_params, ((0, 0), (0, geo.rows * LANES - geo.shard)))
    table = jnp.pad(embed, (0, 8 * LANES - geo.embed_shard))
    out = jax.ShapeDtypeStruct((geo.rows, LANES), BF16)
    return pl.pallas_call(
        functools.partial(pack_kernel, geo),
        out_shape=(out, out),
        in_specs=[SM, VM, VM],
        out_specs=(VM, VM),
        **params(10**6, geo.rows * 1024),
    )(place, layers.reshape(2, geo.rows, LANES), table.reshape(8, LANES))


def finish_kernel(geo, fast, place_ref, *refs):
    grads_ref, embed_ref, moved = refs[-3:]
    parts = refs[:-3]
    count = 4 if fast else 1
    for layer in range(2):
        total = parts[layer * count][...].astype(F32)
        for part in parts[layer * count + 1 : (layer + 1) * count]:
            total = total + part[...].astype(F32)
        moved[pl.ds(layer * geo.rows, geo.rows), :] = shift_out(total, place_ref[1])
        if fast and layer == 0:
            first, size = geo.param_rows, geo.embed_rows
            lower, upper = total[first : first + size], total[first + size : first + 2 * size]
            tail = jnp.where(place_ref[3] >= 2, upper, lower)
            tail = jnp.concatenate([tail, jnp.zeros((8 - size, LANES), F32)], 0)
    if not fast:
        tail = parts[2][...]
    embed_ref[...] = shift_out(tail, place_ref[2])
    for r in range(ceil_to(geo.shard, LANES) // LANES):
        size = min(LANES, geo.shard - r * LANES)
        grads_ref[:, r * LANES : r * LANES + size] = moved[pl.ds(r, 2, stride=geo.rows), :][:, :size]


def finish(geo, fast, place, operands):
    grads, table = pl.pallas_call(
        functools.partial(finish_kernel, geo, fast),
        out_shape=(
            jax.ShapeDtypeStruct((2, geo.shard), F32),
            jax.ShapeDtypeStruct((8, LANES), F32),
        ),
        in_specs=[SM] + [VM] * len(operands),
        out_specs=(VM, VM),
        scratch_shapes=[pltpu.VMEM((3 * geo.rows, LANES), F32)],
        **params(10**6, geo.rows * 4096),
    )(place, *operands)
    return grads, table.reshape(-1)[: geo.embed_shard]


PARTS = {N_W_UP: (1, 4), N_W_DOWN: (0, 4), N_GL: (1, 4), N_SLOPE: (1, 4), N_PROB: (0, 2), N_QKV: (0, 2)}


def parts_of(name, parted):
    return range(PARTS[name][1]) if name in parted else range(1)


def part_of(ref, name, part, parted):
    if name not in parted:
        return ref
    dim, count = PARTS[name]
    size = ref.shape[dim] // count
    index = [slice(None)] * len(ref.shape)
    index[dim] = pl.ds(part * size, size)
    return ref.at[tuple(index)]


class Staged:
    def __init__(self, sources, targets, held, sems, parted):
        self.held, self.pending, self.sent, self.parted = held, {}, [], parted
        self.targets, self.sems = targets, sems
        order = sorted((part, place, name) for place, name in enumerate(sources) for part in parts_of(name, parted))
        for part, _, name in order:
            copy = pltpu.make_async_copy(
                part_of(sources[name], name, part, parted), part_of(held[name], name, part, parted), sems.at[len(self.pending)]
            )
            copy.start()
            self.pending[name, part] = copy
        self.used = len(order)

    def get(self, name, part=None):
        for one in parts_of(name, self.parted) if part is None or name not in self.parted else [part]:
            if (name, one) in self.pending:
                self.pending.pop((name, one)).wait()
        return self.held[name]

    def put(self, name, part=None):
        for one in parts_of(name, self.parted) if part is None else [part]:
            copy = pltpu.make_async_copy(
                part_of(self.held[name], name, one, self.parted), part_of(self.targets[name], name, one, self.parted), self.sems.at[self.used]
            )
            copy.start()
            self.used += 1
            self.sent.append(copy)

    def close(self):
        for copy in list(self.pending.values()) + self.sent:
            copy.wait()


def staged_call(kernel, place, operands, results, scratch, flops, raw=(), semaphores=0, unheld=(), parted=()):
    names, outs, temps = list(operands), list(results), list(scratch)

    held_outs = [name for name in outs if name not in unheld]

    def whole(place_ref, *refs):
        raws, refs = refs[: len(raw)], refs[len(raw) :]
        sources, refs = dict(zip(names, refs)), refs[len(names) :]
        targets, refs = dict(zip(outs, refs)), refs[len(outs) :]
        held, refs = dict(zip(names + held_outs, refs)), refs[len(names) + len(held_outs) :]
        extra, refs = dict(zip(temps, refs)), refs[len(temps) :]
        staged = Staged(sources, targets, held, refs[0], parted)
        kernel(place_ref, raws, staged, extra, refs[-1])
        staged.close()

    buffers = [pltpu.VMEM(v.shape, v.dtype) for v in (*operands.values(), *(results[name] for name in held_outs))]
    sems = [pltpu.SemaphoreType.DMA((sum(len(parts_of(name, parted)) for name in names + held_outs),))]
    if semaphores:
        sems.append(pltpu.SemaphoreType.DMA((semaphores,)))
    found = pl.pallas_call(
        whole,
        out_shape=tuple(results.values()),
        in_specs=[SM] + [HBM] * (len(raw) + len(names)),
        out_specs=(HBM,) * len(outs),
        scratch_shapes=buffers + list(scratch.values()) + sems,
        **params(flops, 2 * 10**7, 1),
    )(place, *raw, *operands.values())
    return dict(zip(outs, found))


def like(dtype, *shape):
    return jax.ShapeDtypeStruct(shape, dtype)


def unpack(geo, layer, plan, me, chunk_refs, held, flat, flat_table, out, sems):
    copies = []
    for source, pieces in zip(chunk_refs, plan):
        for src_at, relative, absolute, dst_at, count in pieces:
            if absolute is None:
                target = held.at[lax.bitwise_xor(me, relative), pl.ds(dst_at, count)]
                origin = source.at[pl.ds(src_at, count)]
            else:
                target, origin = held, source
            copies.append(pltpu.make_async_copy(origin, target, sems.at[len(copies)]))
    for copy in copies:
        copy.start()
    for copy in copies:
        copy.wait()
    for d in range(geo.devices):
        block = held[d].astype(F32)
        start, rows = geo.first(d, geo.shard), geo.count(d, geo.shard)
        split = (d * geo.shard) % LANES != 0
        if split:
            shared = flat[pl.ds(start, 1), :] + block[:1]
        flat[pl.ds(start, rows), :] = block[:rows]
        if split:
            flat[pl.ds(start, 1), :] = shared
        if layer == 0:
            tail = block[geo.embed_at : geo.embed_at + 8]
            start, rows = geo.first(d, geo.embed_shard), geo.count(d, geo.embed_shard)
            split = (d * geo.embed_shard) % LANES != 0
            if split:
                shared = flat_table[pl.ds(start, 1), :] + tail[:1]
            flat_table[pl.ds(start, rows), :] = tail[:rows]
            if split:
                flat_table[pl.ds(start, 1), :] = shared
    vectors = out[N_VECTORS]
    for row, start, width in (
        (0, ROW_GAIN_ONE, 4),
        (1, ROW_BIAS_ONE, 4),
        (2, ROW_B_TIME, 4),
        (3, ROW_GAIN_TWO, 4),
        (4, ROW_BIAS_TWO, 4),
        (5, ROW_B_DOWN, 4),
        (6, ROW_B_UP, 16),
    ):
        for c in range(width):
            vectors[row : row + 1, c * LANES : (c + 1) * LANES] = flat[pl.ds(start + c, 1), :]
    for name, start, rows, width in (
        (N_W_TIME, ROW_W_TIME, TD, 4),
        (N_W_QKV, ROW_QKV, D, 12),
        (N_W_OUT, ROW_OUT, D, 4),
        (N_W_UP, ROW_UP, D, 16),
        (N_W_DOWN, ROW_DOWN, FF, 4),
    ):
        for c in range(width):
            out[name][:, c * LANES : (c + 1) * LANES] = flat[pl.ds(start + c, rows, stride=width), :].astype(BF16)
    if layer == 0:
        table = out[N_TABLE]
        table[...] = jnp.zeros(table.shape, BF16)
        for c in range(4):
            table[0:VOCAB, c * LANES : (c + 1) * LANES] = flat_table[pl.ds(c, VOCAB, stride=4), :].astype(BF16)


WEIGHTS = {
    N_W_QKV: like(BF16, D, 3 * D),
    N_W_OUT: like(BF16, D, D),
    N_W_UP: like(BF16, D, FF),
    N_W_DOWN: like(BF16, FF, D),
    N_VECTORS: like(F32, 8, FF),
}


def unpack_scratch(geo, layer):
    scratch = {
        N_CHUNKS: pltpu.VMEM((geo.devices, geo.rows, LANES), BF16),
        N_FLAT: pltpu.VMEM((ROW_END + CHUNK_PAD, LANES), F32),
        N_FLAT_TABLE: pltpu.VMEM((4 * 34, LANES), F32),
        N_W_TIME: pltpu.VMEM((TD, D), BF16),
    }
    if layer == 0:
        scratch[N_TABLE] = pltpu.VMEM((32, D), BF16)
    return scratch


def split_gathered(gathered):
    plan = tuple(tuple(pieces) for array, pieces in gathered)
    return [array for array, pieces in gathered], plan, sum(len(pieces) for pieces in plan)


def norm_stats(values):
    mean = jnp.mean(values, -1, keepdims=True)
    centered = values - mean
    variance = jnp.mean(centered * centered, -1, keepdims=True)
    scale = lax.rsqrt(variance + EPSILON)
    return centered * scale, scale


ROW_BLOCK = 64


def norm_ahead(values, gain, bias, out):
    for r in range(0, values.shape[0], ROW_BLOCK):
        rows = slice(r, r + ROW_BLOCK)
        unit, _ = norm_stats(values[rows, :])
        out[rows, :] = (unit * gain + bias).astype(BF16)


def norm_back(grad, values, gain, passed, out):
    grad_gain, grad_bias = jnp.zeros((8, D), F32), jnp.zeros((8, D), F32)
    for r in range(0, values.shape[0], ROW_BLOCK):
        rows = slice(r, r + ROW_BLOCK)
        unit, scale = norm_stats(values[rows, :])
        block = grad[rows, :]
        grad_gain = grad_gain + jnp.sum((block * unit).reshape(-1, 8, D), 0)
        grad_bias = grad_bias + jnp.sum(block.reshape(-1, 8, D), 0)
        inner = block * gain
        shifted = inner - jnp.mean(inner, -1, keepdims=True)
        back = scale * (shifted - unit * jnp.mean(inner * unit, -1, keepdims=True))
        out[rows, :] = passed[rows, :].astype(F32) + back
    return jnp.sum(grad_gain, 0, keepdims=True), jnp.sum(grad_bias, 0, keepdims=True)


def gelu_both(u):
    root = math.sqrt(2.0 / math.pi)
    square = u * u
    t = jnp.tanh(root * (u + 0.044715 * (square * u)))
    half = 0.5 * (1.0 + t)
    slope = half + 0.5 * u * (1.0 - t * t) * (root * (1.0 + 3.0 * 0.044715 * square))
    return u * half, slope


def head_masks(shape, scale):
    lane = lax.broadcasted_iota(jnp.int32, shape, 1)
    one = jnp.where(lane < HD, scale, 0.0).astype(BF16)
    two = jnp.where(lane < HD, 0.0, scale).astype(BF16)
    return one, two


def ahead_attn(seqs, stream, emb, w_time, w_qkv, w_out, vectors, x, a, qkv, prob, o, x2, a2, done):
    tokens = x.shape[0]
    length = tokens // seqs
    time_vec = nn(emb[...], w_time[...]) + vectors[2:3, :D]
    for s in range(seqs):
        x[s * length : (s + 1) * length, :] = stream[s * length : (s + 1) * length] + time_vec[s : s + 1]
    done(N_X)
    norm_ahead(x, vectors[0:1, :D], vectors[1:2, :D], a)
    done(N_A)
    for c in range(3):
        part = slice(c * D, (c + 1) * D)
        qkv[:, part] = nn(a[...], w_qkv[:, part]).astype(BF16)
    done(N_QKV)
    masks = head_masks((length, LANES), 1.0 / math.sqrt(HD))
    heads = [(s, pair, h) for s in range(seqs) for pair in range(HEADS // 2) for h in range(2)]

    def cut(s, pair, c):
        return qkv[s * length : (s + 1) * length, c * D + pair * LANES : c * D + (pair + 1) * LANES]

    def scores_of(s, pair, h):
        return nt(cut(s, pair, 1) * masks[h], cut(s, pair, 0))

    ahead = [scores_of(*heads[i]) for i in range(4)]
    mixed = []
    for i, (s, pair, h) in enumerate(heads):
        scores = ahead.pop(0)
        if i + 4 < len(heads):
            ahead.append(scores_of(*heads[i + 4]))
        top = jnp.max(scores, 0, keepdims=True)
        expd = jnp.exp(scores - top)
        low = (expd * (1.0 / jnp.sum(expd, 0, keepdims=True))).astype(BF16)
        prob[s * HEADS + 2 * pair + h] = low
        v_t = cut(s, pair, 2).T
        mixed.append(nn(v_t[h * HD : (h + 1) * HD], low))
        if h == 1:
            rows = slice(s * length, (s + 1) * length)
            o[rows, pair * LANES : (pair + 1) * LANES] = jnp.concatenate(mixed, 0).T.astype(BF16)
            mixed = []
    done(N_PROB)
    done(N_O)
    x2[...] = x[...] + nn(o[...], w_out[...])
    done(N_X2)
    norm_ahead(x2, vectors[3:4, :D], vectors[4:5, :D], a2)
    done(N_A2)


def ahead_mlp(x2, a2, w_up, w_down, vectors, gl, slope, done):
    parts = [slice(c * D, (c + 1) * D) for c in range(FF // D)]

    def up(c):
        return nn(a2()[...], w_up(c)[:, parts[c]])

    total, u = None, up(0)
    for c, part in enumerate(parts):
        value, rate = gelu_both(u + vectors()[6:7, part])
        low = value.astype(BF16)
        gl[:, part] = low
        slope[:, part] = rate.astype(BF16)
        done(N_GL, c)
        done(N_SLOPE, c)
        if c + 1 < len(parts):
            u = up(c + 1)
        step = nn(low, w_down(c)[part, :])
        total = step if total is None else total + step
    return x2()[...] + vectors()[5:6, :D] + total


class Chunks:
    def __init__(self, geo, fast, me, held, targets, sems):
        self.geo, self.fast, self.me, self.held, self.targets, self.sems = geo, fast, me, held, targets, sems
        self.copies = []

    def cut(self, d, flat, base, table=None):
        geo, slot = self.geo, d % (self.geo.devices // 2)
        block = flat[pl.ds(geo.first(d, geo.shard) - base, geo.rows), :]
        if table is not None:
            first, size = geo.param_rows, geo.embed_rows
            tails = [
                table[pl.ds(geo.first(e, geo.embed_shard), size), :] for e in (d, d + geo.devices // 2)
            ]
            block = jnp.concatenate([block[:first], *tails, block[first + 2 * size :]], 0)
        self.held[slot] = block.astype(BF16)
        source, sem = self.held.at[slot], self.sems.at[slot]
        if not self.fast:
            self.copies.append(pltpu.make_async_copy(source, self.targets[0].at[slot], sem))
            self.copies[-1].start()
            return
        relative = lax.bitwise_xor(self.me, d)
        row = lax.bitwise_and(relative, 4) + lax.bitwise_and(relative, 2)
        row = row + lax.bitwise_and(lax.shift_right_logical(relative, 3), 1)
        keep, send = (pltpu.make_async_copy(source, target.at[row], sem) for target in self.targets)
        core = lax.bitwise_and(relative, 1)

        @pl.when(core == 0)
        def _():
            keep.start()

        @pl.when(core == 1)
        def _():
            send.start()

        self.copies.append(keep)

    def close(self):
        for copy in self.copies:
            copy.wait()


def back_mlp(geo, chunks, grad_in, x2, a2, gl, slope, w_up, w_down, vectors, grad, rest, flat, base, normed, done):
    grad_low = grad_in()[...].astype(BF16)
    flat[pl.ds(ROW_END - base, CHUNK_PAD), :] = jnp.zeros((CHUNK_PAD, LANES), F32)
    grad_bias = jnp.sum(grad_low.astype(F32), 0, keepdims=True)
    for c in range(4):
        flat[pl.ds(ROW_B_DOWN - base + c, 1), :] = grad_bias[:, c * LANES : (c + 1) * LANES]
    parts = [slice(j * D, (j + 1) * D) for j in range(FF // D)]

    def hidden_grad(j):
        return nt(grad_low, w_down(j)[parts[j], :])

    total, hidden = None, hidden_grad(0)
    for j, part in enumerate(parts):
        up_grad = (hidden * slope(j)[:, part].astype(F32)).astype(BF16)
        bias_grad = jnp.sum(up_grad.astype(F32), 0, keepdims=True)
        if j + 1 < len(parts):
            hidden = hidden_grad(j + 1)
        down = tn(gl(j)[:, part], grad_low)
        for c in range(4):
            cols = slice(c * LANES, (c + 1) * LANES)
            flat[pl.ds(ROW_B_UP - base + 4 * j + c, 1), :] = bias_grad[:, cols]
            flat[pl.ds(ROW_DOWN - base + 4 * D * j + c, D, stride=4), :] = down[:, cols]
        up = tn(a2()[...], up_grad)
        for c in range(4):
            cols = slice(c * LANES, (c + 1) * LANES)
            flat[pl.ds(ROW_UP - base + 4 * j + c, D, stride=16), :] = up[:, cols]
        step = nt(up_grad, w_up(j)[:, part])
        total = step if total is None else total + step
    normed[...] = total
    for d in range(geo.devices // 2, geo.devices):
        chunks.cut(d, flat, base)
    grad_gain, grad_bias = norm_back(normed, x2(), vectors()[3:4, :D], grad_in(), grad)
    done(N_GRAD)
    for c in range(4):
        cols = slice(c * LANES, (c + 1) * LANES)
        flat[pl.ds(ROW_GAIN_TWO - base + c, 1), :] = grad_gain[:, cols]
        flat[pl.ds(ROW_BIAS_TWO - base + c, 1), :] = grad_bias[:, cols]
    rest[...] = flat[pl.ds(ROW_GAIN_TWO - base, rest.shape[0]), :].astype(BF16)
    done(N_REST)


def back_attn(
    geo, seqs, chunks, table, embed_outs, grad_in, x, a, qkv, prob, o, w_qkv, w_out, vectors, emb_t, rest, total,
    flat, qkv_grad, heads_grad, normed, chars, done,
):
    tokens = normed.shape[0]
    length = tokens // seqs
    grad_low = grad_in()[...].astype(BF16)
    heads_grad[...] = nt(grad_low, w_out()[...]).astype(BF16)
    out_grad = tn(o()[...], grad_low)
    for c in range(4):
        flat[pl.ds(ROW_OUT + c, D, stride=4), :] = out_grad[:, c * LANES : (c + 1) * LANES]
    masks = head_masks((length, LANES), 1.0)
    scale = 1.0 / math.sqrt(HD)
    lane = lax.broadcasted_iota(jnp.int32, (length, LANES), 1)
    qkv, prob = qkv(), prob()
    heads = [(s, pair, h) for s in range(seqs) for pair in range(HEADS // 2) for h in range(2)]

    def cut(s, pair, c):
        return qkv[s * length : (s + 1) * length, c * D + pair * LANES : c * D + (pair + 1) * LANES]

    def go_of(s, pair):
        return heads_grad[s * length : (s + 1) * length, pair * LANES : (pair + 1) * LANES]

    def prob_grad_of(s, pair, h):
        return nt(cut(s, pair, 2) * masks[h], go_of(s, pair))

    ahead = [prob_grad_of(*heads[i]) for i in range(4)]
    to_q, to_k, to_v = [], [], []
    for i, (s, pair, h) in enumerate(heads):
        prob_grad = ahead.pop(0)
        if i + 4 < len(heads):
            ahead.append(prob_grad_of(*heads[i + 4]))
        prob_low = prob[s * HEADS + 2 * pair + h]
        prob_full = prob_low.astype(F32)
        weighted = prob_full * prob_grad
        row_dot = jnp.sum(weighted, 0, keepdims=True)
        score_grad = (weighted - prob_full * row_dot).astype(BF16)
        to_v.append(nn(prob_low, go_of(s, pair)))
        k_t = cut(s, pair, 1).T
        to_q.append(nn(k_t[h * HD : (h + 1) * HD], score_grad))
        to_k.append(nn(score_grad, cut(s, pair, 0)))
        if h == 1:
            rows = slice(s * length, (s + 1) * length)
            cols = [slice(c * D + pair * LANES, c * D + (pair + 1) * LANES) for c in range(3)]
            qkv_grad[rows, cols[0]] = (jnp.concatenate(to_q, 0).T * scale).astype(BF16)
            qkv_grad[rows, cols[1]] = (jnp.where(lane < HD, to_k[0], to_k[1]) * scale).astype(BF16)
            qkv_grad[rows, cols[2]] = jnp.where(lane < HD, to_v[0], to_v[1]).astype(BF16)
            to_q, to_k, to_v = [], [], []
    a_t, steps = a()[...].T, None
    for part in range(3):
        cols = slice(part * D, (part + 1) * D)
        piece = nn(a_t, qkv_grad[:, cols])
        for c in range(4):
            flat[pl.ds(ROW_QKV + 4 * part + c, D, stride=12), :] = piece[:, c * LANES : (c + 1) * LANES]
        step = nt(qkv_grad[:, cols], w_qkv()[:, cols])
        steps = step if steps is None else steps + step
    normed[...] = steps
    flat[pl.ds(ROW_GAIN_TWO, rest().shape[0]), :] = rest()[...].astype(F32)
    middle = geo.devices // 2
    early = [d for d in range(middle) if geo.first(d, geo.shard) >= ROW_QKV] if table is None else []
    for d in early:
        chunks.cut(d, flat, 0)
    grad_gain, grad_bias = norm_back(normed, x(), vectors()[0:1, :D], grad_in(), total)
    done(N_GRAD)
    time_grad = [
        jnp.sum(total[s * length : (s + 1) * length, :], 0, keepdims=True).astype(BF16).astype(F32) for s in range(seqs)
    ]
    bias_grad = sum(time_grad[1:], time_grad[0])
    weight_grad = sum(emb_t()[:, s : s + 1] * time_grad[s] for s in range(seqs))
    for c in range(4):
        cols = slice(c * LANES, (c + 1) * LANES)
        flat[pl.ds(ROW_GAIN_ONE + c, 1), :] = grad_gain[:, cols]
        flat[pl.ds(ROW_BIAS_ONE + c, 1), :] = grad_bias[:, cols]
        flat[pl.ds(ROW_B_TIME + c, 1), :] = bias_grad[:, cols]
        flat[pl.ds(ROW_W_TIME + c, TD, stride=4), :] = weight_grad[:, cols]
    if table is not None:
        kind = lax.broadcasted_iota(jnp.int32, (32, tokens), 0)
        table_grad = nn((chars()[...] == kind).astype(BF16), total[...].astype(BF16))
        for c in range(4):
            table[pl.ds(c, 32, stride=4), :] = table_grad[:, c * LANES : (c + 1) * LANES]
    for d in range(middle):
        if d not in early:
            chunks.cut(d, flat, 0, table if chunks.fast else None)
    if table is not None and not chunks.fast:
        for d in range(geo.devices):
            embed_outs[d] = table[pl.ds(geo.first(d, geo.embed_shard), 8), :]


def kept_shapes(seqs, tokens):
    length = tokens // seqs
    return {
        N_X: like(F32, tokens, D),
        N_A: like(BF16, tokens, D),
        N_QKV: like(BF16, tokens, 3 * D),
        N_PROB: like(BF16, seqs * HEADS, length, length),
        N_O: like(BF16, tokens, D),
    }


def rest_rows(geo):
    middle = geo.first(geo.devices // 2, geo.shard)
    return ceil_to(middle + geo.rows - ROW_GAIN_TWO, 16)


def chunk_results(geo, fast):
    if fast:
        shape = like(BF16, geo.devices // 4, geo.rows, LANES)
        return {N_KEEP: shape, N_SEND: shape}
    return {N_KEEP: like(BF16, geo.devices // 2, geo.rows, LANES)}


def chunk_targets(staged, fast):
    return [staged.targets[name] for name in ((N_KEEP, N_SEND) if fast else (N_KEEP,))]


def chunk_scratch(geo, tokens):
    return {
        N_CUTS: pltpu.VMEM((geo.devices // 2, geo.rows, LANES), BF16),
        N_CUT_SEMS: pltpu.SemaphoreType.DMA((geo.devices // 2,)),
        N_NORMED: pltpu.VMEM((tokens, D), F32),
    }


def first_ahead(geo, seqs, place, gathered, chars, emb):
    tokens = chars.shape[0]
    arrays, plan, count = split_gathered(gathered)
    results = WEIGHTS | kept_shapes(seqs, tokens) | {N_X2: like(F32, tokens, D), N_A2: like(BF16, tokens, D)}

    def kernel(place_ref, chunk_refs, staged, extra, sems):
        held = staged.held
        unpack(
            geo, 0, plan, place_ref[0], chunk_refs, extra[N_CHUNKS], extra[N_FLAT], extra[N_FLAT_TABLE], held | extra, sems
        )
        for name in WEIGHTS:
            staged.put(name)
        lane = lax.broadcasted_iota(jnp.int32, (tokens, 32), 1)
        stream = nn((staged.get(N_CHARS)[...] == lane).astype(BF16), extra[N_TABLE][...])
        weights = [extra[N_W_TIME]] + [held[name] for name in (N_W_QKV, N_W_OUT, N_VECTORS)]
        outs = [held[name] for name in (N_X, N_A, N_QKV, N_PROB, N_O, N_X2, N_A2)]
        ahead_attn(seqs, stream, staged.get(N_EMB), *weights, *outs, staged.put)

    operands = {N_CHARS: chars, N_EMB: emb}
    scratch = unpack_scratch(geo, 0)
    return staged_call(kernel, place, operands, results, scratch, 4 * 10**9, arrays, count, parted=())


def first_ahead_rest(place, found):
    names = (N_A2, N_W_UP, N_VECTORS, N_W_DOWN, N_X2)
    operands = {name: found[name] for name in names}
    tokens = found[N_X2].shape[0]
    results = {N_STREAM: like(F32, tokens, D), N_GL: like(BF16, tokens, FF), N_SLOPE: like(BF16, tokens, FF)}

    def kernel(place_ref, _, staged, extra, sems):
        late = [functools.partial(staged.get, name) for name in (N_X2, N_A2, N_W_UP, N_W_DOWN, N_VECTORS)]
        gl, slope, stream = (staged.held[name] for name in (N_GL, N_SLOPE, N_STREAM))
        stream[...] = ahead_mlp(*late, gl, slope, staged.put)
        staged.put(N_STREAM)

    return found | staged_call(kernel, place, operands, results, {}, 4 * 10**9, parted=(N_W_UP, N_W_DOWN, N_GL, N_SLOPE))


def second_both(geo, fast, seqs, place, gathered, stream, emb, cotangent):
    tokens = stream.shape[0]
    arrays, plan, count = split_gathered(gathered)
    results = {name: WEIGHTS[name] for name in (N_W_QKV, N_W_OUT, N_VECTORS)}
    results = results | kept_shapes(seqs, tokens)
    results = results | {
        N_OUTPUT: like(BF16, tokens, D),
        N_GRAD: like(F32, tokens, D),
        N_REST: like(BF16, rest_rows(geo), LANES),
    }
    results = results | chunk_results(geo, fast)
    scratch = unpack_scratch(geo, 1)
    scratch[N_W_UP], scratch[N_W_DOWN] = pltpu.VMEM((D, FF), BF16), pltpu.VMEM((FF, D), BF16)
    scratch[N_X2], scratch[N_A2] = pltpu.VMEM((tokens, D), F32), pltpu.VMEM((tokens, D), BF16)
    scratch[N_GL], scratch[N_SLOPE] = pltpu.VMEM((tokens, FF), BF16), pltpu.VMEM((tokens, FF), BF16)
    scratch = scratch | chunk_scratch(geo, tokens)

    def kernel(place_ref, chunk_arrays, staged, extra, sems):
        every = staged.held | extra
        unpack(geo, 1, plan, place_ref[0], chunk_arrays, extra[N_CHUNKS], extra[N_FLAT], extra[N_FLAT_TABLE], every, sems)
        for name in (N_W_QKV, N_W_OUT, N_VECTORS):
            staged.put(name)
        weights = [every[name] for name in (N_W_TIME, N_W_QKV, N_W_OUT, N_VECTORS)]
        outs = [every[name] for name in (N_X, N_A, N_QKV, N_PROB, N_O, N_X2, N_A2)]

        def done(name, part=None):
            if name in results:
                staged.put(name, part)

        ahead_attn(seqs, staged.get(N_STREAM)[...], staged.get(N_EMB), *weights, *outs, done)

        def ready(*names):
            return [lambda part=None, ref=every[name]: ref for name in names]

        outputs = ahead_mlp(*ready(N_X2, N_A2, N_W_UP, N_W_DOWN, N_VECTORS), every[N_GL], every[N_SLOPE], done)
        every[N_OUTPUT][...] = outputs.astype(BF16)
        done(N_OUTPUT)
        chunks = Chunks(geo, fast, place_ref[0], extra[N_CUTS], chunk_targets(staged, fast), extra[N_CUT_SEMS])
        back_mlp(
            geo, chunks, functools.partial(staged.get, N_COTANGENT),
            *ready(N_X2, N_A2, N_GL, N_SLOPE, N_W_UP, N_W_DOWN, N_VECTORS),
            every[N_GRAD], every[N_REST], extra[N_FLAT], 0, extra[N_NORMED], done,
        )
        chunks.close()

    operands = {N_STREAM: stream, N_EMB: emb, N_COTANGENT: cotangent}
    return staged_call(kernel, place, operands, results, scratch, 10**10, arrays, count, (N_KEEP, N_SEND))


def first_back_mlp(geo, fast, place, grad, found):
    names = (N_GRAD_IN, N_W_DOWN, N_SLOPE, N_GL, N_A2, N_W_UP, N_X2, N_VECTORS)
    operands = {name: grad if name == N_GRAD_IN else found[name] for name in names}
    tokens = grad.shape[0]
    results = {N_GRAD: like(F32, tokens, D), N_REST: like(BF16, rest_rows(geo), LANES)} | chunk_results(geo, fast)
    base = ROW_GAIN_TWO

    def kernel(place_ref, _, staged, extra, sems):
        late = [
            functools.partial(staged.get, name)
            for name in (N_GRAD_IN, N_X2, N_A2, N_GL, N_SLOPE, N_W_UP, N_W_DOWN, N_VECTORS)
        ]
        chunks = Chunks(geo, fast, place_ref[0], extra[N_CUTS], chunk_targets(staged, fast), extra[N_CUT_SEMS])
        back_mlp(
            geo, chunks, *late, staged.held[N_GRAD], staged.held[N_REST], extra[N_FLAT], base, extra[N_NORMED], staged.put
        )
        chunks.close()

    scratch = {N_FLAT: pltpu.VMEM((ROW_END - base + CHUNK_PAD, LANES), F32)} | chunk_scratch(geo, tokens)
    return staged_call(kernel, place, operands, results, scratch, 6 * 10**9, unheld=(N_KEEP, N_SEND))


def both_back_attn(geo, fast, layer, seqs, place, grad, found, emb_t, rest, chars_row):
    names = (N_GRAD_IN, N_W_OUT, N_O, N_QKV, N_PROB, N_A, N_W_QKV, N_X, N_VECTORS, N_EMB_T, N_REST)
    given = {N_GRAD_IN: grad, N_EMB_T: emb_t, N_REST: rest}
    operands = {name: given[name] if name in given else found[name] for name in names}
    tokens = grad.shape[0]
    results = {} if layer == 0 else {N_GRAD: like(F32, tokens, D)}
    results = results | chunk_results(geo, fast)
    scratch = {
        N_FLAT: pltpu.VMEM((ROW_GAIN_TWO + rest.shape[0], LANES), F32),
        N_QKV_GRAD: pltpu.VMEM((tokens, 3 * D), BF16),
        N_HEADS_GRAD: pltpu.VMEM((tokens, D), BF16),
    } | chunk_scratch(geo, tokens)
    if layer == 0:
        scratch[N_TOTAL] = pltpu.VMEM((tokens, D), F32)
        operands[N_CHARS] = chars_row
        scratch[N_TABLE] = pltpu.VMEM((4 * 34, LANES), F32)
        if not fast:
            results[N_TABLE_OUT] = like(F32, geo.devices, 8, LANES)

    def kernel(place_ref, _, staged, extra, sems):
        late = [functools.partial(staged.get, name) for name in (N_GRAD_IN, N_X, N_A, N_QKV, N_PROB, N_O, N_W_QKV, N_W_OUT)]
        tail = [functools.partial(staged.get, name) for name in (N_VECTORS, N_EMB_T, N_REST)]
        chunks = Chunks(geo, fast, place_ref[0], extra[N_CUTS], chunk_targets(staged, fast), extra[N_CUT_SEMS])

        def done(name, part=None):
            if name in results:
                staged.put(name, part)

        back_attn(
            geo, seqs, chunks, extra.get(N_TABLE), staged.held.get(N_TABLE_OUT), *late, *tail,
            extra[N_TOTAL] if layer == 0 else staged.held[N_GRAD], extra[N_FLAT], extra[N_QKV_GRAD], extra[N_HEADS_GRAD],
            extra[N_NORMED], functools.partial(staged.get, N_CHARS), done,
        )
        done(N_TABLE_OUT)
        chunks.close()

    return staged_call(kernel, place, operands, results, scratch, 6 * 10**9, unheld=(N_KEEP, N_SEND))


def permute(value, distance, devices):
    return lax.ppermute(value, AXES, [(d, d ^ distance) for d in range(devices)])


Z1, Z2, Z3, X, Y, CORE = 8, 16, 24, 4, 2, 1


def after(value, *others):
    return lax.optimization_barrier((value, *others))[0]


def sync(*values):
    return lax.optimization_barrier(values)


def gather_both(geo, first, second):
    n, rows = geo.devices, geo.rows
    half = ceil_to(rows // 2, 16)

    def sides(held):
        return permute(held, X, n), permute(held, Y, n)

    def corners(over_x, over_y):
        return permute(over_x[:half], Y, n), permute(over_y[half:], X, n)

    def other(*arrays):
        return permute(jnp.concatenate(arrays, 0), CORE, n)

    near, over = permute(first, Z1, n), permute(first, Z2, n)
    sides_0 = sides(first)
    sides_0 = sync(*sides_0)
    corners_0 = corners(*sides_0)
    near, _ = sync(near, sides_0[0])
    sides_1 = sides(near)
    over, _ = sync(over, near)
    far = permute(over, Z1, n)
    sides_2 = sides(over)
    *sides_1, _ = sync(*sides_1, over)
    corners_1 = corners(*sides_1)
    far, *corners_0 = sync(far, *corners_0, sides_1[0])[:3]
    sides_3 = sides(far)
    other_0 = other(first, *sides_0, *corners_0)
    second, _ = sync(second, far)
    near_b, over_b = permute(second, Z1, n), permute(second, Z2, n)
    *sides_2, _ = sync(*sides_2, far)
    corners_2 = corners(*sides_2)
    *corners_1, _ = sync(*corners_1, sides_2[0])
    other_1 = other(near, *sides_1, *corners_1)
    *sides_3, _ = sync(*sides_3, sides_2[0])
    corners_3 = corners(*sides_3)
    over_b, near_b, _ = sync(over_b, near_b, sides_3[0])
    far_b = permute(over_b, Z1, n)
    *corners_2, _ = sync(*corners_2, sides_3[0])
    other_2 = other(over, *sides_2, *corners_2)
    *corners_3, far_b, _ = sync(*corners_3, far_b, corners_2[0])
    other_3 = other(far, *sides_3, *corners_3)
    column = jnp.concatenate([second, near_b, over_b, far_b], 0)
    found = []
    for z, arrays, packed in (
        (0, (first, *sides_0, *corners_0), other_0),
        (Z1, (near, *sides_1, *corners_1), other_1),
        (Z2, (over, *sides_2, *corners_2), other_2),
        (Z3, (far, *sides_3, *corners_3), other_3),
    ):
        pieces = [
            (0, z, None, 0, rows),
            (rows, z + X, None, 0, rows),
            (2 * rows, z + Y, None, 0, rows),
            (3 * rows, z + X + Y, None, 0, half),
            (3 * rows + half, z + X + Y, None, half, rows - half),
        ]
        for array, (_, relative, _, at, count) in zip(arrays, pieces):
            found.append((array, [(0, relative, None, at, count)]))
        found.append((packed, [(src, rel + CORE, None, at, count) for src, rel, _, at, count in pieces]))
    return found, column


def gather_sides(geo, column):
    return permute(column, X, geo.devices), permute(column, Y, geo.devices)


def gather_corners(geo, over_x, over_y):
    n, rows = geo.devices, geo.rows
    half = ceil_to(rows // 2, 16)
    cut_x = over_x.reshape(4, rows, LANES)[:, :half].reshape(-1, LANES)
    cut_y = over_y.reshape(4, rows, LANES)[:, half:].reshape(-1, LANES)
    return permute(cut_x, Y, n), permute(cut_y, X, n)


def gathered_pieces(geo, arrays, others):
    rows = geo.rows
    half = ceil_to(rows // 2, 16)
    found = []
    for core, group in ((0, arrays), (CORE, others)):
        for array, (relative, at, count) in zip(
            group, ((0, 0, rows), (X, 0, rows), (Y, 0, rows), (X + Y, 0, half), (X + Y, half, rows - half))
        ):
            found.append((array, [(z * count, relative + core + 8 * z, None, at, count) for z in range(4)]))
    return found


def gather_any(geo, chunk):
    gathered = lax.all_gather(chunk, AXES, axis=0)
    return [(gathered, [(0, 0, 0, 0, 0)])]


def add(*values):
    total = values[0].astype(F32)
    for value in values[1:]:
        total = total + value.astype(F32)
    return total


def plane_start(geo, keep, came):
    shape = (2, 2, 2, geo.rows, LANES)
    half = ceil_to(geo.rows // 2, 16)
    keep, came = keep.reshape(shape), came.reshape(shape)
    one = (keep[:, :, :, :half], came[:, :, :, :half])
    two = (keep[:, :, :, half:], came[:, :, :, half:])
    to_x = add(*(part[1] for part in one)).astype(BF16)
    to_y = add(*(part[:, 1] for part in two)).astype(BF16)
    return [part[0] for part in one], [part[:, 0] for part in two], to_x, to_y


def plane_next(one, two, from_x, from_y):
    one, two = one + [from_x], two + [from_y]
    to_y = add(*(part[1] for part in one)).astype(BF16)
    to_x = add(*(part[1] for part in two)).astype(BF16)
    return [part[0] for part in one], [part[0] for part in two], to_y, to_x


def plane_end(one, two, from_y, from_x):
    return jnp.concatenate([add(*one, from_y), add(*two, from_x)], 1)


def column_sum(geo, place, upper, lower, table):
    n = geo.devices
    if table:
        row = lax.broadcasted_iota(jnp.int32, (1, geo.rows, 1), 1)
        upper = jnp.where(row < geo.param_rows, upper, lower)
    is_upper = place[3] >= 2
    near = jnp.where(is_upper, upper, lower)
    far = jnp.where(is_upper, lower, upper).astype(BF16)
    return [near[0], permute(near[1].astype(BF16), Z1, n), permute(far[0], Z2, n), permute(far[1], Z3, n)]


def sum_any(chunks):
    return lax.psum_scatter(chunks.astype(F32), AXES, scatter_dimension=0, tiled=True)[0]


def timestep_embed(step_ids):
    half_dim = TD // 2
    freq_base = jnp.exp(jnp.arange(half_dim, dtype=F32) * (-math.log(10000.0) / half_dim))
    angle_grid = step_ids.astype(F32)[:, None] * freq_base[None, :]
    return jnp.concatenate([jnp.sin(angle_grid), jnp.cos(angle_grid)], axis=1)


def body(fast, chars, steps, embed, layer_params, cotangent):
    seqs, length = chars.shape
    tokens = seqs * length
    geo = Geometry(lax.axis_size(AXES), layer_params.shape[1], embed.shape[0])
    index = lax.axis_index(AXES).astype(jnp.int32)
    place = jnp.stack(
        [index, index * geo.shard % LANES, index * geo.embed_shard % LANES, index // 8]
    ).astype(jnp.int32)
    chunks = pack_shards(geo, place, layer_params, embed)
    emb = timestep_embed(steps).astype(BF16)
    emb_rows = jnp.concatenate([emb, jnp.zeros((8 - seqs, TD), BF16)], 0) if seqs < 8 else emb
    emb_t = emb.astype(F32).T
    chars_row, chars_col = chars.reshape(1, tokens), chars.reshape(tokens, 1)
    n = geo.devices

    cotangent = cotangent.reshape(tokens, D)
    if not fast:
        first = first_ahead(geo, seqs, place, gather_any(geo, chunks[0]), chars_col, emb_rows)
        first = first_ahead_rest(place, first)
        second = second_both(geo, fast, seqs, place, gather_any(geo, chunks[1]), first[N_STREAM], emb_rows, cotangent)
        low_second = both_back_attn(geo, fast, 1, seqs, place, second[N_GRAD], second, emb_t, second[N_REST], chars_row)
        up_first = first_back_mlp(geo, fast, place, low_second[N_GRAD], first)
        low_first = both_back_attn(geo, fast, 0, seqs, place, up_first[N_GRAD], first, emb_t, up_first[N_REST], chars_row)
        sums = [
            sum_any(jnp.concatenate([low_first[N_KEEP], up_first[N_KEEP]], 0)),
            sum_any(jnp.concatenate([low_second[N_KEEP], second[N_KEEP]], 0)),
            sum_any(low_first[N_TABLE_OUT]),
        ]
        grad_params, grad_embed = finish(geo, fast, place, sums)
        return (second[N_OUTPUT].reshape(seqs, length, D), grad_embed, grad_params)

    gathered, column = gather_both(geo, *chunks)
    sides = gather_sides(geo, column)
    column_other = permute(column, CORE, n)
    first = first_ahead(geo, seqs, place, gathered, chars_col, emb_rows)
    first, sides, column_other = sync(first, sides, column_other)
    corners = gather_corners(geo, *sides)
    sides_other = [permute(side, CORE, n) for side in sides]
    first = first_ahead_rest(place, first)
    first, corners, sides_other = sync(first, corners, sides_other)
    corners_other = [permute(corner, CORE, n) for corner in corners]
    pieces = gathered_pieces(geo, [column, *sides, *corners], [column_other, *sides_other, *corners_other])
    second = second_both(geo, fast, seqs, place, pieces, first[N_STREAM], emb_rows, cotangent)
    output = second[N_OUTPUT].reshape(seqs, length, D)

    def cross(to_one, to_two, one, two):
        return permute(to_one, one, n), permute(to_two, two, n)

    def attn(layer, grad, found, rest):
        got = both_back_attn(geo, fast, layer, seqs, place, grad, found, emb_t, rest, chars_row)
        return (got[N_KEEP], got[N_SEND]) if layer == 0 else (got[N_GRAD], got[N_KEEP], got[N_SEND])

    grad, rest, keep_u, send_u = (second[name] for name in (N_GRAD, N_REST, N_KEEP, N_SEND))
    came_u = permute(send_u, CORE, n)
    grad, keep_l, send_l = attn(1, grad, second, rest)
    grad, keep_u, came_u, keep_l, send_l = sync(grad, keep_u, came_u, keep_l, send_l)
    came_l = permute(send_l, CORE, n)
    one_u, two_u, to_x, to_y = plane_start(geo, keep_u, came_u)
    from_u = cross(to_x, to_y, X, Y)

    got = first_back_mlp(geo, fast, place, after(grad, to_x, to_y), first)
    grad, rest, keep, send = (got[name] for name in (N_GRAD, N_REST, N_KEEP, N_SEND))
    grad, rest, keep, send, came_l, from_u = sync(grad, rest, keep, send, came_l, from_u)
    came = permute(send, CORE, n)
    one_u, two_u, to_y, to_x = plane_next(one_u, two_u, *from_u)
    from_u = cross(to_y, to_x, Y, X)
    one_l, two_l, to_x_l, to_y_l = plane_start(geo, keep_l, came_l)
    from_l = cross(to_x_l, to_y_l, X, Y)

    grad = after(grad, to_x, to_y, to_x_l, to_y_l)
    low_keep, low_send = attn(0, grad, first, rest)
    low_keep, low_send, keep, came, from_u, from_l = sync(low_keep, low_send, keep, came, from_u, from_l)
    low_came = permute(low_send, CORE, n)
    one_l, two_l, to_y, to_x = plane_next(one_l, two_l, *from_l)
    from_l = cross(to_y, to_x, Y, X)
    one, two, to_x, to_y = plane_start(geo, keep, came)
    from_up = cross(to_x, to_y, X, Y)
    upper = plane_end(one_u, two_u, *from_u)

    low_came, low_keep, upper, _, _ = sync(low_came, low_keep, upper, to_x, to_y)
    low_one, low_two, to_x, to_y = plane_start(geo, low_keep, low_came)
    from_low = cross(to_x, to_y, X, Y)

    from_l, from_up, _, _ = sync(from_l, from_up, to_x, to_y)
    lower = plane_end(one_l, two_l, *from_l)
    seconds = column_sum(geo, place, upper, lower, False)
    one, two, to_y, to_x = plane_next(one, two, *from_up)
    from_up = cross(to_y, to_x, Y, X)

    from_low, _, _ = sync(from_low, to_y, to_x)
    low_one, low_two, to_y, to_x = plane_next(low_one, low_two, *from_low)
    from_low = cross(to_y, to_x, Y, X)

    from_low, from_up = sync(from_low, from_up)
    upper, lower = plane_end(one, two, *from_up), plane_end(low_one, low_two, *from_low)
    firsts = column_sum(geo, place, upper, lower, True)
    grad_params, grad_embed = finish(geo, fast, place, firsts + seconds)
    return (output, grad_embed, grad_params)


def solution(mesh):
    both = P(AXES)
    fast = dict(mesh.shape) == {"dp": 8, "fsdp": 4}
    return jax.shard_map(
        functools.partial(body, fast),
        mesh=mesh,
        in_specs=(P(AXES, None), both, both, P(None, AXES), P(AXES, None, None)),
        out_specs=(P(AXES, None, None), both, P(None, AXES)),
        check_vma=False,
    )
```
